512 devices in a mesh: gy: 16 (over z, core), gx: 32 (over x, y).
Axes of the slice: x: 4, y: 8, z: 8, core: 2. Of those that a mesh axis runs over, the one named last changes fastest.
Arguments:
- points: bfloat16 [9, 2097152], P(None, ('gy', 'gx')), may hold values from -6 to 6
- point_pillar: int32 [2097152], P(('gy', 'gx')), may hold values from 0 to 4095, as said below
- point_weight: bfloat16 [9, 128], replicated, may hold values from -2 to 2
- recv_cell: int32 [2097152], P(('gy', 'gx')), may hold values from 0 to 511
- cell_mask: int32 [512, 512], P('gy', 'gx'), may hold values 0 or 1
- occupancy: int32 [512, 512], P('gy', 'gx'), may hold values 0 or 1
- conv_weight: bfloat16 [2, 9, 128, 128], replicated, may hold values from -0.1875 to 0.1875
- head_weight: bfloat16 [128], replicated, may hold values from -0.5 to 0.5
- conv_second: float32 [2, 9, 128, 128], replicated, may hold values from 1e-12 to 1e-07
- point_second: float32 [9, 128], replicated, may hold values from 1e-12 to 1e-07
- head_second: float32 [128], replicated, may hold values from 1e-10 to 1e-05
Outputs:
- conv_step: float32 [2, 9, 128, 128], replicated
- point_step: float32 [9, 128], replicated
- head_step: float32 [128], replicated
The draws below stay inside these ranges and needn't reach their ends.
Inputs may be any that keep to these rules, and one draw needn't show every extreme that they name: `point_pillar`: on each device the ids do not fall; in each block of 128 slots the named slots are the first ones, every one named by at least one point, and on every device one block is full.
All inputs are finite; a program needn't handle non-finite values. No bound on the sum of `cell_mask` or of `occupancy` on one device may be relied on, other than what follows from the above.
Results may differ from the reference program's by a relative error of at most 0.009.
Values may be sent and summed in bfloat16 or wider, within the bound.
A program may use at most 64 MiB of HBM per device.

```python
import math
import jax
import jax.numpy as jnp
from jax import lax

C = 128
PF = 9
BLOCK = 128
LAYERS = 2
ROWS_DEV = 32
COLS_DEV = 16
PTS_DEV = 4096
NY = 512
NX = 512
POINTS = 2097152
RECV = 2097152
N_GY = 16
N_GX = 32


def device_slots(key, busy, first):
    raw_key, top_key, extra_key = jax.random.split(key, 3)
    raw = jax.random.randint(raw_key, (N_GX,), 0, BLOCK)
    counts = 1 + raw * busy // 8
    chosen = jax.random.randint(top_key, (), 0, N_GX)
    chosen = jnp.where(first, N_GX - 1, chosen)
    counts = jnp.where(jnp.arange(N_GX) == chosen, BLOCK, counts).astype(jnp.int32)
    ends = jnp.cumsum(counts).astype(jnp.int32)
    filled = ends[-1]
    extra = jax.random.randint(extra_key, (PTS_DEV,), 0, filled)
    ranks = jnp.arange(PTS_DEV, dtype=jnp.int32)
    ranks = jnp.where(ranks < filled, ranks, extra).astype(jnp.int32)
    column = jnp.searchsorted(ends, ranks, side='right').astype(jnp.int32)
    within = ranks - (ends[column] - counts[column])
    return jnp.sort(column * BLOCK + within).astype(jnp.int32)


def draw_point_pillar(key, part):
    key = jax.random.fold_in(key, 11)
    busy_key, rest_key = jax.random.split(key)
    busy = jax.random.randint(busy_key, (N_GX,), 1, 9)
    device_keys = jax.random.split(rest_key, N_GY * N_GX)
    first = jnp.arange(N_GY * N_GX) == 0
    slots = jax.vmap(device_slots, in_axes=(0, None, 0))(device_keys, busy, first)
    return slots.reshape(N_GY * N_GX * PTS_DEV).astype(jnp.int32)


def place_ends(values, key, least, largest):
    spot = [jax.random.randint(jax.random.fold_in(key, axis), (), 0, length) for axis, length in enumerate(values.shape)]
    widest = values.shape.index(max(values.shape))
    neighbour = spot[:widest] + [(spot[widest] + 1) % values.shape[widest]] + spot[widest + 1:]
    return values.at[tuple(spot)].set(least).at[tuple(neighbour)].set(largest)


def levels(key, shape, shards, smallest, largest):
    def one(dim, parts):
        draws = jax.random.uniform(jax.random.fold_in(jax.random.fold_in(key, 6), dim), (parts,), jnp.float32, smallest / len(shards), largest / len(shards))
        return jnp.repeat(jnp.exp(draws), shape[dim] // parts).reshape((-1,) + (1,) * (len(shape) - dim - 1))

    loudness = one(*shards[0])
    for cut in shards[1:]:
        loudness = loudness * one(*cut)
    return loudness


def gaussian(stream_key, dims, deviation, reach, shards=(), kind=jnp.bfloat16):
    entries = jax.random.normal(stream_key, dims, jnp.float32) * deviation
    if len(shards) > 0:
        entries = levels(stream_key, dims, shards, -0.22, 0.18) * entries
    return jnp.clip(entries, min=-reach, max=reach).astype(kind)


def setup_inputs(seed: int = 0) -> dict:
    seeds = jax.random.split(jax.random.key(seed), 12)
    return {
        "points": gaussian(seeds[0], (PF, POINTS), 1.0, 6.0, ((1, 512),)),
        "point_pillar": draw_point_pillar(jax.random.fold_in(seeds[11], 71), 0),
        "point_weight": gaussian(seeds[2], (PF, C), PF ** -0.5, 2.0),
        "recv_cell": place_ends(jax.random.randint(seeds[3], (RECV,), 0, ROWS_DEV * COLS_DEV), jax.random.fold_in(seeds[3], 1), 0, (ROWS_DEV * COLS_DEV) - 1).astype(jnp.int32),
        "cell_mask": place_ends((jax.random.randint(seeds[4], (NY, NX), 0, 5) < 3).astype(jnp.int32), jax.random.fold_in(seeds[4], 1), 0, 1),
        "occupancy": place_ends((jax.random.randint(seeds[5], (NY, NX), 0, 2) < 1).astype(jnp.int32), jax.random.fold_in(seeds[5], 1), 0, 1),
        "conv_weight": gaussian(seeds[6], (LAYERS, 9, C, C), (9 * C) ** -0.5, 0.1875),
        "head_weight": gaussian(seeds[7], (C,), C ** -0.5, 0.5),
        "conv_second": jnp.clip(jnp.exp(jax.random.uniform(seeds[8], (LAYERS, 9, C, C), jnp.float32, math.log(9.999999960041972e-13), math.log(1.0000000116860974e-07))), 9.999999960041972e-13, 1.0000000116860974e-07),
        "point_second": jnp.clip(jnp.exp(jax.random.uniform(seeds[9], (PF, C), jnp.float32, math.log(9.999999960041972e-13), math.log(1.0000000116860974e-07))), 9.999999960041972e-13, 1.0000000116860974e-07),
        "head_second": jnp.clip(jnp.exp(jax.random.uniform(seeds[10], (C,), jnp.float32, math.log(1.000000013351432e-10), math.log(9.999999747378752e-06))), 1.000000013351432e-10, 9.999999747378752e-06),
    }


def silu_slope(value):
    sig = jax.nn.sigmoid(value)
    return sig * (1.0 + value * (1.0 - sig))

def stencil(padded, weights, out_rows, out_cols):
    channels = padded.shape[2]
    summed = jnp.zeros((out_rows * out_cols, weights.shape[2]), jnp.float32)
    for offset in range(9):
        shift_y, shift_x = divmod(offset, 3)
        window = padded[shift_y:shift_y + out_rows, shift_x:shift_x + out_cols].reshape(out_rows * out_cols, channels)
        summed = summed + jnp.dot(window, weights[offset], preferred_element_type=jnp.float32)
    return summed.reshape(out_rows, out_cols, weights.shape[2])

def kernel_grad(padded, grad_rows, out_rows, out_cols):
    channels = padded.shape[2]
    pieces = []
    for offset in range(9):
        shift_y, shift_x = divmod(offset, 3)
        window = padded[shift_y:shift_y + out_rows, shift_x:shift_x + out_cols].reshape(out_rows * out_cols, channels)
        pieces.append(jnp.dot(window.T, grad_rows, preferred_element_type=jnp.float32))
    return jnp.stack(pieces)

def rms_step(gradient, second):
    moment = 0.95 * second + 0.05 * gradient * gradient
    return gradient / (jnp.sqrt(moment) + 1e-08)

def pick_rows(item):
    tile_rows, tile_cells = item
    return jnp.take(tile_rows, tile_cells, axis=0)

def reference(points, point_pillar, point_weight, recv_cell, cell_mask, occupancy, conv_weight, head_weight, conv_second, point_second, head_second):
    device_count = N_GY * N_GX
    slot_count = N_GX * BLOCK
    cell_count = ROWS_DEV * COLS_DEV
    point_blocks = points.reshape(PF, device_count, PTS_DEV).transpose(1, 0, 2)
    id_blocks = point_pillar.reshape(device_count, PTS_DEV)

    def encode(item):
        block_points, block_ids = item
        pre_points = jnp.einsum('fp,fc->pc', block_points.astype(jnp.float32), point_weight.astype(jnp.float32))
        counts = jax.ops.segment_sum(jnp.ones((PTS_DEV,), jnp.float32), block_ids, num_segments=slot_count)
        pooled = jax.ops.segment_sum(jax.nn.silu(pre_points), block_ids, num_segments=slot_count)
        return (pooled / jnp.maximum(counts, 1.0)[:, None]).astype(jnp.bfloat16)
    pillars = lax.map(encode, (point_blocks, id_blocks))
    arrived = pillars.reshape(N_GY, N_GX, N_GX, BLOCK, C).transpose(0, 2, 1, 3, 4).reshape(device_count, slot_count, C)
    cell_blocks = recv_cell.reshape(device_count, slot_count)

    def place(item):
        block_pillars, block_cells = item
        return jax.ops.segment_sum(block_pillars.astype(jnp.float32), block_cells, num_segments=cell_count)
    placed = lax.map(place, (arrived, cell_blocks))
    placed = placed.reshape(N_GY, N_GX, ROWS_DEV, COLS_DEV, C).transpose(0, 2, 1, 3, 4).reshape(NY, NX, C)
    visible = (1 - cell_mask).astype(jnp.float32)
    current = (placed * visible[:, :, None]).astype(jnp.bfloat16)
    padded_inputs = []
    pre_values = []
    for layer_index in range(LAYERS):
        padded = jnp.pad(current, ((1, 1), (1, 1), (0, 0)))
        padded_inputs.append(padded)
        pre_act = stencil(padded, conv_weight[layer_index], NY, NX)
        pre_values.append(pre_act)
        current = jax.nn.silu(pre_act).astype(jnp.bfloat16)
    logits = lax.optimization_barrier(jnp.sum(current.astype(jnp.float32) * head_weight.astype(jnp.float32), axis=2))
    masked = cell_mask.astype(jnp.float32)
    targets = occupancy.astype(jnp.float32)
    logit_grad = masked * (jax.nn.sigmoid(logits) - targets) / (NY * NX)
    head_grad = lax.optimization_barrier(jnp.sum(logit_grad[:, :, None] * current.astype(jnp.float32), axis=(0, 1)))
    gradient = (logit_grad[:, :, None] * head_weight.astype(jnp.float32) * silu_slope(pre_values[-1])).astype(jnp.bfloat16)
    kernel_terms = [None] * LAYERS
    for layer_index in reversed(range(LAYERS)):
        kernel_terms[layer_index] = kernel_grad(padded_inputs[layer_index], gradient.reshape(NY * NX, C), NY, NX)
        grad_padded = jnp.pad(gradient, ((1, 1), (1, 1), (0, 0)))
        flipped = conv_weight[layer_index][::-1].transpose(0, 2, 1)
        backward = stencil(grad_padded, flipped, NY, NX)
        if layer_index > 0:
            gradient = (backward * silu_slope(pre_values[layer_index - 1])).astype(jnp.bfloat16)
        else:
            gradient = (backward * visible[:, :, None]).astype(jnp.bfloat16)
    tiles = gradient.reshape(N_GY, ROWS_DEV, N_GX, COLS_DEV, C).transpose(0, 2, 1, 3, 4).reshape(device_count, cell_count, C)
    pillar_grad = lax.map(pick_rows, (tiles, cell_blocks))
    returned = pillar_grad.reshape(N_GY, N_GX, N_GX, BLOCK, C).transpose(0, 2, 1, 3, 4).reshape(device_count, slot_count, C)

    def point_term(summed, item):
        block_points, block_ids, block_returned = item
        pre_points = jnp.einsum('fp,fc->pc', block_points.astype(jnp.float32), point_weight.astype(jnp.float32))
        counts = jax.ops.segment_sum(jnp.ones((PTS_DEV,), jnp.float32), block_ids, num_segments=slot_count)
        slot_grad = block_returned.astype(jnp.float32) / jnp.maximum(counts, 1.0)[:, None]
        point_rows = (jnp.take(slot_grad, block_ids, axis=0) * silu_slope(pre_points)).astype(jnp.bfloat16)
        term = jnp.einsum('fp,pc->fc', block_points.astype(jnp.float32), point_rows.astype(jnp.float32))
        return (summed + term, None)
    point_grad, unused = lax.scan(point_term, jnp.zeros((PF, C), jnp.float32), (point_blocks, id_blocks, returned))
    kernels = jnp.stack(kernel_terms)
    return (rms_step(kernels, conv_second), rms_step(point_grad, point_second), rms_step(head_grad, head_second))
```

```python
import functools

import jax
import jax.numpy as jnp
from jax import lax
from jax.experimental import pallas as pl
from jax.experimental.pallas import tpu as pltpu
from jax.sharding import PartitionSpec as P

MESH = pl.DeviceIdType.MESH
F32 = jnp.float32
BF16 = jnp.bfloat16
VMEM_LIMIT = 56 * 1024 * 1024
CHUNK = 128
SIDE = 8
HALO = 4
STEPS = ((0, -1), (0, 1), (-1, 0), (1, 0), (-1, -1), (1, 1), (-1, 1), (1, -1))


def iota(shape, dim):
    return lax.broadcasted_iota(jnp.int32, shape, dim)


def dot(a, b):
    return jnp.dot(a, b, preferred_element_type=F32)


def dot_nt(a, b):
    return lax.dot_general(a, b, (((1,), (1,)), ((), ())), preferred_element_type=F32)


def dot_tn(a, b):
    return lax.dot_general(a, b, (((0,), (0,)), ((), ())), preferred_element_type=F32)


def slope(value):
    sig = jax.nn.sigmoid(value)
    return sig * (1.0 + value * (1.0 - sig))


def rms_step(gradient, second):
    moment = 0.95 * second + 0.05 * gradient * gradient
    return gradient / (jnp.sqrt(moment) + 1e-08)


def pool_kernel(
    points, ids, ids_row, weight, pillars, table, local, counts, table_s, partial, sums, numbers, sem
):
    chunks = ids.shape[0]
    blocks = pillars.shape[0] // CHUNK
    total = chunks * CHUNK
    here = ids[...]
    back = pltpu.roll(here, 1, axis=1)
    lane = iota(here.shape, 1)
    before = jnp.where(lane == 0, pltpu.roll(back, 1, axis=0), back)
    first = (lane == 0) & (iota(here.shape, 0) == 0)
    flags = jnp.where((here != before) | first, 1.0, 0.0).astype(BF16)
    upto = jnp.where(iota((CHUNK, CHUNK), 0) <= iota((CHUNK, CHUNK), 1), 1.0, 0.0).astype(BF16)
    inside = dot(flags, upto)
    whole = dot(flags, jnp.ones((CHUNK, CHUNK), BF16))
    lower = jnp.where(iota((chunks, chunks), 0) > iota((chunks, chunks), 1), 1.0, 0.0)
    ahead = dot(lower.astype(BF16), whole.astype(BF16))
    head = jnp.broadcast_to(inside[:, 0:1], inside.shape)
    local[...] = (inside - head).astype(jnp.int32)
    row = ids_row[...]
    row_before = pltpu.roll(row, 1, axis=1)
    row_first = (row != row_before) | (iota(row.shape, 1) == 0)
    row_block = jnp.where(row_first, row // CHUNK, blocks + 8)
    below = jnp.where(row_block < iota((blocks + 8, total), 0), 1.0, 0.0).astype(BF16)
    table[0:chunks, :] = (ahead + head - 1.0).astype(jnp.int32)
    table[chunks : chunks + blocks + 8, :] = dot(below, jnp.ones((total, CHUNK), BF16)).astype(
        jnp.int32
    )
    copy = pltpu.make_async_copy(table, table_s, sem)
    copy.start()
    ranks = local[...]
    for k in range(chunks):
        part = pl.ds(k * CHUNK, CHUNK)
        pre = dot_tn(points[:, part], weight[...])
        act = (pre * jax.nn.sigmoid(pre)).astype(BF16)
        pick = jnp.where(iota((CHUNK, CHUNK), 0) == ranks[k : k + 1, :], 1.0, 0.0).astype(BF16)
        partial[part, :] = dot(pick, jnp.concatenate([act, jnp.ones_like(act)], axis=1))
    copy.wait()
    edge = jnp.zeros((8, CHUNK), F32)
    for k in range(chunks):
        at = table_s[k, 0]
        for side, compact in enumerate((sums, numbers)):
            got = partial[pl.ds(k * CHUNK, CHUNK), pl.ds(side * CHUNK, CHUNK)]
            first_rows = got[0:8] if k == 0 else compact[pl.ds(at, 8), :] + got[0:8]
            compact[pl.ds(at, CHUNK + 8), :] = jnp.concatenate([first_rows, got[8:], edge], axis=0)
    diagonal = iota((CHUNK, CHUNK), 0) == iota((CHUNK, CHUNK), 1)
    for d in range(blocks):
        at = table_s[chunks + d, 0]
        held = table_s[chunks + d + 1, 0] - at
        named = iota((CHUNK, CHUNK), 0) < held
        count = jnp.where(named, numbers[pl.ds(at, CHUNK), :], 1.0)
        mean = jnp.where(named, sums[pl.ds(at, CHUNK), :] / count, 0.0)
        pillars[pl.ds(d * CHUNK, CHUNK), :] = mean.astype(BF16)
        counts[d : d + 1, :] = jnp.sum(jnp.where(diagonal, count, 0.0), axis=0, keepdims=True)


def pool(points, point_pillar, weight, slots):
    total = point_pillar.shape[0]
    chunks, blocks = total // CHUNK, slots // CHUNK
    channels = weight.shape[1]
    rows = chunks + blocks + 8
    vmem = pl.BlockSpec(memory_space=pltpu.VMEM)
    return pl.pallas_call(
        pool_kernel,
        out_shape=(
            jax.ShapeDtypeStruct((slots, channels), BF16),
            jax.ShapeDtypeStruct((rows, CHUNK), jnp.int32),
            jax.ShapeDtypeStruct((chunks, CHUNK), jnp.int32),
            jax.ShapeDtypeStruct((blocks, CHUNK), F32),
        ),
        in_specs=[vmem] * 4,
        out_specs=(vmem,) * 4,
        scratch_shapes=[
            pltpu.SMEM((rows, CHUNK), jnp.int32),
            pltpu.VMEM((total, 2 * CHUNK), F32),
            pltpu.VMEM((total + 2 * CHUNK, CHUNK), F32),
            pltpu.VMEM((total + 2 * CHUNK, CHUNK), F32),
            pltpu.SemaphoreType.DMA,
        ],
        compiler_params=pltpu.CompilerParams(vmem_limit_bytes=VMEM_LIMIT),
        name="pool",
    )(points, point_pillar.reshape(chunks, CHUNK), point_pillar.reshape(1, total), weight)


def point_kernel(points, local, weight, table_s, counts, returned, out, compact, rows):
    chunks = local.shape[0]
    blocks = counts.shape[0]
    pad = (-counts.shape[0]) % CHUNK
    scale = 1.0 / counts[...]
    scale = jnp.concatenate([scale, jnp.zeros((pad, CHUNK), F32)], axis=0).T
    for d in range(blocks):
        at = table_s[chunks + d, 0]
        block = returned[pl.ds(d * CHUNK, CHUNK), :].astype(F32)
        compact[pl.ds(at, CHUNK), :] = block * scale[:, d : d + 1]
    compact[pl.ds(table_s[chunks + blocks, 0], CHUNK), :] = jnp.zeros((CHUNK, CHUNK), F32)
    ranks = local[...].astype(F32)
    ranks = jnp.concatenate(
        [ranks, jnp.zeros(((-chunks) % CHUNK, CHUNK), F32)], axis=0
    ).T.astype(jnp.int32)
    for k in range(chunks):
        part = pl.ds(k * CHUNK, CHUNK)
        pre = dot_tn(points[:, part], weight[...])
        window = compact[pl.ds(table_s[k, 0], CHUNK), :].astype(BF16)
        pick = jnp.where(ranks[:, k : k + 1] == iota((CHUNK, CHUNK), 1), 1.0, 0.0).astype(BF16)
        rows[part, :] = (dot(pick, window) * slope(pre)).astype(BF16)
    out[...] = dot(points[...], rows[...])


def point_grad(points, local, weight, table, counts, returned):
    total = points.shape[1]
    vmem = pl.BlockSpec(memory_space=pltpu.VMEM)
    smem = pl.BlockSpec(memory_space=pltpu.SMEM)
    return pl.pallas_call(
        point_kernel,
        out_shape=jax.ShapeDtypeStruct(weight.shape, F32),
        in_specs=[vmem, vmem, vmem, smem, vmem, vmem],
        out_specs=vmem,
        scratch_shapes=[
            pltpu.VMEM((total + 2 * CHUNK, CHUNK), F32),
            pltpu.VMEM((total, CHUNK), BF16),
        ],
        compiler_params=pltpu.CompilerParams(vmem_limit_bytes=VMEM_LIMIT),
        name="point_grad",
    )(points, local, weight, table, counts, returned)


def message_rows(tile_rows, tile_cols):
    spans, at = [], 0
    for down, right in STEPS:
        size = (HALO if down else tile_rows) * (SIDE if right else tile_cols)
        spans.append((at, size))
        at += size
    return spans, at


def ring_size(columns):
    return {32: 8, 8: 4, 4: 2}[columns]


def ring_order(ring):
    order = [ring // 2]
    for far in range(ring // 2 - 1, 0, -1):
        order += [far, -far]
    return order + [0]


def map_kernel(
    grid,
    pillars,
    cells,
    mask_t,
    occupied_t,
    weights,
    head_row,
    returned,
    kernel_out,
    head_out,
    place,
    pick,
    send_f,
    got_f,
    send_m,
    got_m,
    v0,
    v1,
    v2,
    v3,
    send_i,
    got_i,
    got_x,
    send_y,
    got_y,
    own_g,
    got_g,
    send_r,
    own_k,
    core_k,
    send_k,
    got_kz,
    got_ky,
    got_kx,
    sem_f,
    sem_m,
    sem_i,
    sem_x,
    sem_y,
    sem_g,
    sem_r,
    sem_c,
    sem_kz,
    sem_ky,
    sem_kx,
):
    n_gy, n_gx, tile_rows, tile_cols = grid
    gy, gx = lax.axis_index("gy"), lax.axis_index("gx")
    ring = ring_size(n_gx)
    across = n_gx // ring
    half_ring = ring // 2
    order = ring_order(ring)
    slot_of = {rel: r for r, rel in enumerate(order)}
    slot_of[-half_ring] = slot_of[half_ring]
    x, y = gx // ring, lax.rem(gx, ring)
    channels = pillars.shape[1]
    spans, _ = message_rows(tile_rows, tile_cols)
    width = tile_cols + 2 * SIDE
    height = tile_rows + 2 * HALO
    count = tile_rows * tile_cols
    part_rows = count // 2
    fan = across * CHUNK

    def neighbour(k):
        down, right = STEPS[k]
        return lax.rem(gy + down + n_gy, n_gy), lax.rem(gx + right + n_gx, n_gx)

    def along(step):
        return lax.rem(y + step + ring, ring)

    def over(step):
        return lax.rem(x + step + across, across)

    def ring_device(step):
        return gy, x * ring + along(step)

    def across_device(step):
        return gy, over(step) * ring + y

    levels = n_gy // 2
    z, core = gy // 2, lax.rem(gy, 2)

    def level_device(step):
        return lax.rem(z + step, levels) * 2 + core, gx

    other_core = (z * 2 + 1 - core, gx)

    def slot_block(column, place_on_ring):
        return pl.ds(pl.multiple_of((column * ring + place_on_ring) * CHUNK, CHUNK), CHUNK)

    def remote(src, dst, send, recv, device):
        return pltpu.make_async_remote_copy(
            src_ref=src,
            dst_ref=dst,
            send_sem=send,
            recv_sem=recv,
            device_id=device,
            device_id_type=MESH,
        )

    def arrival(ref, sem):
        remote(ref, ref, sem, sem, ring_device(1)).wait_recv()

    barrier = pltpu.get_barrier_semaphore()
    partners = [neighbour(k) for k in range(len(STEPS))]
    partners += [ring_device(step) for step in range(1, ring)]
    partners += [across_device(step) for step in range(1, across)]
    partners += [level_device(step) for step in range(1, levels)] + [other_core]
    for device in partners:
        pl.semaphore_signal(barrier, inc=1, device_id=device, device_id_type=MESH)
    pl.semaphore_wait(barrier, len(partners))

    started = []

    def go(copy):
        copy.start()
        started.append(copy)

    def send_pillars(r):
        for o in range(1, across):
            go(
                remote(
                    pillars.at[slot_block(over(o), along(order[r]))],
                    got_x.at[pl.ds((r * across + o) * CHUNK, CHUNK)],
                    sem_x.at[0, r, o],
                    sem_x.at[1, r, o],
                    across_device(o),
                )
            )

    for r in range(min(3, ring)):
        send_pillars(r)

    send_i[...] = jnp.zeros_like(send_i)
    for step in range(ring):
        lead = step * 8
        for o in range(across):
            row = over(-o) * ring + along(step)
            send_i[lead + o : lead + o + 1, :] = cells[pl.ds(row, 1), :]
        if step == 0:
            got_i[pl.ds(slot_of[0] * 8, 8), :] = send_i[pl.ds(0, 8), :]
        else:
            rel = -step if step <= half_ring else ring - step
            slot = slot_of[rel]
            go(
                remote(
                    send_i.at[pl.ds(lead, 8)],
                    got_i.at[pl.ds(slot * 8, 8)],
                    sem_i.at[0, step],
                    sem_i.at[1, slot],
                    ring_device(step),
                )
            )

    def post(own, send, got, sem):
        grid3 = own.reshape(tile_rows, tile_cols, channels)
        for k, (down, right) in enumerate(STEPS):
            part = grid3
            if down:
                part = part[:HALO] if down < 0 else part[tile_rows - HALO :]
            if right:
                part = part[:, :SIDE] if right < 0 else part[:, tile_cols - SIDE :]
            at, size = spans[k]
            send[pl.ds(at, size), :] = part.reshape(size, channels).astype(BF16)
            there, _ = spans[k ^ 1]
            go(
                remote(
                    send.at[pl.ds(at, size)],
                    got.at[pl.ds(there, size)],
                    sem.at[0, k],
                    sem.at[1, k ^ 1],
                    neighbour(k),
                )
            )

    def collect(own, got, sem):
        parts = {}
        for k, (down, right) in enumerate(STEPS):
            at, size = spans[k]
            arrival(got.at[pl.ds(at, size)], sem.at[1, k])
            rows = HALO if down else tile_rows
            parts[down, right] = (
                got[pl.ds(at, size), :].astype(F32).reshape(rows, size // rows, channels)
            )
        parts[0, 0] = own.reshape(tile_rows, tile_cols, channels)
        return jnp.concatenate(
            [
                jnp.concatenate([parts[down, right] for right in (-1, 0, 1)], axis=1).reshape(
                    -1, channels
                )
                for down in (-1, 0, 1)
            ],
            axis=0,
        )

    masks = jnp.concatenate([mask_t[...], mask_t[...] * occupied_t[...]], axis=0)
    masks = masks.astype(F32).astype(BF16)
    of_row = iota((count, tile_rows), 0) // tile_cols == iota((count, tile_rows), 1)
    by_column = dot_nt(jnp.where(of_row, 1.0, 0.0).astype(BF16), masks)
    pairs = (count, 2 * tile_cols)
    of_column = iota(pairs, 0) % tile_cols == iota(pairs, 1) % tile_cols
    halves = (2 * tile_cols, channels)
    same_half = (iota(halves, 0) < tile_cols) == (iota(halves, 1) < channels // 2)
    mask_own = dot(
        jnp.where(of_column, by_column, 0.0).astype(BF16),
        jnp.where(same_half, 1.0, 0.0).astype(BF16),
    )
    post(mask_own, send_m, got_m, sem_m)

    flat = iota((height * width, channels), 0)
    row = flat // width + gy * tile_rows - HALO
    col = flat % width + gx * tile_cols - SIDE
    in_slab = jnp.where(
        (row >= 0) & (row < n_gy * tile_rows) & (col >= 0) & (col < n_gx * tile_cols), 1.0, 0.0
    )
    column = iota((tile_rows * width, channels), 0) % width
    own_column = jnp.where((column >= SIDE) & (column < SIDE + tile_cols), 1.0, 0.0)

    for r in range(ring - 1):
        arrival(got_i.at[pl.ds(r * 8, 8)], sem_i.at[1, r])
    rows_i = ring * 8
    cells_i = got_i[...]
    cells_t = jnp.concatenate(
        [cells_i.astype(F32), jnp.zeros(((-rows_i) % CHUNK, CHUNK), F32)], axis=0
    ).T.astype(jnp.int32)
    for r in range(ring):
        for o in range(across):
            at = r * 8 + o
            place[r, :, pl.ds(o * CHUNK, CHUNK)] = jnp.where(
                iota((count, CHUNK), 0) == cells_i[at : at + 1, :], 1.0, 0.0
            ).astype(BF16)
            pick[r, pl.ds(o * CHUNK, CHUNK), :] = jnp.where(
                cells_t[:, at : at + 1] == iota((CHUNK, count), 1), 1.0, 0.0
            ).astype(BF16)

    mask_all = (collect(mask_own, got_m, sem_m) * in_slab).astype(BF16)
    half = channels // 2
    spread = jnp.where(
        iota((channels, 2 * channels), 0)
        == jnp.where(iota((channels, 2 * channels), 1) < channels, 0, half),
        1.0,
        0.0,
    ).astype(BF16)
    mask_all = dot(mask_all, spread)
    hidden_cell = mask_all[:, :channels]
    target = mask_all[:, channels:]

    def cut(value, lead, rows):
        return value[lead * width : (lead + rows) * width]

    def side_by_side(value, ref):
        size = value.shape[0]
        left = pltpu.roll(value, 1, axis=0)
        right = pltpu.roll(value, size - 1, axis=0)
        ref[...] = jnp.concatenate([left.astype(BF16), value.astype(BF16), right.astype(BF16)], 1)

    def windows(ref, lead, rows):
        return jnp.concatenate(
            [ref[pl.ds((lead + a) * width, rows * width), :] for a in (0, 1, 2)], axis=1
        )

    def flipped(layer):
        return jnp.concatenate(
            [weights[layer, pl.ds((8 - k) * channels, channels), :] for k in range(9)], axis=1
        )

    visible = 1.0 - cut(hidden_cell, HALO, tile_rows).reshape(tile_rows, width, channels)[
        :, SIDE : SIDE + tile_cols
    ].reshape(count, channels)

    def placed_for(r):
        for o in range(1, across):
            arrival(got_x.at[pl.ds((r * across + o) * CHUNK, CHUNK)], sem_x.at[1, r, o])
        own = pillars[slot_block(x, along(order[r])), :]
        rest = got_x[pl.ds((r * across + 1) * CHUNK, fan - CHUNK), :]
        return dot(place[r], jnp.concatenate([own, rest], axis=0))

    sides = ((0, 1, pl.ds(0, part_rows)), (1, -1, pl.ds(part_rows, part_rows)))
    for t in range(half_ring):
        for r in range(2 * t + 1, min(2 * t + 3, ring)) if t else ():
            send_pillars(r)
        for side, step, part in sides:
            if t == 0:
                if side == 0:
                    summed = placed_for(0)
                    send_y[0, 0] = summed.astype(BF16)
                src = send_y.at[0, 0, part]
                dst = got_y.at[side, 0, part]
            else:
                summed = placed_for(slot_of[step * (half_ring - t)])
                before = got_y.at[side, t - 1]
                if t == 1:
                    arrival(before.at[part], sem_y.at[1, side, 0])
                    low, high = summed[:part_rows], summed[part_rows:]
                    if side == 0:
                        low = low + got_y[side, 0, part, :].astype(F32)
                    else:
                        high = high + got_y[side, 0, part, :].astype(F32)
                    summed = jnp.concatenate([low, high], axis=0)
                else:
                    arrival(before, sem_y.at[1, side, t - 1])
                    summed = summed + before[...].astype(F32)
                send_y[side, t] = summed.astype(BF16)
                src = send_y.at[side, t]
                dst = got_y.at[side, t]
            go(remote(src, dst, sem_y.at[0, side, t], sem_y.at[1, side, t], ring_device(step)))
    placed = placed_for(slot_of[0])
    last = half_ring - 1
    if last:
        for side, _, _ in sides:
            arrival(got_y.at[side, last], sem_y.at[1, side, last])
            placed = placed + got_y[side, last].astype(F32)
    else:
        for side, _, part in sides:
            arrival(got_y.at[side, 0, part], sem_y.at[1, side, 0])
        placed = placed + jnp.concatenate(
            [got_y[0, 0, pl.ds(0, part_rows), :], got_y[1, 0, pl.ds(part_rows, part_rows), :]], 0
        ).astype(F32)

    features = (placed * visible).astype(BF16).astype(F32)
    post(features, send_f, got_f, sem_f)
    side_by_side(collect(features, got_f, sem_f) * in_slab, v0)

    pre1 = dot(windows(v0, 0, height - 2), weights[0])
    side_by_side(pre1 * jax.nn.sigmoid(pre1) * cut(in_slab, 1, height - 2), v1)
    pre2 = dot(windows(v1, 0, height - 4), weights[1])
    sig2 = jax.nn.sigmoid(pre2)
    hidden2 = (pre2 * sig2).astype(BF16)
    head = jnp.broadcast_to(head_row[...], (channels, channels))
    logits = dot_nt(hidden2, head)
    cells_all = n_gy * tile_rows * n_gx * tile_cols
    logit_grad = (
        cut(hidden_cell, 2, height - 4) * jax.nn.sigmoid(logits) - cut(target, 2, height - 4)
    ) / cells_all
    grad2 = logit_grad * head_row[...].astype(F32) * (sig2 * (1.0 + pre2 * (1.0 - sig2)))
    side_by_side(grad2, v2)
    back2 = dot_nt(windows(v2, 0, height - 6), flipped(1))
    grad1 = back2 * slope(cut(pre1, 2, height - 6)) * cut(in_slab, 3, height - 6)
    side_by_side(grad1, v3)
    back1 = dot_nt(windows(v3, 0, tile_rows), flipped(0))
    back1 = back1.reshape(tile_rows, width, channels)[:, SIDE : SIDE + tile_cols].reshape(
        count, channels
    )
    own_g[...] = (back1 * visible).astype(BF16)

    def pass_on(t):
        for side, step, part in sides:
            src = own_g if t == 1 else got_g.at[side, t - 2]
            dst = got_g.at[side, t - 1]
            if t == half_ring:
                src, dst = src.at[part], dst.at[part]
            go(
                remote(
                    src, dst, sem_g.at[0, side, t - 1], sem_g.at[1, side, t - 1], ring_device(step)
                )
            )

    def hand_out(rel, gradient):
        r = slot_of[rel]
        rows = dot(pick[r], gradient).astype(BF16)
        returned[slot_block(x, along(rel)), :] = rows[:CHUNK]
        send_r[r] = rows
        for o in range(1, across):
            go(
                remote(
                    send_r.at[r, pl.ds(o * CHUNK, CHUNK)],
                    returned.at[slot_block(x, along(rel))],
                    sem_r.at[0, r, o],
                    sem_r.at[1, r, o],
                    across_device(-o),
                )
            )

    share = own_k.shape[2]

    def halve(layer, gradient):
        parts = levels // 2
        own_k[pl.ds(layer * parts, parts)] = gradient.reshape(
            parts, 2, share, channels
        ).astype(BF16)
        go(
            remote(
                own_k.at[pl.ds(layer * parts, parts), 1 - core],
                core_k.at[pl.ds(layer * parts, parts)],
                sem_c.at[0, layer],
                sem_c.at[1, layer],
                other_core,
            )
        )

    def to_levels():
        parts = levels // 2
        for layer in range(2):
            arrival(core_k.at[pl.ds(layer * parts, parts)], sem_c.at[1, layer])
        for k in range(levels):
            send_k[k] = (own_k[k, core].astype(F32) + core_k[k].astype(F32)).astype(BF16)
        got_kz[z] = send_k[z]
        for step in range(1, levels):
            go(
                remote(
                    send_k.at[lax.rem(z + step, levels)],
                    got_kz.at[z],
                    sem_kz.at[0, step],
                    sem_kz.at[1, step],
                    level_device(step),
                )
            )

    def gathered(got, sem):
        summed = None
        for step in range(1, got.shape[0]):
            arrival(got.at[0], sem.at[1, step])
        for k in range(got.shape[0]):
            term = got[k].astype(F32)
            summed = term if summed is None else summed + term
        return summed

    def to_all(summed, got, sem, me, device):
        got[me] = summed.astype(BF16)
        for step in range(1, got.shape[0]):
            go(remote(got.at[me], got.at[me], sem.at[0, step], sem.at[1, step], device(step)))

    pass_on(1)
    hand_out(0, own_g[...])
    own2 = (cut(grad2, 2, tile_rows) * own_column).astype(BF16)
    halve(1, dot_tn(windows(v1, 2, tile_rows), own2))
    for t in range(1, half_ring + 1):
        for side, _, part in sides:
            ref = got_g.at[side, t - 1]
            arrival(ref.at[part] if t == half_ring else ref, sem_g.at[1, side, t - 1])
        if t < half_ring:
            pass_on(t + 1)
            hand_out(-t, got_g[0, t - 1])
            hand_out(t, got_g[1, t - 1])
        else:
            hand_out(
                t,
                jnp.concatenate(
                    [
                        got_g[0, t - 1, pl.ds(0, part_rows), :],
                        got_g[1, t - 1, pl.ds(part_rows, part_rows), :],
                    ],
                    axis=0,
                ),
            )
        if t == 1:
            own1 = (cut(grad1, 1, tile_rows) * own_column).astype(BF16)
            halve(0, dot_tn(windows(v0, 3, tile_rows), own1))
            if half_ring == 1:
                to_levels()
        if t == 2:
            to_levels()
    to_all(gathered(got_kz, sem_kz), got_ky, sem_ky, y, ring_device)
    head_terms = cut(logit_grad * hidden2.astype(F32), 2, tile_rows) * own_column
    head_out[...] = jnp.sum(head_terms, axis=0, keepdims=True)
    to_all(gathered(got_ky, sem_ky), got_kx, sem_kx, x, across_device)
    for r, rel in enumerate(order):
        for o in range(1, across):
            arrival(returned.at[slot_block(over(o), along(rel))], sem_r.at[1, r, o])
    kernel_out[...] = gathered(got_kx, sem_kx)
    for copy in started:
        copy.wait_send()


def map_step(grid, pillars, recv_cell, cell_mask, occupancy, weights, head_weight):
    n_gy, n_gx, tile_rows, tile_cols = grid
    slots, channels = pillars.shape
    blocks = slots // CHUNK
    count = tile_rows * tile_cols
    width = tile_cols + 2 * SIDE
    height = tile_rows + 2 * HALO
    ring = ring_size(n_gx)
    across, half_ring = n_gx // ring, ring // 2
    _, rows = message_rows(tile_rows, tile_cols)
    vmem = pl.BlockSpec(memory_space=pltpu.VMEM)
    taps = weights.shape[1]
    levels = n_gy // 2
    share = 2 * taps * channels // n_gy
    return pl.pallas_call(
        functools.partial(map_kernel, grid),
        out_shape=(
            jax.ShapeDtypeStruct((slots, channels), BF16),
            jax.ShapeDtypeStruct((share, channels), F32),
            jax.ShapeDtypeStruct((1, channels), F32),
        ),
        in_specs=[vmem] * 6,
        out_specs=(vmem,) * 3,
        scratch_shapes=[
            pltpu.VMEM((ring, count, across * CHUNK), BF16),
            pltpu.VMEM((ring, across * CHUNK, count), BF16),
            pltpu.VMEM((rows, channels), BF16),
            pltpu.VMEM((rows, channels), BF16),
            pltpu.VMEM((rows, channels), BF16),
            pltpu.VMEM((rows, channels), BF16),
            pltpu.VMEM((height * width, 3 * channels), BF16),
            pltpu.VMEM(((height - 2) * width, 3 * channels), BF16),
            pltpu.VMEM(((height - 4) * width, 3 * channels), BF16),
            pltpu.VMEM(((height - 6) * width, 3 * channels), BF16),
            pltpu.VMEM((ring * 8, CHUNK), jnp.int32),
            pltpu.VMEM((ring * 8, CHUNK), jnp.int32),
            pltpu.VMEM((slots, channels), BF16),
            pltpu.VMEM((2, half_ring, count, channels), BF16),
            pltpu.VMEM((2, half_ring, count, channels), BF16),
            pltpu.VMEM((count, channels), BF16),
            pltpu.VMEM((2, half_ring, count, channels), BF16),
            pltpu.VMEM((ring, across * CHUNK, channels), BF16),
            pltpu.VMEM((levels, 2, share, channels), BF16),
            pltpu.VMEM((levels, share, channels), BF16),
            pltpu.VMEM((levels, share, channels), BF16),
            pltpu.VMEM((levels, share, channels), BF16),
            pltpu.VMEM((ring, share, channels), BF16),
            pltpu.VMEM((across, share, channels), BF16),
            pltpu.SemaphoreType.DMA((2, len(STEPS))),
            pltpu.SemaphoreType.DMA((2, len(STEPS))),
            pltpu.SemaphoreType.DMA((2, ring)),
            pltpu.SemaphoreType.DMA((2, ring, across)),
            pltpu.SemaphoreType.DMA((2, 2, half_ring)),
            pltpu.SemaphoreType.DMA((2, 2, half_ring)),
            pltpu.SemaphoreType.DMA((2, ring, across)),
            pltpu.SemaphoreType.DMA((2, 2)),
            pltpu.SemaphoreType.DMA((2, levels)),
            pltpu.SemaphoreType.DMA((2, ring)),
            pltpu.SemaphoreType.DMA((2, across)),
        ],
        compiler_params=pltpu.CompilerParams(
            vmem_limit_bytes=VMEM_LIMIT, collective_id=1, has_side_effects=True
        ),
        name="map_step",
    )(
        pillars,
        recv_cell.reshape(blocks, CHUNK),
        cell_mask.T,
        occupancy.T,
        weights.reshape(2, taps * channels, channels),
        head_weight.reshape(1, channels),
    )


def finish_kernel(
    grid,
    chunk,
    point_local,
    head_local,
    conv_second,
    point_second,
    head_second,
    conv_out,
    point_out,
    head_out,
    second,
    own_s,
    got_sz,
    got_sc,
    got_sy,
    got_sx,
    sem_l,
    sem_a,
    sem_p,
    sem_sz,
    sem_sc,
    sem_sy,
    sem_sx,
):
    n_gy, n_gx, _, _ = grid
    gy, gx = lax.axis_index("gy"), lax.axis_index("gx")
    ring = ring_size(n_gx)
    across = n_gx // ring
    levels = n_gy // 2
    x, y = gx // ring, lax.rem(gx, ring)
    z, core = gy // 2, lax.rem(gy, 2)
    share = chunk.shape[0]

    def level_device(step):
        return lax.rem(z + step, levels) * 2 + core, gx

    def ring_device(step):
        return gy, x * ring + lax.rem(y + step, ring)

    def across_device(step):
        return gy, lax.rem(x + step, across) * ring + y

    def core_device(step):
        return z * 2 + lax.rem(core + step, 2), gx

    def remote(src, dst, send, recv, device):
        return pltpu.make_async_remote_copy(
            src_ref=src,
            dst_ref=dst,
            send_sem=send,
            recv_sem=recv,
            device_id=device,
            device_id_type=MESH,
        )

    def arrival(ref, sem):
        remote(ref, ref, sem, sem, core_device(1)).wait_recv()

    load = pltpu.make_async_copy(
        conv_second.at[pl.ds(pl.multiple_of(gy * share, 8), share)], second, sem_l
    )
    load.start()
    barrier = pltpu.get_barrier_semaphore()
    partners = [ring_device(step) for step in range(1, ring)]
    partners += [across_device(step) for step in range(1, across)]
    partners += [level_device(step) for step in range(1, levels)] + [core_device(1)]
    for device in partners:
        pl.semaphore_signal(barrier, inc=1, device_id=device, device_id_type=MESH)
    pl.semaphore_wait(barrier, len(partners))

    started = []

    def go(copy):
        copy.start()
        started.append(copy)

    def to_all(value, got, sem, me, device):
        got[me] = value
        for step in range(1, got.shape[0]):
            go(remote(got.at[me], got.at[me], sem.at[0, step], sem.at[1, step], device(step)))

    def gathered(got, sem):
        for step in range(1, got.shape[0]):
            arrival(got.at[0], sem.at[1, step])
        summed = got[0]
        for k in range(1, got.shape[0]):
            summed = summed + got[k]
        return summed

    own_s[...] = jnp.zeros_like(own_s)
    own_s[0 : point_local.shape[0], :] = point_local[...]
    own_s[point_local.shape[0] : point_local.shape[0] + 1, :] = head_local[...]
    to_all(own_s[...], got_sy, sem_sy, y, ring_device)
    load.wait()
    conv_out[z * 2 + core] = rms_step(chunk[...], second[...]).astype(BF16)
    mine = conv_out.at[z * 2 + core]
    for step in range(1, levels):
        go(remote(mine, mine, sem_a.at[0, step], sem_a.at[1, step], level_device(step)))
    go(remote(mine, mine, sem_p.at[0, 0], sem_p.at[1, 0], core_device(1)))
    to_all(gathered(got_sy, sem_sy), got_sx, sem_sx, x, across_device)
    small = None
    for step in range(1, levels):
        level = lax.rem(z - step + levels, levels)
        held = conv_out.at[level * 2 + core]
        arrival(held, sem_a.at[1, step])
        go(remote(held, held, sem_p.at[0, step], sem_p.at[1, step], core_device(1)))
        if step == min(2, levels - 1):
            to_all(gathered(got_sx, sem_sx), got_sc, sem_sc, core, core_device)
        if step == min(4, levels - 1):
            to_all(gathered(got_sc, sem_sc), got_sz, sem_sz, z, level_device)
    small = gathered(got_sz, sem_sz)
    features = point_local.shape[0]
    point_out[...] = rms_step(small[:features], point_second[...])
    head_out[...] = rms_step(small[features : features + 1], head_second[...])
    for step in range(levels):
        level = lax.rem(z - step + levels, levels)
        arrival(conv_out.at[level * 2 + 1 - core], sem_p.at[1, step])
    for copy in started:
        copy.wait_send()


def finish(grid, chunk, point_local, head_local, conv_second, point_second, head_second):
    n_gy, n_gx, _, _ = grid
    share, channels = chunk.shape
    ring = ring_size(n_gx)
    across, levels = n_gx // ring, n_gy // 2
    rows = -(-(point_local.shape[0] + 1) // 8) * 8
    vmem = pl.BlockSpec(memory_space=pltpu.VMEM)
    return pl.pallas_call(
        functools.partial(finish_kernel, grid),
        out_shape=(
            jax.ShapeDtypeStruct((n_gy, share, channels), BF16),
            jax.ShapeDtypeStruct(point_local.shape, F32),
            jax.ShapeDtypeStruct((1, channels), F32),
        ),
        in_specs=[vmem, vmem, vmem, pl.BlockSpec(memory_space=pl.ANY), vmem, vmem],
        out_specs=(vmem,) * 3,
        scratch_shapes=[
            pltpu.VMEM((share, channels), F32),
            pltpu.VMEM((rows, channels), F32),
            pltpu.VMEM((levels, rows, channels), F32),
            pltpu.VMEM((2, rows, channels), F32),
            pltpu.VMEM((ring, rows, channels), F32),
            pltpu.VMEM((across, rows, channels), F32),
            pltpu.SemaphoreType.DMA,
            pltpu.SemaphoreType.DMA((2, levels)),
            pltpu.SemaphoreType.DMA((2, levels)),
            pltpu.SemaphoreType.DMA((2, levels)),
            pltpu.SemaphoreType.DMA((2, 2)),
            pltpu.SemaphoreType.DMA((2, ring)),
            pltpu.SemaphoreType.DMA((2, across)),
        ],
        compiler_params=pltpu.CompilerParams(
            vmem_limit_bytes=VMEM_LIMIT, collective_id=2, has_side_effects=True
        ),
        name="finish",
    )(
        chunk,
        point_local,
        head_local,
        conv_second.reshape(n_gy * share, channels),
        point_second,
        head_second.reshape(1, channels),
    )


def on_device(
    points,
    point_pillar,
    point_weight,
    recv_cell,
    cell_mask,
    occupancy,
    conv_weight,
    head_weight,
    conv_second,
    point_second,
    head_second,
):
    rows, columns = lax.axis_size("gy"), lax.axis_size("gx")
    tile_rows, tile_cols = cell_mask.shape
    channels = point_weight.shape[1]
    slots = recv_cell.shape[0]
    grid = (rows, columns, tile_rows, tile_cols)

    pillars, table, local, counts = pool(points, point_pillar, point_weight, slots)
    returned, kernels, head_local = map_step(
        grid, pillars, recv_cell, cell_mask, occupancy, conv_weight, head_weight
    )
    point_local = point_grad(points, local, point_weight, table, counts, returned)
    conv_step, point_step, head_step = finish(
        grid, kernels, point_local, head_local, conv_second, point_second, head_second
    )
    return conv_step.astype(F32).reshape(conv_second.shape), point_step, head_step[0]


def solution(mesh):
    return jax.shard_map(
        on_device,
        mesh=mesh,
        in_specs=(
            P(None, ("gy", "gx")),
            P(("gy", "gx")),
            P(),
            P(("gy", "gx")),
            P("gy", "gx"),
            P("gy", "gx"),
            P(),
            P(),
            P(),
            P(),
            P(),
        ),
        out_specs=(P(), P(), P()),
        check_vma=False,
    )
```

```python
import functools

import jax
import jax.numpy as jnp
from jax import lax
from jax.experimental import pallas as pl
from jax.experimental.pallas import tpu as pltpu
from jax.sharding import PartitionSpec as P

MESH = pl.DeviceIdType.MESH
F32 = jnp.float32
BF16 = jnp.bfloat16
VMEM_LIMIT = 56 * 1024 * 1024
CHUNK = 128
SIDE = 8
HALO = 4
STEPS = ((0, -1), (0, 1), (-1, 0), (1, 0), (-1, -1), (1, 1), (-1, 1), (1, -1))


def iota(shape, dim):
    return lax.broadcasted_iota(jnp.int32, shape, dim)


def dot(a, b):
    return jnp.dot(a, b, preferred_element_type=F32)


def dot_nt(a, b):
    return lax.dot_general(a, b, (((1,), (1,)), ((), ())), preferred_element_type=F32)


def dot_tn(a, b):
    return lax.dot_general(a, b, (((0,), (0,)), ((), ())), preferred_element_type=F32)


def slope(value):
    sig = jax.nn.sigmoid(value)
    return sig * (1.0 + value * (1.0 - sig))


def rms_step(gradient, second):
    moment = 0.95 * second + 0.05 * gradient * gradient
    return gradient / (jnp.sqrt(moment) + 1e-08)


def pool_kernel(
    points, ids, ids_row, weight, pillars, table, local, counts, table_s, partial, sums, numbers, sem
):
    chunks = ids.shape[0]
    blocks = pillars.shape[0] // CHUNK
    total = chunks * CHUNK
    here = ids[...]
    back = pltpu.roll(here, 1, axis=1)
    lane = iota(here.shape, 1)
    before = jnp.where(lane == 0, pltpu.roll(back, 1, axis=0), back)
    first = (lane == 0) & (iota(here.shape, 0) == 0)
    flags = jnp.where((here != before) | first, 1.0, 0.0).astype(BF16)
    upto = jnp.where(iota((CHUNK, CHUNK), 0) <= iota((CHUNK, CHUNK), 1), 1.0, 0.0).astype(BF16)
    inside = dot(flags, upto)
    whole = dot(flags, jnp.ones((CHUNK, CHUNK), BF16))
    lower = jnp.where(iota((chunks, chunks), 0) > iota((chunks, chunks), 1), 1.0, 0.0)
    ahead = dot(lower.astype(BF16), whole.astype(BF16))
    head = jnp.broadcast_to(inside[:, 0:1], inside.shape)
    local[...] = (inside - head).astype(jnp.int32)
    row = ids_row[...]
    row_before = pltpu.roll(row, 1, axis=1)
    row_first = (row != row_before) | (iota(row.shape, 1) == 0)
    row_block = jnp.where(row_first, row // CHUNK, blocks + 8)
    below = jnp.where(row_block < iota((blocks + 8, total), 0), 1.0, 0.0).astype(BF16)
    table[0:chunks, :] = (ahead + head - 1.0).astype(jnp.int32)
    table[chunks : chunks + blocks + 8, :] = dot(below, jnp.ones((total, CHUNK), BF16)).astype(
        jnp.int32
    )
    copy = pltpu.make_async_copy(table, table_s, sem)
    copy.start()
    ranks = local[...]
    for k in range(chunks):
        part = pl.ds(k * CHUNK, CHUNK)
        pre = dot_tn(points[:, part], weight[...])
        act = (pre * jax.nn.sigmoid(pre)).astype(BF16)
        pick = jnp.where(iota((CHUNK, CHUNK), 0) == ranks[k : k + 1, :], 1.0, 0.0).astype(BF16)
        partial[part, :] = dot(pick, jnp.concatenate([act, jnp.ones_like(act)], axis=1))
    copy.wait()
    edge = jnp.zeros((8, CHUNK), F32)
    for k in range(chunks):
        at = table_s[k, 0]
        for side, compact in enumerate((sums, numbers)):
            got = partial[pl.ds(k * CHUNK, CHUNK), pl.ds(side * CHUNK, CHUNK)]
            first_rows = got[0:8] if k == 0 else compact[pl.ds(at, 8), :] + got[0:8]
            compact[pl.ds(at, CHUNK + 8), :] = jnp.concatenate([first_rows, got[8:], edge], axis=0)
    diagonal = iota((CHUNK, CHUNK), 0) == iota((CHUNK, CHUNK), 1)
    for d in range(blocks):
        at = table_s[chunks + d, 0]
        held = table_s[chunks + d + 1, 0] - at
        named = iota((CHUNK, CHUNK), 0) < held
        count = jnp.where(named, numbers[pl.ds(at, CHUNK), :], 1.0)
        mean = jnp.where(named, sums[pl.ds(at, CHUNK), :] / count, 0.0)
        pillars[pl.ds(d * CHUNK, CHUNK), :] = mean.astype(BF16)
        counts[d : d + 1, :] = jnp.sum(jnp.where(diagonal, count, 0.0), axis=0, keepdims=True)


def pool(points, point_pillar, weight, slots):
    total = point_pillar.shape[0]
    chunks, blocks = total // CHUNK, slots // CHUNK
    channels = weight.shape[1]
    rows = chunks + blocks + 8
    vmem = pl.BlockSpec(memory_space=pltpu.VMEM)
    return pl.pallas_call(
        pool_kernel,
        out_shape=(
            jax.ShapeDtypeStruct((slots, channels), BF16),
            jax.ShapeDtypeStruct((rows, CHUNK), jnp.int32),
            jax.ShapeDtypeStruct((chunks, CHUNK), jnp.int32),
            jax.ShapeDtypeStruct((blocks, CHUNK), F32),
        ),
        in_specs=[vmem] * 4,
        out_specs=(vmem,) * 4,
        scratch_shapes=[
            pltpu.SMEM((rows, CHUNK), jnp.int32),
            pltpu.VMEM((total, 2 * CHUNK), F32),
            pltpu.VMEM((total + 2 * CHUNK, CHUNK), F32),
            pltpu.VMEM((total + 2 * CHUNK, CHUNK), F32),
            pltpu.SemaphoreType.DMA,
        ],
        compiler_params=pltpu.CompilerParams(vmem_limit_bytes=VMEM_LIMIT),
        name="pool",
    )(points, point_pillar.reshape(chunks, CHUNK), point_pillar.reshape(1, total), weight)


def message_rows(tile_rows, tile_cols):
    spans, at = [], 0
    for down, right in STEPS:
        size = (HALO if down else tile_rows) * (SIDE if right else tile_cols)
        spans.append((at, size))
        at += size
    return spans, at


def ring_size(columns):
    return {32: 8, 8: 4, 4: 2}[columns]


def ring_order(ring):
    order = [ring // 2]
    for far in range(ring // 2 - 1, 0, -1):
        order += [far, -far]
    return order + [0]


def map_kernel(
    grid,
    pillars,
    cells,
    mask_t,
    occupied_t,
    weights,
    head_row,
    points,
    local,
    point_weight,
    table,
    counts,
    conv_second,
    point_second,
    head_second,
    conv_out,
    point_out,
    head_out,
    place,
    pick,
    send_f,
    got_f,
    send_m,
    got_m,
    v0,
    v1,
    v2,
    v3,
    send_i,
    got_i,
    got_x,
    send_y,
    got_y,
    own_g,
    got_g,
    send_r,
    returned,
    own_k,
    core_k,
    send_k,
    got_kz,
    send_kx,
    got_kx,
    got_ky,
    got_ax,
    second,
    merge_a,
    merge_b,
    slopes,
    picks,
    rows_b,
    own_s,
    got_sy,
    got_sx,
    got_sz,
    sem_f,
    sem_m,
    sem_i,
    sem_x,
    sem_y,
    sem_g,
    sem_r,
    sem_c,
    sem_kz,
    sem_kx,
    sem_ky,
    sem_ax,
    sem_az,
    sem_ac,
    sem_sy,
    sem_sx,
    sem_sz,
    sem_l,
):
    n_gy, n_gx, tile_rows, tile_cols = grid
    gy, gx = lax.axis_index("gy"), lax.axis_index("gx")
    ring = ring_size(n_gx)
    across = n_gx // ring
    half_ring = ring // 2
    order = ring_order(ring)
    slot_of = {rel: r for r, rel in enumerate(order)}
    slot_of[-half_ring] = slot_of[half_ring]
    x, y = gx // ring, lax.rem(gx, ring)
    channels = pillars.shape[1]
    spans, _ = message_rows(tile_rows, tile_cols)
    width = tile_cols + 2 * SIDE
    height = tile_rows + 2 * HALO
    count = tile_rows * tile_cols
    part_rows = count // 2
    fan = across * CHUNK

    def neighbour(k):
        down, right = STEPS[k]
        return lax.rem(gy + down + n_gy, n_gy), lax.rem(gx + right + n_gx, n_gx)

    def along(step):
        return lax.rem(y + step + ring, ring)

    def over(step):
        return lax.rem(x + step + across, across)

    def ring_device(step):
        return gy, x * ring + along(step)

    def across_device(step):
        return gy, over(step) * ring + y

    levels = n_gy // 2
    z, core = gy // 2, lax.rem(gy, 2)

    def level_device(step):
        return lax.rem(z + step, levels) * 2 + core, gx

    other_core = (z * 2 + 1 - core, gx)

    def stack_device(step):
        return lax.rem(gy + step, n_gy), gx

    def slot_block(column, place_on_ring):
        return pl.ds(pl.multiple_of((column * ring + place_on_ring) * CHUNK, CHUNK), CHUNK)

    def remote(src, dst, send, recv, device):
        return pltpu.make_async_remote_copy(
            src_ref=src,
            dst_ref=dst,
            send_sem=send,
            recv_sem=recv,
            device_id=device,
            device_id_type=MESH,
        )

    def arrival(ref, sem):
        remote(ref, ref, sem, sem, ring_device(1)).wait_recv()

    share = own_k.shape[2]
    piece = got_ky.shape[1]
    load = pltpu.make_async_copy(
        conv_second.at[pl.ds(pl.multiple_of(gy * share, 8), share)],
        second.at[pl.ds(0, share)],
        sem_l,
    )
    load.start()
    barrier = pltpu.get_barrier_semaphore()
    partners = [neighbour(k) for k in range(len(STEPS))]
    partners += [ring_device(step) for step in range(1, ring)]
    partners += [across_device(step) for step in range(1, across)]
    partners += [stack_device(step) for step in range(1, n_gy)]
    for device in partners:
        pl.semaphore_signal(barrier, inc=1, device_id=device, device_id_type=MESH)
    pl.semaphore_wait(barrier, len(partners))

    started = []

    def go(copy):
        copy.start()
        started.append(copy)

    def send_pillars(r):
        for o in range(1, across):
            go(
                remote(
                    pillars.at[slot_block(over(o), along(order[r]))],
                    got_x.at[pl.ds((r * across + o) * CHUNK, CHUNK)],
                    sem_x.at[0, r, o],
                    sem_x.at[1, r, o],
                    across_device(o),
                )
            )

    for r in range(min(3, ring)):
        send_pillars(r)

    send_i[...] = jnp.zeros_like(send_i)
    for step in range(ring):
        lead = step * 8
        for o in range(across):
            row = over(-o) * ring + along(step)
            send_i[lead + o : lead + o + 1, :] = cells[pl.ds(row, 1), :]
        if step == 0:
            got_i[pl.ds(slot_of[0] * 8, 8), :] = send_i[pl.ds(0, 8), :]
        else:
            rel = -step if step <= half_ring else ring - step
            slot = slot_of[rel]
            go(
                remote(
                    send_i.at[pl.ds(lead, 8)],
                    got_i.at[pl.ds(slot * 8, 8)],
                    sem_i.at[0, step],
                    sem_i.at[1, slot],
                    ring_device(step),
                )
            )

    def post(own, send, got, sem):
        grid3 = own.reshape(tile_rows, tile_cols, channels)
        for k, (down, right) in enumerate(STEPS):
            part = grid3
            if down:
                part = part[:HALO] if down < 0 else part[tile_rows - HALO :]
            if right:
                part = part[:, :SIDE] if right < 0 else part[:, tile_cols - SIDE :]
            at, size = spans[k]
            send[pl.ds(at, size), :] = part.reshape(size, channels).astype(BF16)
            there, _ = spans[k ^ 1]
            go(
                remote(
                    send.at[pl.ds(at, size)],
                    got.at[pl.ds(there, size)],
                    sem.at[0, k],
                    sem.at[1, k ^ 1],
                    neighbour(k),
                )
            )

    def collect(own, got, sem):
        parts = {}
        for k, (down, right) in enumerate(STEPS):
            at, size = spans[k]
            arrival(got.at[pl.ds(at, size)], sem.at[1, k])
            rows = HALO if down else tile_rows
            parts[down, right] = (
                got[pl.ds(at, size), :].astype(F32).reshape(rows, size // rows, channels)
            )
        parts[0, 0] = own.reshape(tile_rows, tile_cols, channels)
        return jnp.concatenate(
            [
                jnp.concatenate([parts[down, right] for right in (-1, 0, 1)], axis=1).reshape(
                    -1, channels
                )
                for down in (-1, 0, 1)
            ],
            axis=0,
        )

    masks = jnp.concatenate([mask_t[...], mask_t[...] * occupied_t[...]], axis=0)
    masks = masks.astype(F32).astype(BF16)
    of_row = iota((count, tile_rows), 0) // tile_cols == iota((count, tile_rows), 1)
    by_column = dot_nt(jnp.where(of_row, 1.0, 0.0).astype(BF16), masks)
    pairs = (count, 2 * tile_cols)
    of_column = iota(pairs, 0) % tile_cols == iota(pairs, 1) % tile_cols
    halves = (2 * tile_cols, channels)
    same_half = (iota(halves, 0) < tile_cols) == (iota(halves, 1) < channels // 2)
    mask_own = dot(
        jnp.where(of_column, by_column, 0.0).astype(BF16),
        jnp.where(same_half, 1.0, 0.0).astype(BF16),
    )
    post(mask_own, send_m, got_m, sem_m)

    flat = iota((height * width, channels), 0)
    row = flat // width + gy * tile_rows - HALO
    col = flat % width + gx * tile_cols - SIDE
    in_slab = jnp.where(
        (row >= 0) & (row < n_gy * tile_rows) & (col >= 0) & (col < n_gx * tile_cols), 1.0, 0.0
    )
    column = iota((tile_rows * width, channels), 0) % width
    own_column = jnp.where((column >= SIDE) & (column < SIDE + tile_cols), 1.0, 0.0)

    for r in range(ring - 1):
        arrival(got_i.at[pl.ds(r * 8, 8)], sem_i.at[1, r])
    rows_i = ring * 8
    cells_i = got_i[...]
    cells_t = jnp.concatenate(
        [cells_i.astype(F32), jnp.zeros(((-rows_i) % CHUNK, CHUNK), F32)], axis=0
    ).T.astype(jnp.int32)
    def build_place(r):
        for o in range(across):
            at = r * 8 + o
            place[r, :, pl.ds(o * CHUNK, CHUNK)] = jnp.where(
                iota((count, CHUNK), 0) == cells_i[at : at + 1, :], 1.0, 0.0
            ).astype(BF16)

    def build_pick(r):
        for o in range(across):
            at = r * 8 + o
            pick[r, pl.ds(o * CHUNK, CHUNK), :] = jnp.where(
                cells_t[:, at : at + 1] == iota((CHUNK, count), 1), 1.0, 0.0
            ).astype(BF16)

    def cut(value, lead, rows):
        return value[lead * width : (lead + rows) * width]

    def side_by_side(value, ref):
        size = value.shape[0]
        left = pltpu.roll(value, 1, axis=0)
        right = pltpu.roll(value, size - 1, axis=0)
        ref[...] = jnp.concatenate([left.astype(BF16), value.astype(BF16), right.astype(BF16)], 1)

    def windows(ref, lead, rows):
        return jnp.concatenate(
            [ref[pl.ds((lead + a) * width, rows * width), :] for a in (0, 1, 2)], axis=1
        )

    def flipped(layer):
        return jnp.concatenate(
            [weights[layer, pl.ds((8 - k) * channels, channels), :] for k in range(9)], axis=1
        )

    def placed_for(r):
        for o in range(1, across):
            arrival(got_x.at[pl.ds((r * across + o) * CHUNK, CHUNK)], sem_x.at[1, r, o])
        own = pillars[slot_block(x, along(order[r])), :]
        rest = got_x[pl.ds((r * across + 1) * CHUNK, fan - CHUNK), :]
        return dot(place[r], jnp.concatenate([own, rest], axis=0))

    halves = (pl.ds(0, part_rows), pl.ds(part_rows, part_rows))

    def half_of(value, half):
        return value[half * part_rows : (half + 1) * part_rows]

    def grow(t, side, half, value):
        if t > 1 or (t == 1 and half == side):
            arrival(got_y.at[side, t - 1, halves[half]], sem_y.at[1, side, t - 1, half])
            value = value + got_y[side, t - 1, halves[half], :].astype(F32)
        send_y[side, t, halves[half], :] = value.astype(BF16)
        go(
            remote(
                send_y.at[side, t, halves[half]],
                got_y.at[side, t, halves[half]],
                sem_y.at[0, side, t, half],
                sem_y.at[1, side, t, half],
                ring_device(1 - 2 * side),
            )
        )

    left = list(range(ring))
    for t in range(half_ring):
        for r in range(2 * t + 1, min(2 * t + 3, ring)) if t else ():
            send_pillars(r)
        if t == 0:
            build_place(0)
            summed = placed_for(0)
            for side in (0, 1):
                grow(0, side, side, half_of(summed, side))
        else:
            summed = {}
            for side in (0, 1):
                r = slot_of[(1 - 2 * side) * (half_ring - t)]
                build_place(r)
                summed[side] = placed_for(r)
                if t == 1:
                    grow(t, side, 1 - side, half_of(summed[side], 1 - side))
            for order_half in (0, 1):
                for side in (0, 1):
                    half = 1 - side if order_half == 0 else side
                    if t > 1 or half == side:
                        grow(t, side, half, half_of(summed[side], half))
        for r in left[:2]:
            build_pick(r)
        left = left[2:]
    build_place(slot_of[0])
    placed = placed_for(slot_of[0])
    for r in left:
        build_pick(r)
    mask_all = (collect(mask_own, got_m, sem_m) * in_slab).astype(BF16)
    half = channels // 2
    spread = jnp.where(
        iota((channels, 2 * channels), 0)
        == jnp.where(iota((channels, 2 * channels), 1) < channels, 0, half),
        1.0,
        0.0,
    ).astype(BF16)
    mask_all = dot(mask_all, spread)
    hidden_cell = mask_all[:, :channels]
    target = mask_all[:, channels:]

    visible = 1.0 - cut(hidden_cell, HALO, tile_rows).reshape(tile_rows, width, channels)[
        :, SIDE : SIDE + tile_cols
    ].reshape(count, channels)

    last = half_ring - 1
    ends = []
    for half in (0, 1):
        value = half_of(placed, half)
        for side in (0, 1):
            if last or half == side:
                arrival(got_y.at[side, last, halves[half]], sem_y.at[1, side, last, half])
                value = value + got_y[side, last, halves[half], :].astype(F32)
        ends.append(value)
    placed = jnp.concatenate(ends, axis=0)
    features = (placed * visible).astype(BF16).astype(F32)
    post(features, send_f, got_f, sem_f)
    side_by_side(collect(features, got_f, sem_f) * in_slab, v0)

    pre1 = dot(windows(v0, 0, height - 2), weights[0])
    side_by_side(pre1 * jax.nn.sigmoid(pre1) * cut(in_slab, 1, height - 2), v1)
    pre2 = dot(windows(v1, 0, height - 4), weights[1])
    sig2 = jax.nn.sigmoid(pre2)
    hidden2 = (pre2 * sig2).astype(BF16)
    head = jnp.broadcast_to(head_row[...], (channels, channels))
    logits = dot_nt(hidden2, head)
    cells_all = n_gy * tile_rows * n_gx * tile_cols
    logit_grad = (
        cut(hidden_cell, 2, height - 4) * jax.nn.sigmoid(logits) - cut(target, 2, height - 4)
    ) / cells_all
    grad2 = logit_grad * head_row[...].astype(F32) * (sig2 * (1.0 + pre2 * (1.0 - sig2)))
    side_by_side(grad2, v2)
    back2 = dot_nt(windows(v2, 0, height - 6), flipped(1))
    grad1 = back2 * slope(cut(pre1, 2, height - 6)) * cut(in_slab, 3, height - 6)
    side_by_side(grad1, v3)
    back1 = dot_nt(windows(v3, 0, tile_rows), flipped(0))
    back1 = back1.reshape(tile_rows, width, channels)[:, SIDE : SIDE + tile_cols].reshape(
        count, channels
    )
    own_g[...] = (back1 * visible).astype(BF16)

    def pass_on(t, side, half):
        src = own_g if t == 1 else got_g.at[side, t - 2]
        go(
            remote(
                src.at[halves[half]],
                got_g.at[side, t - 1, halves[half]],
                sem_g.at[0, side, t - 1, half],
                sem_g.at[1, side, t - 1, half],
                ring_device(1 - 2 * side),
            )
        )

    def hand_out(rel, gradient):
        r = slot_of[rel]
        rows = dot(pick[r], gradient).astype(BF16)
        returned[slot_block(x, along(rel)), :] = rows[:CHUNK]
        send_r[r] = rows
        for o in range(1, across):
            go(
                remote(
                    send_r.at[r, pl.ds(o * CHUNK, CHUNK)],
                    returned.at[slot_block(x, along(rel))],
                    sem_r.at[0, r, o],
                    sem_r.at[1, r, o],
                    across_device(-o),
                )
            )

    parts = levels // 2

    def halve(layer, gradient):
        own_k[pl.ds(layer * parts, parts)] = gradient.reshape(
            parts, 2, share, channels
        ).astype(BF16)
        go(
            remote(
                own_k.at[pl.ds(layer * parts, parts), 1 - core],
                core_k.at[pl.ds(layer * parts, parts)],
                sem_c.at[0, layer],
                sem_c.at[1, layer],
                other_core,
            )
        )

    def to_levels():
        for layer in (0, 1):
            arrival(core_k.at[pl.ds(layer * parts, parts)], sem_c.at[1, layer])
        for k in range(levels):
            send_k[k] = (own_k[k, core].astype(F32) + core_k[k].astype(F32)).astype(BF16)
        got_kz[z] = send_k[z]
        for step in range(1, levels):
            go(
                remote(
                    send_k.at[lax.rem(z + step, levels)],
                    got_kz.at[z],
                    sem_kz.at[0, step],
                    sem_kz.at[1, step],
                    level_device(step),
                )
            )

    def gathered(got, sem):
        summed = None
        for step in range(1, got.shape[0]):
            arrival(got.at[0], sem.at[1, step])
        for k in range(got.shape[0]):
            term = got[k].astype(F32)
            summed = term if summed is None else summed + term
        return summed

    def to_all(value, got, sem, me, device):
        got[me] = value.astype(got.dtype)
        for step in range(1, got.shape[0]):
            go(remote(got.at[me], got.at[me], sem.at[0, step], sem.at[1, step], device(step)))

    def to_pieces(summed):
        spare = across * piece - share
        if spare:
            summed = jnp.concatenate([summed, jnp.zeros((spare, channels), F32)], axis=0)
        send_kx[...] = summed.reshape(across, piece, channels).astype(BF16)
        got_kx[x] = send_kx[x]
        for step in range(1, across):
            go(
                remote(
                    send_kx.at[over(step)],
                    got_kx.at[x],
                    sem_kx.at[0, step],
                    sem_kx.at[1, step],
                    across_device(step),
                )
            )

    def take_step(summed):
        load.wait()
        if across * piece > share:
            second[pl.ds(share, across * piece - share), :] = jnp.ones(
                (across * piece - share, channels), F32
            )
        rows = pl.ds(pl.multiple_of(x * piece, 8), piece)
        return rms_step(summed, second[rows, :])

    chunks = local.shape[0]
    blocks = counts.shape[0]

    def turned(value):
        spare = (-value.shape[0]) % CHUNK
        return jnp.concatenate([value, jnp.zeros((spare, CHUNK), F32)], axis=0).T

    ranks_t = turned(local[...].astype(F32)).astype(jnp.int32)

    def prepare(begin, end):
        for k in range(begin, end):
            part = pl.ds(k * CHUNK, CHUNK)
            slopes[part, :] = slope(dot_tn(points[:, part], point_weight[...]))
            picks[part, :] = jnp.where(
                ranks_t[:, k : k + 1] == iota((CHUNK, CHUNK), 1), 1.0, 0.0
            ).astype(BF16)

    scale = turned(1.0 / counts[...])

    def start_merge():
        for d in range(blocks):
            part = pl.ds(d * CHUNK, CHUNK)
            merge_a[part, :] = returned[part, :].astype(F32) * scale[:, d : d + 1]
        spare = merge_a.shape[0] - blocks * CHUNK
        for ref in (merge_a, merge_b):
            ref[pl.ds(blocks * CHUNK, spare), :] = jnp.zeros((spare, CHUNK), F32)

    def merge_level(level, src, dst):
        size = CHUNK << level
        for pair in range(blocks >> (level + 1)):
            lead = pair * 2 * size
            first = chunks + pair * (2 << level)
            held = table[first + (1 << level), 0] - table[first, 0]
            for at in range(0, 2 * size, 2 * CHUNK):
                rows = iota((2 * CHUNK, CHUNK), 0) + at
                dst[pl.ds(lead + at, 2 * CHUNK), :] = jnp.where(
                    rows < held,
                    src[pl.ds(lead + at, 2 * CHUNK), :],
                    src[pl.ds(lead + at + size - held, 2 * CHUNK), :],
                )

    levels_m = blocks.bit_length() - 1
    refs = (merge_a, merge_b)

    def merge(begin, end):
        for level in range(begin, end):
            merge_level(level, refs[level % 2], refs[1 - level % 2])

    def point_terms():
        joined = refs[levels_m % 2]
        for k in range(chunks):
            part = pl.ds(k * CHUNK, CHUNK)
            window = joined[pl.ds(table[k, 0], CHUNK), :].astype(BF16)
            rows_b[part, :] = (dot(picks[part, :], window) * slopes[part, :]).astype(BF16)
        return dot(points[...], rows_b[...])

    for order_half in (0, 1):
        for side in (0, 1):
            pass_on(1, side, side if order_half == 0 else 1 - side)
    own1 = (cut(grad1, 1, tile_rows) * own_column).astype(BF16)
    halve(0, dot_tn(windows(v0, 3, tile_rows), own1))
    own2 = (cut(grad2, 2, tile_rows) * own_column).astype(BF16)
    halve(1, dot_tn(windows(v1, 2, tile_rows), own2))
    hand_out(0, own_g[...])
    head_terms = cut(logit_grad * hidden2.astype(F32), 2, tile_rows) * own_column
    head_local = jnp.sum(head_terms, axis=0, keepdims=True)
    prepared = 0
    for t in range(1, half_ring + 1):
        if t < half_ring:
            for order_half in (0, 1):
                for side in (0, 1):
                    half = side if order_half == 0 else 1 - side
                    arrival(got_g.at[side, t - 1, halves[half]], sem_g.at[1, side, t - 1, half])
                    if t + 1 < half_ring or order_half == 0:
                        pass_on(t + 1, side, half)
        else:
            for side in (0, 1):
                arrival(got_g.at[side, t - 1, halves[side]], sem_g.at[1, side, t - 1, side])
        if t == 1:
            to_levels()
        if t == half_ring:
            to_pieces(gathered(got_kz, sem_kz))
            hand_out(
                t,
                jnp.concatenate(
                    [got_g[side, t - 1, halves[side], :] for side in (0, 1)], axis=0
                ),
            )
        else:
            hand_out(-t, got_g[0, t - 1])
            hand_out(t, got_g[1, t - 1])
        share_to = chunks * t // half_ring
        prepare(prepared, share_to)
        prepared = share_to
    to_all(gathered(got_kx, sem_kx), got_ky, sem_ky, y, ring_device)
    for r, rel in enumerate(order):
        for o in range(1, across):
            arrival(returned.at[slot_block(over(o), along(rel))], sem_r.at[1, r, o])
    start_merge()
    merge(0, min(2, levels_m))
    to_all(take_step(gathered(got_ky, sem_ky)), got_ax, sem_ax, x, across_device)
    merge(min(2, levels_m), levels_m)
    for step in range(1, across):
        arrival(got_ax.at[0], sem_ax.at[1, step])
    conv_out[gy] = got_ax[...].reshape(across * piece, channels)[:share]
    mine = conv_out.at[gy]
    for step in range(1, levels):
        go(remote(mine, mine, sem_az.at[0, step], sem_az.at[1, step], level_device(step)))
    go(remote(mine, mine, sem_ac.at[0, 0], sem_ac.at[1, 0], other_core))
    features_in = points.shape[0]
    own_s[...] = jnp.zeros_like(own_s)
    own_s[0:features_in, :] = point_terms()
    own_s[features_in : features_in + 1, :] = head_local
    to_all(own_s[...], got_sy, sem_sy, y, ring_device)

    def relay(begin, end):
        for step in range(begin, end):
            held = conv_out.at[lax.rem(z - step + levels, levels) * 2 + core]
            arrival(held, sem_az.at[1, step])
            go(remote(held, held, sem_ac.at[0, step], sem_ac.at[1, step], other_core))

    relay(1, min(3, levels))
    to_all(gathered(got_sy, sem_sy), got_sx, sem_sx, x, across_device)
    relay(min(3, levels), min(6, levels))
    to_all(gathered(got_sx, sem_sx), got_sz, sem_sz, gy, stack_device)
    relay(min(6, levels), levels)
    small = gathered(got_sz, sem_sz)
    point_out[...] = rms_step(small[:features_in], point_second[...])
    head_out[...] = rms_step(small[features_in : features_in + 1], head_second[...])
    for step in range(levels):
        level = lax.rem(z - step + levels, levels)
        arrival(conv_out.at[level * 2 + 1 - core], sem_ac.at[1, step])
    for copy in started:
        copy.wait_send()


def map_step(grid, pillars, recv_cell, cell_mask, occupancy, weights, head_weight, points, local,
             point_weight, table, counts, conv_second, point_second, head_second):
    n_gy, n_gx, tile_rows, tile_cols = grid
    slots, channels = pillars.shape
    total = points.shape[1]
    blocks = slots // CHUNK
    count = tile_rows * tile_cols
    width = tile_cols + 2 * SIDE
    height = tile_rows + 2 * HALO
    ring = ring_size(n_gx)
    across, half_ring = n_gx // ring, ring // 2
    _, rows = message_rows(tile_rows, tile_cols)
    vmem = pl.BlockSpec(memory_space=pltpu.VMEM)
    smem = pl.BlockSpec(memory_space=pltpu.SMEM)
    taps = weights.shape[1]
    levels = n_gy // 2
    share = 2 * taps * channels // n_gy
    piece = -(-share // (across * 16)) * 16
    few = -(-(points.shape[0] + 1) // 8) * 8
    return pl.pallas_call(
        functools.partial(map_kernel, grid),
        out_shape=(
            jax.ShapeDtypeStruct((n_gy, share, channels), BF16),
            jax.ShapeDtypeStruct(point_weight.shape, F32),
            jax.ShapeDtypeStruct((1, channels), F32),
        ),
        in_specs=[vmem] * 9 + [smem, vmem, pl.BlockSpec(memory_space=pl.ANY), vmem, vmem],
        out_specs=(vmem,) * 3,
        scratch_shapes=[
            pltpu.VMEM((ring, count, across * CHUNK), BF16),
            pltpu.VMEM((ring, across * CHUNK, count), BF16),
            pltpu.VMEM((rows, channels), BF16),
            pltpu.VMEM((rows, channels), BF16),
            pltpu.VMEM((rows, channels), BF16),
            pltpu.VMEM((rows, channels), BF16),
            pltpu.VMEM((height * width, 3 * channels), BF16),
            pltpu.VMEM(((height - 2) * width, 3 * channels), BF16),
            pltpu.VMEM(((height - 4) * width, 3 * channels), BF16),
            pltpu.VMEM(((height - 6) * width, 3 * channels), BF16),
            pltpu.VMEM((ring * 8, CHUNK), jnp.int32),
            pltpu.VMEM((ring * 8, CHUNK), jnp.int32),
            pltpu.VMEM((slots, channels), BF16),
            pltpu.VMEM((2, half_ring, count, channels), BF16),
            pltpu.VMEM((2, half_ring, count, channels), BF16),
            pltpu.VMEM((count, channels), BF16),
            pltpu.VMEM((2, half_ring, count, channels), BF16),
            pltpu.VMEM((ring, across * CHUNK, channels), BF16),
            pltpu.VMEM((slots, channels), BF16),
            pltpu.VMEM((levels, 2, share, channels), BF16),
            pltpu.VMEM((levels, share, channels), BF16),
            pltpu.VMEM((levels, share, channels), BF16),
            pltpu.VMEM((levels, share, channels), BF16),
            pltpu.VMEM((across, piece, channels), BF16),
            pltpu.VMEM((across, piece, channels), BF16),
            pltpu.VMEM((ring, piece, channels), BF16),
            pltpu.VMEM((across, piece, channels), BF16),
            pltpu.VMEM((across * piece, channels), F32),
            pltpu.VMEM((slots + slots // 2, channels), F32),
            pltpu.VMEM((slots + slots // 2, channels), F32),
            pltpu.VMEM((total, channels), F32),
            pltpu.VMEM((total, CHUNK), BF16),
            pltpu.VMEM((total, channels), BF16),
            pltpu.VMEM((few, channels), F32),
            pltpu.VMEM((ring, few, channels), F32),
            pltpu.VMEM((across, few, channels), F32),
            pltpu.VMEM((n_gy, few, channels), F32),
            pltpu.SemaphoreType.DMA((2, len(STEPS))),
            pltpu.SemaphoreType.DMA((2, len(STEPS))),
            pltpu.SemaphoreType.DMA((2, ring)),
            pltpu.SemaphoreType.DMA((2, ring, across)),
            pltpu.SemaphoreType.DMA((2, 2, half_ring, 2)),
            pltpu.SemaphoreType.DMA((2, 2, half_ring, 2)),
            pltpu.SemaphoreType.DMA((2, ring, across)),
            pltpu.SemaphoreType.DMA((2, 2)),
            pltpu.SemaphoreType.DMA((2, levels)),
            pltpu.SemaphoreType.DMA((2, across)),
            pltpu.SemaphoreType.DMA((2, ring)),
            pltpu.SemaphoreType.DMA((2, across)),
            pltpu.SemaphoreType.DMA((2, levels)),
            pltpu.SemaphoreType.DMA((2, levels)),
            pltpu.SemaphoreType.DMA((2, ring)),
            pltpu.SemaphoreType.DMA((2, across)),
            pltpu.SemaphoreType.DMA((2, n_gy)),
            pltpu.SemaphoreType.DMA,
        ],
        compiler_params=pltpu.CompilerParams(
            vmem_limit_bytes=VMEM_LIMIT, collective_id=1, has_side_effects=True
        ),
        name="map_step",
    )(
        pillars,
        recv_cell.reshape(blocks, CHUNK),
        cell_mask.T,
        occupancy.T,
        weights.reshape(2, taps * channels, channels),
        head_weight.reshape(1, channels),
        points,
        local,
        point_weight,
        table,
        counts,
        conv_second.reshape(n_gy * share, channels),
        point_second,
        head_second.reshape(1, channels),
    )


def on_device(
    points,
    point_pillar,
    point_weight,
    recv_cell,
    cell_mask,
    occupancy,
    conv_weight,
    head_weight,
    conv_second,
    point_second,
    head_second,
):
    rows, columns = lax.axis_size("gy"), lax.axis_size("gx")
    tile_rows, tile_cols = cell_mask.shape
    channels = point_weight.shape[1]
    slots = recv_cell.shape[0]
    grid = (rows, columns, tile_rows, tile_cols)

    pillars, table, local, counts = pool(points, point_pillar, point_weight, slots)
    conv_step, point_step, head_step = map_step(
        grid,
        pillars,
        recv_cell,
        cell_mask,
        occupancy,
        conv_weight,
        head_weight,
        points,
        local,
        point_weight,
        table,
        counts,
        conv_second,
        point_second,
        head_second,
    )
    return conv_step.astype(F32).reshape(conv_second.shape), point_step, head_step[0]


def solution(mesh):
    return jax.shard_map(
        on_device,
        mesh=mesh,
        in_specs=(
            P(None, ("gy", "gx")),
            P(("gy", "gx")),
            P(),
            P(("gy", "gx")),
            P("gy", "gx"),
            P("gy", "gx"),
            P(),
            P(),
            P(),
            P(),
            P(),
        ),
        out_specs=(P(), P(), P()),
        check_vma=False,
    )
```

```python
import functools

import jax
import jax.numpy as jnp
from jax import lax
from jax.experimental import pallas as pl
from jax.experimental.pallas import tpu as pltpu
from jax.sharding import PartitionSpec as P

MESH = pl.DeviceIdType.MESH
F32 = jnp.float32
BF16 = jnp.bfloat16
VMEM_LIMIT = 56 * 1024 * 1024
CHUNK = 128
SIDE = 8
HALO = 4
STEPS = ((0, -1), (0, 1), (-1, 0), (1, 0), (-1, -1), (1, 1), (-1, 1), (1, -1))


def iota(shape, dim):
    return lax.broadcasted_iota(jnp.int32, shape, dim)


def dot(a, b):
    return jnp.dot(a, b, preferred_element_type=F32)


def dot_nt(a, b):
    return lax.dot_general(a, b, (((1,), (1,)), ((), ())), preferred_element_type=F32)


def dot_tn(a, b):
    return lax.dot_general(a, b, (((0,), (0,)), ((), ())), preferred_element_type=F32)


def slope(value):
    sig = jax.nn.sigmoid(value)
    return sig * (1.0 + value * (1.0 - sig))


def rms_step(gradient, second):
    moment = 0.95 * second + 0.05 * gradient * gradient
    return gradient / (jnp.sqrt(moment) + 1e-08)


def pool_kernel(
    points, ids, ids_row, weight, pillars, table, local, counts, table_s, partial, sums, numbers, sem
):
    chunks = ids.shape[0]
    blocks = pillars.shape[0] // CHUNK
    total = chunks * CHUNK
    here = ids[...]
    back = pltpu.roll(here, 1, axis=1)
    lane = iota(here.shape, 1)
    before = jnp.where(lane == 0, pltpu.roll(back, 1, axis=0), back)
    first = (lane == 0) & (iota(here.shape, 0) == 0)
    flags = jnp.where((here != before) | first, 1.0, 0.0).astype(BF16)
    upto = jnp.where(iota((CHUNK, CHUNK), 0) <= iota((CHUNK, CHUNK), 1), 1.0, 0.0).astype(BF16)
    inside = dot(flags, upto)
    whole = dot(flags, jnp.ones((CHUNK, CHUNK), BF16))
    lower = jnp.where(iota((chunks, chunks), 0) > iota((chunks, chunks), 1), 1.0, 0.0)
    ahead = dot(lower.astype(BF16), whole.astype(BF16))
    head = jnp.broadcast_to(inside[:, 0:1], inside.shape)
    local[...] = (inside - head).astype(jnp.int32)
    row = ids_row[...]
    row_before = pltpu.roll(row, 1, axis=1)
    row_first = (row != row_before) | (iota(row.shape, 1) == 0)
    row_block = jnp.where(row_first, row // CHUNK, blocks + 8)
    below = jnp.where(row_block < iota((blocks + 8, total), 0), 1.0, 0.0).astype(BF16)
    table[0:chunks, :] = (ahead + head - 1.0).astype(jnp.int32)
    table[chunks : chunks + blocks + 8, :] = dot(below, jnp.ones((total, CHUNK), BF16)).astype(
        jnp.int32
    )
    copy = pltpu.make_async_copy(table, table_s, sem)
    copy.start()
    ranks = local[...]
    for k in range(chunks):
        part = pl.ds(k * CHUNK, CHUNK)
        pre = dot_tn(points[:, part], weight[...])
        act = (pre * jax.nn.sigmoid(pre)).astype(BF16)
        pick = jnp.where(iota((CHUNK, CHUNK), 0) == ranks[k : k + 1, :], 1.0, 0.0).astype(BF16)
        partial[part, :] = dot(pick, jnp.concatenate([act, jnp.ones_like(act)], axis=1))
    copy.wait()
    edge = jnp.zeros((8, CHUNK), F32)
    for k in range(chunks):
        at = table_s[k, 0]
        for side, compact in enumerate((sums, numbers)):
            got = partial[pl.ds(k * CHUNK, CHUNK), pl.ds(side * CHUNK, CHUNK)]
            first_rows = got[0:8] if k == 0 else compact[pl.ds(at, 8), :] + got[0:8]
            compact[pl.ds(at, CHUNK + 8), :] = jnp.concatenate([first_rows, got[8:], edge], axis=0)
    diagonal = iota((CHUNK, CHUNK), 0) == iota((CHUNK, CHUNK), 1)
    for d in range(blocks):
        at = table_s[chunks + d, 0]
        held = table_s[chunks + d + 1, 0] - at
        named = iota((CHUNK, CHUNK), 0) < held
        count = jnp.where(named, numbers[pl.ds(at, CHUNK), :], 1.0)
        mean = jnp.where(named, sums[pl.ds(at, CHUNK), :] / count, 0.0)
        pillars[pl.ds(d * CHUNK, CHUNK), :] = mean.astype(BF16)
        counts[d : d + 1, :] = jnp.sum(jnp.where(diagonal, count, 0.0), axis=0, keepdims=True)


def pool(points, point_pillar, weight, slots):
    total = point_pillar.shape[0]
    chunks, blocks = total // CHUNK, slots // CHUNK
    channels = weight.shape[1]
    rows = chunks + blocks + 8
    vmem = pl.BlockSpec(memory_space=pltpu.VMEM)
    return pl.pallas_call(
        pool_kernel,
        out_shape=(
            jax.ShapeDtypeStruct((slots, channels), BF16),
            jax.ShapeDtypeStruct((rows, CHUNK), jnp.int32),
            jax.ShapeDtypeStruct((chunks, CHUNK), jnp.int32),
            jax.ShapeDtypeStruct((blocks, CHUNK), F32),
        ),
        in_specs=[vmem] * 4,
        out_specs=(vmem,) * 4,
        scratch_shapes=[
            pltpu.SMEM((rows, CHUNK), jnp.int32),
            pltpu.VMEM((total, 2 * CHUNK), F32),
            pltpu.VMEM((total + 2 * CHUNK, CHUNK), F32),
            pltpu.VMEM((total + 2 * CHUNK, CHUNK), F32),
            pltpu.SemaphoreType.DMA,
        ],
        compiler_params=pltpu.CompilerParams(vmem_limit_bytes=VMEM_LIMIT),
        name="pool",
    )(points, point_pillar.reshape(chunks, CHUNK), point_pillar.reshape(1, total), weight)


def message_rows(tile_rows, tile_cols):
    spans, at = [], 0
    for down, right in STEPS:
        size = (HALO if down else tile_rows) * (SIDE if right else tile_cols)
        spans.append((at, size))
        at += size
    return spans, at


def ring_size(columns):
    return {32: 8, 8: 4, 4: 2}[columns]


def ring_order(ring):
    order = [ring // 2]
    for far in range(ring // 2 - 1, 0, -1):
        order += [far, -far]
    return order + [0]


def map_kernel(
    grid,
    pillars,
    cells,
    mask_t,
    occupied_t,
    weights,
    head_row,
    points,
    local,
    point_weight,
    table,
    counts,
    conv_second,
    point_second,
    head_second,
    conv_out,
    point_out,
    head_out,
    place,
    pick,
    send_f,
    got_f,
    send_m,
    got_m,
    v0,
    v1,
    v2,
    v3,
    send_i,
    got_i,
    got_x,
    send_y,
    got_y,
    own_g,
    got_g,
    send_r,
    returned,
    own_k,
    core_k,
    send_k,
    got_kz,
    send_kx,
    got_kx,
    got_ky,
    got_ax,
    second,
    merge_a,
    merge_b,
    slopes,
    picks,
    rows_b,
    own_s,
    got_sy,
    got_sx,
    got_sz,
    sem_f,
    sem_m,
    sem_i,
    sem_x,
    sem_y,
    sem_g,
    sem_r,
    sem_c,
    sem_kz,
    sem_kx,
    sem_ky,
    sem_ax,
    sem_az,
    sem_ac,
    sem_sy,
    sem_sx,
    sem_sz,
    sem_l,
    pass_x,
    pass_r,
    sem_px,
    sem_pr,
):
    n_gy, n_gx, tile_rows, tile_cols = grid
    gy, gx = lax.axis_index("gy"), lax.axis_index("gx")
    ring = ring_size(n_gx)
    across = n_gx // ring
    half_ring = ring // 2
    order = ring_order(ring)
    slot_of = {rel: r for r, rel in enumerate(order)}
    slot_of[-half_ring] = slot_of[half_ring]
    x, y = gx // ring, lax.rem(gx, ring)
    channels = pillars.shape[1]
    spans, _ = message_rows(tile_rows, tile_cols)
    width = tile_cols + 2 * SIDE
    height = tile_rows + 2 * HALO
    count = tile_rows * tile_cols
    part_rows = count // 2
    fan = across * CHUNK

    def neighbour(k):
        down, right = STEPS[k]
        return lax.rem(gy + down + n_gy, n_gy), lax.rem(gx + right + n_gx, n_gx)

    def along(step):
        return lax.rem(y + step + ring, ring)

    def over(step):
        return lax.rem(x + step + across, across)

    def ring_device(step):
        return gy, x * ring + along(step)

    def across_device(step):
        return gy, over(step) * ring + y

    levels = n_gy // 2
    z, core = gy // 2, lax.rem(gy, 2)

    def level_device(step):
        return lax.rem(z + step, levels) * 2 + core, gx

    other_core = (z * 2 + 1 - core, gx)

    def stack_device(step):
        return lax.rem(gy + step, n_gy), gx

    def slot_block(column, place_on_ring):
        return pl.ds(pl.multiple_of((column * ring + place_on_ring) * CHUNK, CHUNK), CHUNK)

    def remote(src, dst, send, recv, device):
        return pltpu.make_async_remote_copy(
            src_ref=src,
            dst_ref=dst,
            send_sem=send,
            recv_sem=recv,
            device_id=device,
            device_id_type=MESH,
        )

    def arrival(ref, sem):
        remote(ref, ref, sem, sem, ring_device(1)).wait_recv()

    share = own_k.shape[2]
    piece = got_ky.shape[1]
    load = pltpu.make_async_copy(
        conv_second.at[pl.ds(pl.multiple_of(gy * share, 8), share)],
        second.at[pl.ds(0, share)],
        sem_l,
    )
    load.start()
    barrier = pltpu.get_barrier_semaphore()
    partners = [neighbour(k) for k in range(len(STEPS))]
    partners += [ring_device(step) for step in range(1, ring)]
    partners += [across_device(step) for step in range(1, across)]
    partners += [stack_device(step) for step in range(1, n_gy)]
    for device in partners:
        pl.semaphore_signal(barrier, inc=1, device_id=device, device_id_type=MESH)
    pl.semaphore_wait(barrier, len(partners))

    started = []

    def go(copy):
        copy.start()
        started.append(copy)

    def between(r):
        if across != 4:
            return 0
        return 1 if r % 2 == 0 else -1

    def send_pillars(r):
        for o in (2, 1, 3) if between(r) else range(1, across):
            src = pillars.at[slot_block(over(o), along(order[r]))]
            dst = got_x.at[pl.ds((r * across + o) * CHUNK, CHUNK)]
            if o == 2 and between(r):
                device = across_device(between(r))
                go(remote(src, pass_x.at[r], sem_x.at[0, r, o], sem_px.at[1, r], device))
            else:
                device = across_device(o)
                go(remote(src, dst, sem_x.at[0, r, o], sem_x.at[1, r, o], device))

    def pass_pillars(r):
        if between(r):
            arrival(pass_x.at[r], sem_px.at[1, r])
            dst = got_x.at[pl.ds((r * across + 2) * CHUNK, CHUNK)]
            device = across_device(between(r))
            go(remote(pass_x.at[r], dst, sem_px.at[0, r], sem_x.at[1, r, 2], device))

    for r in range(min(3, ring)):
        send_pillars(r)

    send_i[...] = jnp.zeros_like(send_i)
    for step in range(ring):
        lead = step * 8
        for o in range(across):
            row = over(-o) * ring + along(step)
            send_i[lead + o : lead + o + 1, :] = cells[pl.ds(row, 1), :]
        if step == 0:
            got_i[pl.ds(slot_of[0] * 8, 8), :] = send_i[pl.ds(0, 8), :]
        else:
            rel = -step if step <= half_ring else ring - step
            slot = slot_of[rel]
            go(
                remote(
                    send_i.at[pl.ds(lead, 8)],
                    got_i.at[pl.ds(slot * 8, 8)],
                    sem_i.at[0, step],
                    sem_i.at[1, slot],
                    ring_device(step),
                )
            )

    def post(own, send, got, sem):
        grid3 = own.reshape(tile_rows, tile_cols, channels)
        for k, (down, right) in enumerate(STEPS):
            part = grid3
            if down:
                part = part[:HALO] if down < 0 else part[tile_rows - HALO :]
            if right:
                part = part[:, :SIDE] if right < 0 else part[:, tile_cols - SIDE :]
            at, size = spans[k]
            send[pl.ds(at, size), :] = part.reshape(size, channels).astype(BF16)
            there, _ = spans[k ^ 1]
            go(
                remote(
                    send.at[pl.ds(at, size)],
                    got.at[pl.ds(there, size)],
                    sem.at[0, k],
                    sem.at[1, k ^ 1],
                    neighbour(k),
                )
            )

    def collect(own, got, sem):
        parts = {}
        for k, (down, right) in enumerate(STEPS):
            at, size = spans[k]
            arrival(got.at[pl.ds(at, size)], sem.at[1, k])
            rows = HALO if down else tile_rows
            parts[down, right] = (
                got[pl.ds(at, size), :].astype(F32).reshape(rows, size // rows, channels)
            )
        parts[0, 0] = own.reshape(tile_rows, tile_cols, channels)
        return jnp.concatenate(
            [
                jnp.concatenate([parts[down, right] for right in (-1, 0, 1)], axis=1).reshape(
                    -1, channels
                )
                for down in (-1, 0, 1)
            ],
            axis=0,
        )

    masks = jnp.concatenate([mask_t[...], mask_t[...] * occupied_t[...]], axis=0)
    masks = masks.astype(F32).astype(BF16)
    of_row = iota((count, tile_rows), 0) // tile_cols == iota((count, tile_rows), 1)
    by_column = dot_nt(jnp.where(of_row, 1.0, 0.0).astype(BF16), masks)
    pairs = (count, 2 * tile_cols)
    of_column = iota(pairs, 0) % tile_cols == iota(pairs, 1) % tile_cols
    halves = (2 * tile_cols, channels)
    same_half = (iota(halves, 0) < tile_cols) == (iota(halves, 1) < channels // 2)
    mask_own = dot(
        jnp.where(of_column, by_column, 0.0).astype(BF16),
        jnp.where(same_half, 1.0, 0.0).astype(BF16),
    )
    post(mask_own, send_m, got_m, sem_m)

    flat = iota((height * width, channels), 0)
    row = flat // width + gy * tile_rows - HALO
    col = flat % width + gx * tile_cols - SIDE
    in_slab = jnp.where(
        (row >= 0) & (row < n_gy * tile_rows) & (col >= 0) & (col < n_gx * tile_cols), 1.0, 0.0
    )
    column = iota((tile_rows * width, channels), 0) % width
    own_column = jnp.where((column >= SIDE) & (column < SIDE + tile_cols), 1.0, 0.0)

    for r in range(ring - 1):
        arrival(got_i.at[pl.ds(r * 8, 8)], sem_i.at[1, r])
    rows_i = ring * 8
    cells_i = got_i[...]
    cells_t = jnp.concatenate(
        [cells_i.astype(F32), jnp.zeros(((-rows_i) % CHUNK, CHUNK), F32)], axis=0
    ).T.astype(jnp.int32)
    def build_place(r):
        for o in range(across):
            at = r * 8 + o
            place[r, :, pl.ds(o * CHUNK, CHUNK)] = jnp.where(
                iota((count, CHUNK), 0) == cells_i[at : at + 1, :], 1.0, 0.0
            ).astype(BF16)

    def build_pick(r):
        for o in range(across):
            at = r * 8 + o
            pick[r, pl.ds(o * CHUNK, CHUNK), :] = jnp.where(
                cells_t[:, at : at + 1] == iota((CHUNK, count), 1), 1.0, 0.0
            ).astype(BF16)

    def cut(value, lead, rows):
        return value[lead * width : (lead + rows) * width]

    def side_by_side(value, ref):
        size = value.shape[0]
        left = pltpu.roll(value, 1, axis=0)
        right = pltpu.roll(value, size - 1, axis=0)
        ref[...] = jnp.concatenate([left.astype(BF16), value.astype(BF16), right.astype(BF16)], 1)

    def windows(ref, lead, rows):
        return jnp.concatenate(
            [ref[pl.ds((lead + a) * width, rows * width), :] for a in (0, 1, 2)], axis=1
        )

    def flipped(layer):
        return jnp.concatenate(
            [weights[layer, pl.ds((8 - k) * channels, channels), :] for k in range(9)], axis=1
        )

    def placed_for(r):
        for o in range(1, across):
            arrival(got_x.at[pl.ds((r * across + o) * CHUNK, CHUNK)], sem_x.at[1, r, o])
        own = pillars[slot_block(x, along(order[r])), :]
        rest = got_x[pl.ds((r * across + 1) * CHUNK, fan - CHUNK), :]
        return dot(place[r], jnp.concatenate([own, rest], axis=0))

    halves = (pl.ds(0, part_rows), pl.ds(part_rows, part_rows))

    def half_of(value, half):
        return value[half * part_rows : (half + 1) * part_rows]

    def grow(t, side, half, value):
        if t > 1 or (t == 1 and half == side):
            arrival(got_y.at[side, t - 1, halves[half]], sem_y.at[1, side, t - 1, half])
            value = value + got_y[side, t - 1, halves[half], :].astype(F32)
        send_y[side, t, halves[half], :] = value.astype(BF16)
        go(
            remote(
                send_y.at[side, t, halves[half]],
                got_y.at[side, t, halves[half]],
                sem_y.at[0, side, t, half],
                sem_y.at[1, side, t, half],
                ring_device(1 - 2 * side),
            )
        )

    left = list(range(ring))
    for t in range(half_ring):
        for r in range(2 * t + 1, min(2 * t + 3, ring)) if t else ():
            send_pillars(r)
        if t == 0:
            pass_pillars(0)
            build_place(0)
            summed = placed_for(0)
            for side in (0, 1):
                grow(0, side, side, half_of(summed, side))
        else:
            summed = {}
            for side in (0, 1):
                r = slot_of[(1 - 2 * side) * (half_ring - t)]
                build_place(r)
                summed[side] = placed_for(r)
                if t == 1:
                    grow(t, side, 1 - side, half_of(summed[side], 1 - side))
            for order_half in (0, 1):
                for side in (0, 1):
                    half = 1 - side if order_half == 0 else side
                    if t > 1 or half == side:
                        grow(t, side, half, half_of(summed[side], half))
        for r in range(2 * t + 1, min(2 * t + 3, ring)):
            pass_pillars(r)
        for r in left[:2]:
            build_pick(r)
        left = left[2:]
    build_place(slot_of[0])
    placed = placed_for(slot_of[0])
    for r in left:
        build_pick(r)
    mask_all = (collect(mask_own, got_m, sem_m) * in_slab).astype(BF16)
    half = channels // 2
    spread = jnp.where(
        iota((channels, 2 * channels), 0)
        == jnp.where(iota((channels, 2 * channels), 1) < channels, 0, half),
        1.0,
        0.0,
    ).astype(BF16)
    mask_all = dot(mask_all, spread)
    hidden_cell = mask_all[:, :channels]
    target = mask_all[:, channels:]

    visible = 1.0 - cut(hidden_cell, HALO, tile_rows).reshape(tile_rows, width, channels)[
        :, SIDE : SIDE + tile_cols
    ].reshape(count, channels)

    last = half_ring - 1
    ends = []
    for half in (0, 1):
        value = half_of(placed, half)
        for side in (0, 1):
            if last or half == side:
                arrival(got_y.at[side, last, halves[half]], sem_y.at[1, side, last, half])
                value = value + got_y[side, last, halves[half], :].astype(F32)
        ends.append(value)
    placed = jnp.concatenate(ends, axis=0)
    features = (placed * visible).astype(BF16).astype(F32)
    post(features, send_f, got_f, sem_f)
    side_by_side(collect(features, got_f, sem_f) * in_slab, v0)

    pre1 = dot(windows(v0, 0, height - 2), weights[0])
    side_by_side(pre1 * jax.nn.sigmoid(pre1) * cut(in_slab, 1, height - 2), v1)
    pre2 = dot(windows(v1, 0, height - 4), weights[1])
    sig2 = jax.nn.sigmoid(pre2)
    hidden2 = (pre2 * sig2).astype(BF16)
    head = jnp.broadcast_to(head_row[...], (channels, channels))
    logits = dot_nt(hidden2, head)
    cells_all = n_gy * tile_rows * n_gx * tile_cols
    logit_grad = (
        cut(hidden_cell, 2, height - 4) * jax.nn.sigmoid(logits) - cut(target, 2, height - 4)
    ) / cells_all
    grad2 = logit_grad * head_row[...].astype(F32) * (sig2 * (1.0 + pre2 * (1.0 - sig2)))
    side_by_side(grad2, v2)
    back2 = dot_nt(windows(v2, 0, height - 6), flipped(1))
    grad1 = back2 * slope(cut(pre1, 2, height - 6)) * cut(in_slab, 3, height - 6)
    side_by_side(grad1, v3)
    back1 = dot_nt(windows(v3, 0, tile_rows), flipped(0))
    back1 = back1.reshape(tile_rows, width, channels)[:, SIDE : SIDE + tile_cols].reshape(
        count, channels
    )
    own_g[...] = (back1 * visible).astype(BF16)

    def pass_on(t, side, half):
        src = own_g if t == 1 else got_g.at[side, t - 2]
        go(
            remote(
                src.at[halves[half]],
                got_g.at[side, t - 1, halves[half]],
                sem_g.at[0, side, t - 1, half],
                sem_g.at[1, side, t - 1, half],
                ring_device(1 - 2 * side),
            )
        )

    def passes(r):
        return between(r) and r != slot_of[half_ring]

    def hand_out(rel, gradient):
        r = slot_of[rel]
        rows = dot(pick[r], gradient).astype(BF16)
        returned[slot_block(x, along(rel)), :] = rows[:CHUNK]
        send_r[r] = rows
        for o in (2, 1, 3) if passes(r) else range(1, across):
            src = send_r.at[r, pl.ds(o * CHUNK, CHUNK)]
            if o == 2 and passes(r):
                device = across_device(between(r))
                go(remote(src, pass_r.at[r], sem_r.at[0, r, o], sem_pr.at[1, r], device))
            else:
                dst = returned.at[slot_block(x, along(rel))]
                device = across_device(-o)
                go(remote(src, dst, sem_r.at[0, r, o], sem_r.at[1, r, o], device))

    def pass_back(rel):
        r = slot_of[rel]
        if passes(r):
            arrival(pass_r.at[r], sem_pr.at[1, r])
            device = across_device(between(r))
            dst = returned.at[slot_block(over(-between(r)), along(rel))]
            go(remote(pass_r.at[r], dst, sem_pr.at[0, r], sem_r.at[1, r, 2], device))

    parts = levels // 2

    def halve(layer, gradient):
        own_k[pl.ds(layer * parts, parts)] = gradient.reshape(
            parts, 2, share, channels
        ).astype(BF16)
        go(
            remote(
                own_k.at[pl.ds(layer * parts, parts), 1 - core],
                core_k.at[pl.ds(layer * parts, parts)],
                sem_c.at[0, layer],
                sem_c.at[1, layer],
                other_core,
            )
        )

    def to_levels():
        for layer in (0, 1):
            arrival(core_k.at[pl.ds(layer * parts, parts)], sem_c.at[1, layer])
        for k in range(levels):
            send_k[k] = (own_k[k, core].astype(F32) + core_k[k].astype(F32)).astype(BF16)
        got_kz[z] = send_k[z]
        for step in range(1, levels):
            go(
                remote(
                    send_k.at[lax.rem(z + step, levels)],
                    got_kz.at[z],
                    sem_kz.at[0, step],
                    sem_kz.at[1, step],
                    level_device(step),
                )
            )

    def gathered(got, sem):
        summed = None
        for step in range(1, got.shape[0]):
            arrival(got.at[0], sem.at[1, step])
        for k in range(got.shape[0]):
            term = got[k].astype(F32)
            summed = term if summed is None else summed + term
        return summed

    def to_all(value, got, sem, me, device):
        got[me] = value.astype(got.dtype)
        for step in range(1, got.shape[0]):
            go(remote(got.at[me], got.at[me], sem.at[0, step], sem.at[1, step], device(step)))

    def to_pieces(summed):
        spare = across * piece - share
        if spare:
            summed = jnp.concatenate([summed, jnp.zeros((spare, channels), F32)], axis=0)
        send_kx[...] = summed.reshape(across, piece, channels).astype(BF16)
        got_kx[x] = send_kx[x]
        for step in range(1, across):
            go(
                remote(
                    send_kx.at[over(step)],
                    got_kx.at[x],
                    sem_kx.at[0, step],
                    sem_kx.at[1, step],
                    across_device(step),
                )
            )

    def take_step(summed):
        load.wait()
        if across * piece > share:
            second[pl.ds(share, across * piece - share), :] = jnp.ones(
                (across * piece - share, channels), F32
            )
        rows = pl.ds(pl.multiple_of(x * piece, 8), piece)
        return rms_step(summed, second[rows, :])

    chunks = local.shape[0]
    blocks = counts.shape[0]

    def turned(value):
        spare = (-value.shape[0]) % CHUNK
        return jnp.concatenate([value, jnp.zeros((spare, CHUNK), F32)], axis=0).T

    ranks_t = turned(local[...].astype(F32)).astype(jnp.int32)

    def prepare(begin, end):
        for k in range(begin, end):
            part = pl.ds(k * CHUNK, CHUNK)
            slopes[part, :] = slope(dot_tn(points[:, part], point_weight[...]))
            picks[part, :] = jnp.where(
                ranks_t[:, k : k + 1] == iota((CHUNK, CHUNK), 1), 1.0, 0.0
            ).astype(BF16)

    scale = turned(1.0 / counts[...])

    def start_merge():
        for d in range(blocks):
            part = pl.ds(d * CHUNK, CHUNK)
            merge_a[part, :] = returned[part, :].astype(F32) * scale[:, d : d + 1]
        spare = merge_a.shape[0] - blocks * CHUNK
        for ref in (merge_a, merge_b):
            ref[pl.ds(blocks * CHUNK, spare), :] = jnp.zeros((spare, CHUNK), F32)

    def merge_level(level, src, dst):
        size = CHUNK << level
        for pair in range(blocks >> (level + 1)):
            lead = pair * 2 * size
            first = chunks + pair * (2 << level)
            held = table[first + (1 << level), 0] - table[first, 0]
            for at in range(0, 2 * size, 2 * CHUNK):
                rows = iota((2 * CHUNK, CHUNK), 0) + at
                dst[pl.ds(lead + at, 2 * CHUNK), :] = jnp.where(
                    rows < held,
                    src[pl.ds(lead + at, 2 * CHUNK), :],
                    src[pl.ds(lead + at + size - held, 2 * CHUNK), :],
                )

    levels_m = blocks.bit_length() - 1
    refs = (merge_a, merge_b)

    def merge(begin, end):
        for level in range(begin, end):
            merge_level(level, refs[level % 2], refs[1 - level % 2])

    def point_terms():
        joined = refs[levels_m % 2]
        for k in range(chunks):
            part = pl.ds(k * CHUNK, CHUNK)
            window = joined[pl.ds(table[k, 0], CHUNK), :].astype(BF16)
            rows_b[part, :] = (dot(picks[part, :], window) * slopes[part, :]).astype(BF16)
        return dot(points[...], rows_b[...])

    for order_half in (0, 1):
        for side in (0, 1):
            pass_on(1, side, side if order_half == 0 else 1 - side)
    hand_out(0, own_g[...])
    own1 = (cut(grad1, 1, tile_rows) * own_column).astype(BF16)
    halve(0, dot_tn(windows(v0, 3, tile_rows), own1))

    def second_kernel():
        own2 = (cut(grad2, 2, tile_rows) * own_column).astype(BF16)
        halve(1, dot_tn(windows(v1, 2, tile_rows), own2))

    if half_ring == 1:
        second_kernel()
    head_terms = cut(logit_grad * hidden2.astype(F32), 2, tile_rows) * own_column
    head_local = jnp.sum(head_terms, axis=0, keepdims=True)
    prepared = 0
    for t in range(1, half_ring + 1):
        if t < half_ring:
            for order_half in (0, 1):
                for side in (0, 1):
                    half = side if order_half == 0 else 1 - side
                    arrival(got_g.at[side, t - 1, halves[half]], sem_g.at[1, side, t - 1, half])
                    if t + 1 < half_ring or order_half == 0:
                        pass_on(t + 1, side, half)
        else:
            for side in (0, 1):
                arrival(got_g.at[side, t - 1, halves[side]], sem_g.at[1, side, t - 1, side])
        if t == min(2, half_ring):
            to_levels()
        if t == half_ring:
            hand_out(
                t,
                jnp.concatenate(
                    [got_g[side, t - 1, halves[side], :] for side in (0, 1)], axis=0
                ),
            )
        else:
            hand_out(-t, got_g[0, t - 1])
            hand_out(t, got_g[1, t - 1])
            if t == 1:
                second_kernel()
        for rel in (0,) if t == 1 else (1 - t, t - 1):
            pass_back(rel)
        if t == half_ring:
            to_pieces(gathered(got_kz, sem_kz))
        share_to = chunks * t // half_ring
        prepare(prepared, share_to)
        prepared = share_to
    to_all(gathered(got_kx, sem_kx), got_ky, sem_ky, y, ring_device)
    for r, rel in enumerate(order):
        for o in range(1, across):
            arrival(returned.at[slot_block(over(o), along(rel))], sem_r.at[1, r, o])
    start_merge()
    merge(0, min(2, levels_m))
    to_all(take_step(gathered(got_ky, sem_ky)), got_ax, sem_ax, x, across_device)
    merge(min(2, levels_m), levels_m)
    for step in range(1, across):
        arrival(got_ax.at[0], sem_ax.at[1, step])
    conv_out[gy] = got_ax[...].reshape(across * piece, channels)[:share]
    mine = conv_out.at[gy]
    for step in range(1, levels):
        go(remote(mine, mine, sem_az.at[0, step], sem_az.at[1, step], level_device(step)))
    go(remote(mine, mine, sem_ac.at[0, 0], sem_ac.at[1, 0], other_core))
    features_in = points.shape[0]
    own_s[...] = jnp.zeros_like(own_s)
    own_s[0:features_in, :] = point_terms()
    own_s[features_in : features_in + 1, :] = head_local
    to_all(own_s[...], got_sy, sem_sy, y, ring_device)

    def relay(begin, end):
        for step in range(begin, end):
            held = conv_out.at[lax.rem(z - step + levels, levels) * 2 + core]
            arrival(held, sem_az.at[1, step])
            go(remote(held, held, sem_ac.at[0, step], sem_ac.at[1, step], other_core))

    relay(1, min(3, levels))
    to_all(gathered(got_sy, sem_sy), got_sx, sem_sx, x, across_device)
    relay(min(3, levels), min(6, levels))
    to_all(gathered(got_sx, sem_sx), got_sz, sem_sz, gy, stack_device)
    relay(min(6, levels), levels)
    small = gathered(got_sz, sem_sz)
    point_out[...] = rms_step(small[:features_in], point_second[...])
    head_out[...] = rms_step(small[features_in : features_in + 1], head_second[...])
    for step in range(levels):
        level = lax.rem(z - step + levels, levels)
        arrival(conv_out.at[level * 2 + 1 - core], sem_ac.at[1, step])
    for copy in started:
        copy.wait_send()


def map_step(grid, pillars, recv_cell, cell_mask, occupancy, weights, head_weight, points, local,
             point_weight, table, counts, conv_second, point_second, head_second):
    n_gy, n_gx, tile_rows, tile_cols = grid
    slots, channels = pillars.shape
    total = points.shape[1]
    blocks = slots // CHUNK
    count = tile_rows * tile_cols
    width = tile_cols + 2 * SIDE
    height = tile_rows + 2 * HALO
    ring = ring_size(n_gx)
    across, half_ring = n_gx // ring, ring // 2
    _, rows = message_rows(tile_rows, tile_cols)
    vmem = pl.BlockSpec(memory_space=pltpu.VMEM)
    smem = pl.BlockSpec(memory_space=pltpu.SMEM)
    taps = weights.shape[1]
    levels = n_gy // 2
    share = 2 * taps * channels // n_gy
    piece = -(-share // (across * 16)) * 16
    few = -(-(points.shape[0] + 1) // 8) * 8
    return pl.pallas_call(
        functools.partial(map_kernel, grid),
        out_shape=(
            jax.ShapeDtypeStruct((n_gy, share, channels), BF16),
            jax.ShapeDtypeStruct(point_weight.shape, F32),
            jax.ShapeDtypeStruct((1, channels), F32),
        ),
        in_specs=[vmem] * 9 + [smem, vmem, pl.BlockSpec(memory_space=pl.ANY), vmem, vmem],
        out_specs=(vmem,) * 3,
        scratch_shapes=[
            pltpu.VMEM((ring, count, across * CHUNK), BF16),
            pltpu.VMEM((ring, across * CHUNK, count), BF16),
            pltpu.VMEM((rows, channels), BF16),
            pltpu.VMEM((rows, channels), BF16),
            pltpu.VMEM((rows, channels), BF16),
            pltpu.VMEM((rows, channels), BF16),
            pltpu.VMEM((height * width, 3 * channels), BF16),
            pltpu.VMEM(((height - 2) * width, 3 * channels), BF16),
            pltpu.VMEM(((height - 4) * width, 3 * channels), BF16),
            pltpu.VMEM(((height - 6) * width, 3 * channels), BF16),
            pltpu.VMEM((ring * 8, CHUNK), jnp.int32),
            pltpu.VMEM((ring * 8, CHUNK), jnp.int32),
            pltpu.VMEM((slots, channels), BF16),
            pltpu.VMEM((2, half_ring, count, channels), BF16),
            pltpu.VMEM((2, half_ring, count, channels), BF16),
            pltpu.VMEM((count, channels), BF16),
            pltpu.VMEM((2, half_ring, count, channels), BF16),
            pltpu.VMEM((ring, across * CHUNK, channels), BF16),
            pltpu.VMEM((slots, channels), BF16),
            pltpu.VMEM((levels, 2, share, channels), BF16),
            pltpu.VMEM((levels, share, channels), BF16),
            pltpu.VMEM((levels, share, channels), BF16),
            pltpu.VMEM((levels, share, channels), BF16),
            pltpu.VMEM((across, piece, channels), BF16),
            pltpu.VMEM((across, piece, channels), BF16),
            pltpu.VMEM((ring, piece, channels), BF16),
            pltpu.VMEM((across, piece, channels), BF16),
            pltpu.VMEM((across * piece, channels), F32),
            pltpu.VMEM((slots + slots // 2, channels), F32),
            pltpu.VMEM((slots + slots // 2, channels), F32),
            pltpu.VMEM((total, channels), F32),
            pltpu.VMEM((total, CHUNK), BF16),
            pltpu.VMEM((total, channels), BF16),
            pltpu.VMEM((few, channels), F32),
            pltpu.VMEM((ring, few, channels), F32),
            pltpu.VMEM((across, few, channels), F32),
            pltpu.VMEM((n_gy, few, channels), F32),
            pltpu.SemaphoreType.DMA((2, len(STEPS))),
            pltpu.SemaphoreType.DMA((2, len(STEPS))),
            pltpu.SemaphoreType.DMA((2, ring)),
            pltpu.SemaphoreType.DMA((2, ring, across)),
            pltpu.SemaphoreType.DMA((2, 2, half_ring, 2)),
            pltpu.SemaphoreType.DMA((2, 2, half_ring, 2)),
            pltpu.SemaphoreType.DMA((2, ring, across)),
            pltpu.SemaphoreType.DMA((2, 2)),
            pltpu.SemaphoreType.DMA((2, levels)),
            pltpu.SemaphoreType.DMA((2, across)),
            pltpu.SemaphoreType.DMA((2, ring)),
            pltpu.SemaphoreType.DMA((2, across)),
            pltpu.SemaphoreType.DMA((2, levels)),
            pltpu.SemaphoreType.DMA((2, levels)),
            pltpu.SemaphoreType.DMA((2, ring)),
            pltpu.SemaphoreType.DMA((2, across)),
            pltpu.SemaphoreType.DMA((2, n_gy)),
            pltpu.SemaphoreType.DMA,
            pltpu.VMEM((ring, CHUNK, channels), BF16),
            pltpu.VMEM((ring, CHUNK, channels), BF16),
            pltpu.SemaphoreType.DMA((2, ring)),
            pltpu.SemaphoreType.DMA((2, ring)),
        ],
        compiler_params=pltpu.CompilerParams(
            vmem_limit_bytes=VMEM_LIMIT, collective_id=1, has_side_effects=True
        ),
        name="map_step",
    )(
        pillars,
        recv_cell.reshape(blocks, CHUNK),
        cell_mask.T,
        occupancy.T,
        weights.reshape(2, taps * channels, channels),
        head_weight.reshape(1, channels),
        points,
        local,
        point_weight,
        table,
        counts,
        conv_second.reshape(n_gy * share, channels),
        point_second,
        head_second.reshape(1, channels),
    )


def on_device(
    points,
    point_pillar,
    point_weight,
    recv_cell,
    cell_mask,
    occupancy,
    conv_weight,
    head_weight,
    conv_second,
    point_second,
    head_second,
):
    rows, columns = lax.axis_size("gy"), lax.axis_size("gx")
    tile_rows, tile_cols = cell_mask.shape
    channels = point_weight.shape[1]
    slots = recv_cell.shape[0]
    grid = (rows, columns, tile_rows, tile_cols)

    pillars, table, local, counts = pool(points, point_pillar, point_weight, slots)
    conv_step, point_step, head_step = map_step(
        grid,
        pillars,
        recv_cell,
        cell_mask,
        occupancy,
        conv_weight,
        head_weight,
        points,
        local,
        point_weight,
        table,
        counts,
        conv_second,
        point_second,
        head_second,
    )
    return conv_step.astype(F32).reshape(conv_second.shape), point_step, head_step[0]


def solution(mesh):
    return jax.shard_map(
        on_device,
        mesh=mesh,
        in_specs=(
            P(None, ("gy", "gx")),
            P(("gy", "gx")),
            P(),
            P(("gy", "gx")),
            P("gy", "gx"),
            P("gy", "gx"),
            P(),
            P(),
            P(),
            P(),
            P(),
        ),
        out_specs=(P(), P(), P()),
        check_vma=False,
    )
```

```python
import functools

import jax
import jax.numpy as jnp
from jax import lax
from jax.experimental import pallas as pl
from jax.experimental.pallas import tpu as pltpu
from jax.sharding import PartitionSpec as P

MESH = pl.DeviceIdType.MESH
F32 = jnp.float32
BF16 = jnp.bfloat16
VMEM_LIMIT = 56 * 1024 * 1024
CHUNK = 128
SIDE = 8
HALO = 4
PARTS = 4
STEPS = ((0, -1), (0, 1), (-1, 0), (1, 0), (-1, -1), (1, 1), (-1, 1), (1, -1))


def iota(shape, dim):
    return lax.broadcasted_iota(jnp.int32, shape, dim)


def dot(a, b):
    return jnp.dot(a, b, preferred_element_type=F32)


def dot_nt(a, b):
    return lax.dot_general(a, b, (((1,), (1,)), ((), ())), preferred_element_type=F32)


def dot_tn(a, b):
    return lax.dot_general(a, b, (((0,), (0,)), ((), ())), preferred_element_type=F32)


def slope(value):
    sig = jax.nn.sigmoid(value)
    return sig * (1.0 + value * (1.0 - sig))


def rms_step(gradient, second):
    moment = 0.95 * second + 0.05 * gradient * gradient
    return gradient / (jnp.sqrt(moment) + 1e-08)


def pool_kernel(
    points, ids, ids_row, weight, pillars, table, local, counts, table_s, partial, sums, numbers, sem
):
    chunks = ids.shape[0]
    blocks = pillars.shape[0] // CHUNK
    total = chunks * CHUNK
    here = ids[...]
    back = pltpu.roll(here, 1, axis=1)
    lane = iota(here.shape, 1)
    before = jnp.where(lane == 0, pltpu.roll(back, 1, axis=0), back)
    first = (lane == 0) & (iota(here.shape, 0) == 0)
    flags = jnp.where((here != before) | first, 1.0, 0.0).astype(BF16)
    upto = jnp.where(iota((CHUNK, CHUNK), 0) <= iota((CHUNK, CHUNK), 1), 1.0, 0.0).astype(BF16)
    inside = dot(flags, upto)
    whole = dot(flags, jnp.ones((CHUNK, CHUNK), BF16))
    lower = jnp.where(iota((chunks, chunks), 0) > iota((chunks, chunks), 1), 1.0, 0.0)
    ahead = dot(lower.astype(BF16), whole.astype(BF16))
    head = jnp.broadcast_to(inside[:, 0:1], inside.shape)
    local[...] = (inside - head).astype(jnp.int32)
    row = ids_row[...]
    row_before = pltpu.roll(row, 1, axis=1)
    row_first = (row != row_before) | (iota(row.shape, 1) == 0)
    row_block = jnp.where(row_first, row // CHUNK, blocks + 8)
    below = jnp.where(row_block < iota((blocks + 8, total), 0), 1.0, 0.0).astype(BF16)
    table[0:chunks, :] = (ahead + head - 1.0).astype(jnp.int32)
    table[chunks : chunks + blocks + 8, :] = dot(below, jnp.ones((total, CHUNK), BF16)).astype(
        jnp.int32
    )
    copy = pltpu.make_async_copy(table, table_s, sem)
    copy.start()
    ranks = local[...]
    for k in range(chunks):
        part = pl.ds(k * CHUNK, CHUNK)
        pre = dot_tn(points[:, part], weight[...])
        act = (pre * jax.nn.sigmoid(pre)).astype(BF16)
        pick = jnp.where(iota((CHUNK, CHUNK), 0) == ranks[k : k + 1, :], 1.0, 0.0).astype(BF16)
        partial[part, :] = dot(pick, jnp.concatenate([act, jnp.ones_like(act)], axis=1))
    copy.wait()
    edge = jnp.zeros((8, CHUNK), F32)
    for k in range(chunks):
        at = table_s[k, 0]
        for side, compact in enumerate((sums, numbers)):
            got = partial[pl.ds(k * CHUNK, CHUNK), pl.ds(side * CHUNK, CHUNK)]
            first_rows = got[0:8] if k == 0 else compact[pl.ds(at, 8), :] + got[0:8]
            compact[pl.ds(at, CHUNK + 8), :] = jnp.concatenate([first_rows, got[8:], edge], axis=0)
    diagonal = iota((CHUNK, CHUNK), 0) == iota((CHUNK, CHUNK), 1)
    for d in range(blocks):
        at = table_s[chunks + d, 0]
        held = table_s[chunks + d + 1, 0] - at
        named = iota((CHUNK, CHUNK), 0) < held
        count = jnp.where(named, numbers[pl.ds(at, CHUNK), :], 1.0)
        mean = jnp.where(named, sums[pl.ds(at, CHUNK), :] / count, 0.0)
        pillars[pl.ds(d * CHUNK, CHUNK), :] = mean.astype(BF16)
        counts[d : d + 1, :] = jnp.sum(jnp.where(diagonal, count, 0.0), axis=0, keepdims=True)


def pool(points, point_pillar, weight, slots):
    total = point_pillar.shape[0]
    chunks, blocks = total // CHUNK, slots // CHUNK
    channels = weight.shape[1]
    rows = chunks + blocks + 8
    vmem = pl.BlockSpec(memory_space=pltpu.VMEM)
    return pl.pallas_call(
        pool_kernel,
        out_shape=(
            jax.ShapeDtypeStruct((slots, channels), BF16),
            jax.ShapeDtypeStruct((rows, CHUNK), jnp.int32),
            jax.ShapeDtypeStruct((chunks, CHUNK), jnp.int32),
            jax.ShapeDtypeStruct((blocks, CHUNK), F32),
        ),
        in_specs=[vmem] * 4,
        out_specs=(vmem,) * 4,
        scratch_shapes=[
            pltpu.SMEM((rows, CHUNK), jnp.int32),
            pltpu.VMEM((total, 2 * CHUNK), F32),
            pltpu.VMEM((total + 2 * CHUNK, CHUNK), F32),
            pltpu.VMEM((total + 2 * CHUNK, CHUNK), F32),
            pltpu.SemaphoreType.DMA,
        ],
        compiler_params=pltpu.CompilerParams(vmem_limit_bytes=VMEM_LIMIT),
        name="pool",
    )(points, point_pillar.reshape(chunks, CHUNK), point_pillar.reshape(1, total), weight)


def message_rows(tile_rows, tile_cols):
    spans, at = [], 0
    for down, right in STEPS:
        size = (HALO if down else tile_rows) * (SIDE if right else tile_cols)
        spans.append((at, size))
        at += size
    return spans, at


def ring_size(columns):
    return 8 if columns % 16 == 0 else columns


def ring_order(ring):
    order = []
    for far in range(ring // 2 - 1, 0, -1):
        order += [far, -far]
    return order + [0]


def map_kernel(
    grid,
    pillars,
    cells,
    mask_t,
    occupied_t,
    weights,
    head_row,
    points,
    local,
    point_weight,
    table,
    counts,
    conv_second,
    point_second,
    head_second,
    conv_out,
    point_out,
    head_out,
    place,
    pick,
    send_f,
    got_f,
    send_m,
    got_m,
    v0,
    v1,
    v2,
    v3,
    send_i,
    got_i,
    got_x,
    send_y,
    got_y,
    own_g,
    got_g,
    send_r,
    returned,
    own_k,
    core_k,
    send_k,
    got_kz,
    send_kx,
    got_kx,
    got_ky,
    got_ax,
    second,
    merge_a,
    merge_b,
    slopes,
    picks,
    rows_b,
    own_s,
    got_sy,
    got_sx,
    got_sz,
    sem_f,
    sem_m,
    sem_i,
    sem_x,
    sem_y,
    sem_g,
    sem_r,
    sem_c,
    sem_kz,
    sem_kx,
    sem_ky,
    sem_ax,
    sem_az,
    sem_ac,
    sem_sy,
    sem_sx,
    sem_sz,
    sem_l,
    got_far,
    send_far,
    place_far,
    pick_far,
    sem_far,
    sem_back,
):
    n_gy, n_gx, tile_rows, tile_cols = grid
    gy, gx = lax.axis_index("gy"), lax.axis_index("gx")
    ring = ring_size(n_gx)
    across = n_gx // ring
    half_ring = ring // 2
    order = ring_order(ring)
    slot_of = {rel: r for r, rel in enumerate(order)}
    middle = half_ring // 2
    half_block = CHUNK // 2
    x, y = gx // ring, lax.rem(gx, ring)
    channels = pillars.shape[1]
    spans, _ = message_rows(tile_rows, tile_cols)
    width = tile_cols + 2 * SIDE
    height = tile_rows + 2 * HALO
    count = tile_rows * tile_cols
    part_rows = count // PARTS
    fan = across * CHUNK

    def neighbour(k):
        down, right = STEPS[k]
        return lax.rem(gy + down + n_gy, n_gy), lax.rem(gx + right + n_gx, n_gx)

    def along(step):
        return lax.rem(y + step + ring, ring)

    def over(step):
        return lax.rem(x + step + across, across)

    def ring_device(step):
        return gy, x * ring + along(step)

    def across_device(step):
        return gy, over(step) * ring + y

    levels = n_gy // 2
    z, core = gy // 2, lax.rem(gy, 2)

    def level_device(step):
        return lax.rem(z + step, levels) * 2 + core, gx

    other_core = (z * 2 + 1 - core, gx)

    def stack_device(step):
        return lax.rem(gy + step, n_gy), gx

    def slot_half(column, place_on_ring, side):
        at = (column * ring + place_on_ring) * CHUNK + side * half_block
        return pl.ds(pl.multiple_of(at, half_block), half_block)

    def middle_device(o, side):
        away = half_ring - middle if side == 0 else middle - half_ring
        return gy, over(o) * ring + along(away)

    def slot_block(column, place_on_ring):
        return pl.ds(pl.multiple_of((column * ring + place_on_ring) * CHUNK, CHUNK), CHUNK)

    def remote(src, dst, send, recv, device):
        return pltpu.make_async_remote_copy(
            src_ref=src,
            dst_ref=dst,
            send_sem=send,
            recv_sem=recv,
            device_id=device,
            device_id_type=MESH,
        )

    def arrival(ref, sem):
        remote(ref, ref, sem, sem, ring_device(1)).wait_recv()

    share = own_k.shape[2]
    piece = got_ky.shape[1]
    load = pltpu.make_async_copy(
        conv_second.at[pl.ds(pl.multiple_of(gy * share, 8), share)],
        second.at[pl.ds(0, share)],
        sem_l,
    )
    load.start()
    barrier = pltpu.get_barrier_semaphore()
    partners = [neighbour(k) for k in range(len(STEPS))]
    partners += [ring_device(step) for step in range(1, ring)]
    partners += [across_device(step) for step in range(1, across)]
    partners += [stack_device(step) for step in range(1, n_gy)]
    partners += [middle_device(o, side) for o in range(1, across) for side in (0, 1)]
    for device in partners:
        pl.semaphore_signal(barrier, inc=1, device_id=device, device_id_type=MESH)
    pl.semaphore_wait(barrier, len(partners))

    started = []

    def go(copy):
        copy.start()
        started.append(copy)

    def send_pillars(r):
        for o in range(1, across):
            go(
                remote(
                    pillars.at[slot_block(over(o), along(order[r]))],
                    got_x.at[pl.ds((r * across + o) * CHUNK, CHUNK)],
                    sem_x.at[0, r, o],
                    sem_x.at[1, r, o],
                    across_device(o),
                )
            )

    for r in (0, 1):
        send_pillars(r)
    for side in (0, 1):
        for o in range(across):
            go(
                remote(
                    pillars.at[slot_half(over(o), along(half_ring), side)],
                    got_far.at[side, pl.ds(o * half_block, half_block)],
                    sem_far.at[0, side, o],
                    sem_far.at[1, side, o],
                    middle_device(o, side),
                )
            )

    send_i[...] = jnp.zeros_like(send_i)
    for step in range(ring):
        lead = step * 8
        for o in range(across):
            row = over(-o) * ring + along(step)
            send_i[lead + o : lead + o + 1, :] = cells[pl.ds(row, 1), :]
            row = over(-o) * ring + along(half_ring)
            send_i[lead + 4 + o : lead + 5 + o, :] = cells[pl.ds(row, 1), :]
        if step == 0:
            got_i[pl.ds(slot_of[0] * 8, 8), :] = send_i[pl.ds(0, 8), :]
        elif step != half_ring:
            slot = slot_of[-step if step < half_ring else ring - step]
            go(
                remote(
                    send_i.at[pl.ds(lead, 8)],
                    got_i.at[pl.ds(slot * 8, 8)],
                    sem_i.at[0, step],
                    sem_i.at[1, slot],
                    ring_device(step),
                )
            )

    def post(own, send, got, sem):
        grid3 = own.reshape(tile_rows, tile_cols, channels)
        for k, (down, right) in enumerate(STEPS):
            part = grid3
            if down:
                part = part[:HALO] if down < 0 else part[tile_rows - HALO :]
            if right:
                part = part[:, :SIDE] if right < 0 else part[:, tile_cols - SIDE :]
            at, size = spans[k]
            send[pl.ds(at, size), :] = part.reshape(size, channels).astype(BF16)
            there, _ = spans[k ^ 1]
            go(
                remote(
                    send.at[pl.ds(at, size)],
                    got.at[pl.ds(there, size)],
                    sem.at[0, k],
                    sem.at[1, k ^ 1],
                    neighbour(k),
                )
            )

    def collect(own, got, sem):
        parts = {}
        for k, (down, right) in enumerate(STEPS):
            at, size = spans[k]
            arrival(got.at[pl.ds(at, size)], sem.at[1, k])
            rows = HALO if down else tile_rows
            parts[down, right] = (
                got[pl.ds(at, size), :].astype(F32).reshape(rows, size // rows, channels)
            )
        parts[0, 0] = own.reshape(tile_rows, tile_cols, channels)
        return jnp.concatenate(
            [
                jnp.concatenate([parts[down, right] for right in (-1, 0, 1)], axis=1).reshape(
                    -1, channels
                )
                for down in (-1, 0, 1)
            ],
            axis=0,
        )

    masks = jnp.concatenate([mask_t[...], mask_t[...] * occupied_t[...]], axis=0)
    masks = masks.astype(F32).astype(BF16)
    of_row = iota((count, tile_rows), 0) // tile_cols == iota((count, tile_rows), 1)
    by_column = dot_nt(jnp.where(of_row, 1.0, 0.0).astype(BF16), masks)
    pairs = (count, 2 * tile_cols)
    of_column = iota(pairs, 0) % tile_cols == iota(pairs, 1) % tile_cols
    halves = (2 * tile_cols, channels)
    same_half = (iota(halves, 0) < tile_cols) == (iota(halves, 1) < channels // 2)
    mask_own = dot(
        jnp.where(of_column, by_column, 0.0).astype(BF16),
        jnp.where(same_half, 1.0, 0.0).astype(BF16),
    )
    post(mask_own, send_m, got_m, sem_m)

    flat = iota((height * width, channels), 0)
    row = flat // width + gy * tile_rows - HALO
    col = flat % width + gx * tile_cols - SIDE
    in_slab = jnp.where(
        (row >= 0) & (row < n_gy * tile_rows) & (col >= 0) & (col < n_gx * tile_cols), 1.0, 0.0
    )
    column = iota((tile_rows * width, channels), 0) % width
    own_column = jnp.where((column >= SIDE) & (column < SIDE + tile_cols), 1.0, 0.0)

    for r in range(len(order) - 1):
        arrival(got_i.at[pl.ds(r * 8, 8)], sem_i.at[1, r])
    rows_i = len(order) * 8
    cells_i = got_i[...]
    cells_t = jnp.concatenate(
        [cells_i.astype(F32), jnp.zeros(((-rows_i) % CHUNK, CHUNK), F32)], axis=0
    ).T.astype(jnp.int32)
    def build_place(r):
        for o in range(across):
            at = r * 8 + o
            place[r, :, pl.ds(o * CHUNK, CHUNK)] = jnp.where(
                iota((count, CHUNK), 0) == cells_i[at : at + 1, :], 1.0, 0.0
            ).astype(BF16)

    def build_pick(r):
        for o in range(across):
            at = r * 8 + o
            pick[r, pl.ds(o * CHUNK, CHUNK), :] = jnp.where(
                cells_t[:, at : at + 1] == iota((CHUNK, count), 1), 1.0, 0.0
            ).astype(BF16)

    def build_far(side):
        lead = slot_of[middle if side == 0 else -middle] * 8 + 4
        lower = iota((1, CHUNK), 1) < half_block
        for o in range(0, across, 2):
            one, two = (cells_i[at : at + 1, :] for at in (lead + o, lead + o + 1))
            if side == 0:
                two = pltpu.roll(two, half_block, axis=1)
            else:
                one = pltpu.roll(one, half_block, axis=1)
            place_far[side, :, pl.ds(o * half_block, CHUNK)] = jnp.where(
                iota((count, CHUNK), 0) == jnp.where(lower, one, two), 1.0, 0.0
            ).astype(BF16)
        for o in range(across):
            rows = cells_t[side * half_block : (side + 1) * half_block, lead + o : lead + o + 1]
            pick_far[side, pl.ds(o * half_block, half_block), :] = jnp.where(
                rows == iota((half_block, count), 1), 1.0, 0.0
            ).astype(BF16)

    def cut(value, lead, rows):
        return value[lead * width : (lead + rows) * width]

    def side_by_side(value, ref):
        size = value.shape[0]
        left = pltpu.roll(value, 1, axis=0)
        right = pltpu.roll(value, size - 1, axis=0)
        ref[...] = jnp.concatenate([left.astype(BF16), value.astype(BF16), right.astype(BF16)], 1)

    def windows(ref, lead, rows):
        return jnp.concatenate(
            [ref[pl.ds((lead + a) * width, rows * width), :] for a in (0, 1, 2)], axis=1
        )

    def flipped(layer):
        return jnp.concatenate(
            [weights[layer, pl.ds((8 - k) * channels, channels), :] for k in range(9)], axis=1
        )

    def placed_for(r):
        for o in range(1, across):
            arrival(got_x.at[pl.ds((r * across + o) * CHUNK, CHUNK)], sem_x.at[1, r, o])
        own = pillars[slot_block(x, along(order[r])), :]
        rest = got_x[pl.ds((r * across + 1) * CHUNK, fan - CHUNK), :]
        return dot(place[r], jnp.concatenate([own, rest], axis=0))

    pieces = [pl.ds(q * part_rows, part_rows) for q in range(PARTS)]

    def grow(t, side, q, value):
        if t:
            arrival(got_y.at[side, t - 1, pieces[q]], sem_y.at[1, side, t - 1, q])
            value = value + got_y[side, t - 1, pieces[q], :].astype(F32)
        send_y[side, t, pieces[q], :] = value.astype(BF16)
        go(
            remote(
                send_y.at[side, t, pieces[q]],
                got_y.at[side, t, pieces[q]],
                sem_y.at[0, side, t, q],
                sem_y.at[1, side, t, q],
                ring_device(1 - 2 * side),
            )
        )

    left = list(range(len(order)))
    for t in range(half_ring - 1):
        for r in range(2 * t + 2, min(2 * t + 4, len(order))):
            send_pillars(r)
        summed = {}
        for side in (0, 1):
            away = half_ring - 1 - t
            r = slot_of[away if side == 0 else -away]
            build_place(r)
            if away == middle:
                build_far(side)
            value = placed_for(r)
            if away == middle:
                for o in range(across):
                    arrival(
                        got_far.at[side, pl.ds(o * half_block, half_block)], sem_far.at[1, side, o]
                    )
                value = value + dot(place_far[side], got_far[side])
            summed[side] = value
        for q in range(PARTS):
            for side in (0, 1):
                grow(t, side, q, summed[side][q * part_rows : (q + 1) * part_rows])
        for r in left[:2]:
            build_pick(r)
        left = left[2:]
    build_place(slot_of[0])
    placed = placed_for(slot_of[0])
    for r in left:
        build_pick(r)
    mask_all = (collect(mask_own, got_m, sem_m) * in_slab).astype(BF16)
    half = channels // 2
    spread = jnp.where(
        iota((channels, 2 * channels), 0)
        == jnp.where(iota((channels, 2 * channels), 1) < channels, 0, half),
        1.0,
        0.0,
    ).astype(BF16)
    mask_all = dot(mask_all, spread)
    hidden_cell = mask_all[:, :channels]
    target = mask_all[:, channels:]

    visible = 1.0 - cut(hidden_cell, HALO, tile_rows).reshape(tile_rows, width, channels)[
        :, SIDE : SIDE + tile_cols
    ].reshape(count, channels)

    last = half_ring - 2
    ends = []
    for q in range(PARTS):
        value = placed[q * part_rows : (q + 1) * part_rows]
        for side in (0, 1):
            arrival(got_y.at[side, last, pieces[q]], sem_y.at[1, side, last, q])
            value = value + got_y[side, last, pieces[q], :].astype(F32)
        ends.append(value)
    placed = jnp.concatenate(ends, axis=0)

    parts = levels // 2

    def halve(layer, gradient):
        own_k[pl.ds(layer * parts, parts)] = gradient.reshape(
            parts, 2, share, channels
        ).astype(BF16)
        go(
            remote(
                own_k.at[pl.ds(layer * parts, parts), 1 - core],
                core_k.at[pl.ds(layer * parts, parts)],
                sem_c.at[0, layer],
                sem_c.at[1, layer],
                other_core,
            )
        )

    features = (placed * visible).astype(BF16).astype(F32)
    post(features, send_f, got_f, sem_f)
    side_by_side(collect(features, got_f, sem_f) * in_slab, v0)

    pre1 = dot(windows(v0, 0, height - 2), weights[0])
    side_by_side(pre1 * jax.nn.sigmoid(pre1) * cut(in_slab, 1, height - 2), v1)
    pre2 = dot(windows(v1, 0, height - 4), weights[1])
    sig2 = jax.nn.sigmoid(pre2)
    hidden2 = (pre2 * sig2).astype(BF16)
    head = jnp.broadcast_to(head_row[...], (channels, channels))
    logits = dot_nt(hidden2, head)
    cells_all = n_gy * tile_rows * n_gx * tile_cols
    logit_grad = (
        cut(hidden_cell, 2, height - 4) * jax.nn.sigmoid(logits) - cut(target, 2, height - 4)
    ) / cells_all
    grad2 = logit_grad * head_row[...].astype(F32) * (sig2 * (1.0 + pre2 * (1.0 - sig2)))
    side_by_side(grad2, v2)
    own2 = (cut(grad2, 2, tile_rows) * own_column).astype(BF16)
    halve(1, dot_tn(windows(v1, 2, tile_rows), own2))
    back2 = dot_nt(windows(v2, 0, height - 6), flipped(1))
    grad1 = back2 * slope(cut(pre1, 2, height - 6)) * cut(in_slab, 3, height - 6)
    side_by_side(grad1, v3)
    own1 = (cut(grad1, 1, tile_rows) * own_column).astype(BF16)
    halve(0, dot_tn(windows(v0, 3, tile_rows), own1))
    back1 = dot_nt(windows(v3, 0, tile_rows), flipped(0))
    back1 = back1.reshape(tile_rows, width, channels)[:, SIDE : SIDE + tile_cols].reshape(
        count, channels
    )
    own_g[...] = (back1 * visible).astype(BF16)

    def pass_on(t, side, q):
        src = own_g if t == 1 else got_g.at[side, t - 2]
        go(
            remote(
                src.at[pieces[q]],
                got_g.at[side, t - 1, pieces[q]],
                sem_g.at[0, side, t - 1, q],
                sem_g.at[1, side, t - 1, q],
                ring_device(1 - 2 * side),
            )
        )

    def hand_far(side, gradient):
        rel = middle if side == 0 else -middle
        send_far[side] = dot(pick_far[side], gradient).astype(BF16)
        for o in range(across):
            go(
                remote(
                    send_far.at[side, pl.ds(o * half_block, half_block)],
                    returned.at[slot_half(x, along(rel), side)],
                    sem_back.at[0, side, o],
                    sem_back.at[1, side, o],
                    middle_device(-o, 1 - side),
                )
            )

    def hand_out(rel, gradient):
        r = slot_of[rel]
        rows = dot(pick[r], gradient).astype(BF16)
        returned[slot_block(x, along(rel)), :] = rows[:CHUNK]
        send_r[r] = rows
        for o in range(1, across):
            go(
                remote(
                    send_r.at[r, pl.ds(o * CHUNK, CHUNK)],
                    returned.at[slot_block(x, along(rel))],
                    sem_r.at[0, r, o],
                    sem_r.at[1, r, o],
                    across_device(-o),
                )
            )

    def to_levels():
        for layer in (0, 1):
            arrival(core_k.at[pl.ds(layer * parts, parts)], sem_c.at[1, layer])
        for k in range(levels):
            send_k[k] = (own_k[k, core].astype(F32) + core_k[k].astype(F32)).astype(BF16)
        got_kz[z] = send_k[z]
        for step in range(1, levels):
            go(
                remote(
                    send_k.at[lax.rem(z + step, levels)],
                    got_kz.at[z],
                    sem_kz.at[0, step],
                    sem_kz.at[1, step],
                    level_device(step),
                )
            )

    def gathered(got, sem):
        summed = None
        for step in range(1, got.shape[0]):
            arrival(got.at[0], sem.at[1, step])
        for k in range(got.shape[0]):
            term = got[k].astype(F32)
            summed = term if summed is None else summed + term
        return summed

    def to_all(value, got, sem, me, device):
        got[me] = value.astype(got.dtype)
        for step in range(1, got.shape[0]):
            go(remote(got.at[me], got.at[me], sem.at[0, step], sem.at[1, step], device(step)))

    def to_pieces(summed):
        spare = across * piece - share
        if spare:
            summed = jnp.concatenate([summed, jnp.zeros((spare, channels), F32)], axis=0)
        send_kx[...] = summed.reshape(across, piece, channels).astype(BF16)
        got_kx[x] = send_kx[x]
        for step in range(1, across):
            go(
                remote(
                    send_kx.at[over(step)],
                    got_kx.at[x],
                    sem_kx.at[0, step],
                    sem_kx.at[1, step],
                    across_device(step),
                )
            )

    def take_step(summed):
        load.wait()
        if across * piece > share:
            second[pl.ds(share, across * piece - share), :] = jnp.ones(
                (across * piece - share, channels), F32
            )
        rows = pl.ds(pl.multiple_of(x * piece, 8), piece)
        return rms_step(summed, second[rows, :])

    chunks = local.shape[0]
    blocks = counts.shape[0]

    def turned(value):
        spare = (-value.shape[0]) % CHUNK
        return jnp.concatenate([value, jnp.zeros((spare, CHUNK), F32)], axis=0).T

    ranks_t = turned(local[...].astype(F32)).astype(jnp.int32)

    def prepare(begin, end):
        for k in range(begin, end):
            part = pl.ds(k * CHUNK, CHUNK)
            slopes[part, :] = slope(dot_tn(points[:, part], point_weight[...]))
            picks[part, :] = jnp.where(
                ranks_t[:, k : k + 1] == iota((CHUNK, CHUNK), 1), 1.0, 0.0
            ).astype(BF16)

    scale = turned(1.0 / counts[...])

    def start_merge():
        for d in range(blocks):
            part = pl.ds(d * CHUNK, CHUNK)
            merge_a[part, :] = returned[part, :].astype(F32) * scale[:, d : d + 1]
        spare = merge_a.shape[0] - blocks * CHUNK
        for ref in (merge_a, merge_b):
            ref[pl.ds(blocks * CHUNK, spare), :] = jnp.zeros((spare, CHUNK), F32)

    def merge_level(level, src, dst):
        size = CHUNK << level
        for pair in range(blocks >> (level + 1)):
            lead = pair * 2 * size
            first = chunks + pair * (2 << level)
            held = table[first + (1 << level), 0] - table[first, 0]
            for at in range(0, 2 * size, 2 * CHUNK):
                rows = iota((2 * CHUNK, CHUNK), 0) + at
                dst[pl.ds(lead + at, 2 * CHUNK), :] = jnp.where(
                    rows < held,
                    src[pl.ds(lead + at, 2 * CHUNK), :],
                    src[pl.ds(lead + at + size - held, 2 * CHUNK), :],
                )

    levels_m = blocks.bit_length() - 1
    refs = (merge_a, merge_b)

    def merge(begin, end):
        for level in range(begin, end):
            merge_level(level, refs[level % 2], refs[1 - level % 2])

    def point_terms():
        joined = refs[levels_m % 2]
        for k in range(chunks):
            part = pl.ds(k * CHUNK, CHUNK)
            window = joined[pl.ds(table[k, 0], CHUNK), :].astype(BF16)
            rows_b[part, :] = (dot(picks[part, :], window) * slopes[part, :]).astype(BF16)
        return dot(points[...], rows_b[...])

    for q in range(PARTS):
        for side in (0, 1):
            pass_on(1, side, q)
    hand_out(0, own_g[...])
    to_levels()
    head_terms = cut(logit_grad * hidden2.astype(F32), 2, tile_rows) * own_column
    head_local = jnp.sum(head_terms, axis=0, keepdims=True)
    prepared = 0
    for t in range(1, half_ring):
        for q in range(PARTS):
            for side in (0, 1):
                arrival(got_g.at[side, t - 1, pieces[q]], sem_g.at[1, side, t - 1, q])
                if t + 1 < half_ring:
                    pass_on(t + 1, side, q)
        if t == middle:
            hand_far(0, got_g[1, t - 1])
            hand_far(1, got_g[0, t - 1])
        hand_out(-t, got_g[0, t - 1])
        hand_out(t, got_g[1, t - 1])
        share_to = chunks * t // (half_ring - 1)
        prepare(prepared, share_to)
        prepared = share_to
    to_pieces(gathered(got_kz, sem_kz))
    for r, rel in enumerate(order):
        for o in range(1, across):
            arrival(returned.at[slot_block(over(o), along(rel))], sem_r.at[1, r, o])
    for side in (0, 1):
        for o in range(across):
            arrival(
                returned.at[slot_half(over(o), along(half_ring), side)], sem_back.at[1, side, o]
            )
    start_merge()
    to_all(gathered(got_kx, sem_kx), got_ky, sem_ky, y, ring_device)
    merge(0, min(3, levels_m))
    to_all(take_step(gathered(got_ky, sem_ky)), got_ax, sem_ax, x, across_device)
    merge(min(3, levels_m), levels_m)
    for step in range(1, across):
        arrival(got_ax.at[0], sem_ax.at[1, step])
    conv_out[gy] = got_ax[...].reshape(across * piece, channels)[:share]
    mine = conv_out.at[gy]
    for step in range(1, levels):
        go(remote(mine, mine, sem_az.at[0, step], sem_az.at[1, step], level_device(step)))
    go(remote(mine, mine, sem_ac.at[0, 0], sem_ac.at[1, 0], other_core))
    features_in = points.shape[0]
    own_s[...] = jnp.zeros_like(own_s)
    own_s[0:features_in, :] = point_terms()
    own_s[features_in : features_in + 1, :] = head_local
    to_all(own_s[...], got_sy, sem_sy, y, ring_device)

    def relay(begin, end):
        for step in range(begin, end):
            held = conv_out.at[lax.rem(z - step + levels, levels) * 2 + core]
            arrival(held, sem_az.at[1, step])
            go(remote(held, held, sem_ac.at[0, step], sem_ac.at[1, step], other_core))

    relay(1, min(3, levels))
    to_all(gathered(got_sy, sem_sy), got_sx, sem_sx, x, across_device)
    relay(min(3, levels), min(6, levels))
    to_all(gathered(got_sx, sem_sx), got_sz, sem_sz, gy, stack_device)
    relay(min(6, levels), levels)
    small = gathered(got_sz, sem_sz)
    point_out[...] = rms_step(small[:features_in], point_second[...])
    head_out[...] = rms_step(small[features_in : features_in + 1], head_second[...])
    for step in range(levels):
        level = lax.rem(z - step + levels, levels)
        arrival(conv_out.at[level * 2 + 1 - core], sem_ac.at[1, step])
    for copy in started:
        copy.wait_send()


def map_step(grid, pillars, recv_cell, cell_mask, occupancy, weights, head_weight, points, local,
             point_weight, table, counts, conv_second, point_second, head_second):
    n_gy, n_gx, tile_rows, tile_cols = grid
    slots, channels = pillars.shape
    total = points.shape[1]
    blocks = slots // CHUNK
    count = tile_rows * tile_cols
    width = tile_cols + 2 * SIDE
    height = tile_rows + 2 * HALO
    ring = ring_size(n_gx)
    across, half_ring = n_gx // ring, ring // 2
    _, rows = message_rows(tile_rows, tile_cols)
    vmem = pl.BlockSpec(memory_space=pltpu.VMEM)
    smem = pl.BlockSpec(memory_space=pltpu.SMEM)
    taps = weights.shape[1]
    levels = n_gy // 2
    share = 2 * taps * channels // n_gy
    piece = -(-share // (across * 16)) * 16
    few = -(-(points.shape[0] + 1) // 8) * 8
    return pl.pallas_call(
        functools.partial(map_kernel, grid),
        out_shape=(
            jax.ShapeDtypeStruct((n_gy, share, channels), BF16),
            jax.ShapeDtypeStruct(point_weight.shape, F32),
            jax.ShapeDtypeStruct((1, channels), F32),
        ),
        in_specs=[vmem] * 9 + [smem, vmem, pl.BlockSpec(memory_space=pl.ANY), vmem, vmem],
        out_specs=(vmem,) * 3,
        scratch_shapes=[
            pltpu.VMEM((ring - 1, count, across * CHUNK), BF16),
            pltpu.VMEM((ring - 1, across * CHUNK, count), BF16),
            pltpu.VMEM((rows, channels), BF16),
            pltpu.VMEM((rows, channels), BF16),
            pltpu.VMEM((rows, channels), BF16),
            pltpu.VMEM((rows, channels), BF16),
            pltpu.VMEM((height * width, 3 * channels), BF16),
            pltpu.VMEM(((height - 2) * width, 3 * channels), BF16),
            pltpu.VMEM(((height - 4) * width, 3 * channels), BF16),
            pltpu.VMEM(((height - 6) * width, 3 * channels), BF16),
            pltpu.VMEM((ring * 8, CHUNK), jnp.int32),
            pltpu.VMEM(((ring - 1) * 8, CHUNK), jnp.int32),
            pltpu.VMEM(((ring - 1) * across * CHUNK, channels), BF16),
            pltpu.VMEM((2, half_ring - 1, count, channels), BF16),
            pltpu.VMEM((2, half_ring - 1, count, channels), BF16),
            pltpu.VMEM((count, channels), BF16),
            pltpu.VMEM((2, half_ring - 1, count, channels), BF16),
            pltpu.VMEM((ring - 1, across * CHUNK, channels), BF16),
            pltpu.VMEM((slots, channels), BF16),
            pltpu.VMEM((levels, 2, share, channels), BF16),
            pltpu.VMEM((levels, share, channels), BF16),
            pltpu.VMEM((levels, share, channels), BF16),
            pltpu.VMEM((levels, share, channels), BF16),
            pltpu.VMEM((across, piece, channels), BF16),
            pltpu.VMEM((across, piece, channels), BF16),
            pltpu.VMEM((ring, piece, channels), BF16),
            pltpu.VMEM((across, piece, channels), BF16),
            pltpu.VMEM((across * piece, channels), F32),
            pltpu.VMEM((slots + slots // 2, channels), F32),
            pltpu.VMEM((slots + slots // 2, channels), F32),
            pltpu.VMEM((total, channels), F32),
            pltpu.VMEM((total, CHUNK), BF16),
            pltpu.VMEM((total, channels), BF16),
            pltpu.VMEM((few, channels), F32),
            pltpu.VMEM((ring, few, channels), F32),
            pltpu.VMEM((across, few, channels), F32),
            pltpu.VMEM((n_gy, few, channels), F32),
            pltpu.SemaphoreType.DMA((2, len(STEPS))),
            pltpu.SemaphoreType.DMA((2, len(STEPS))),
            pltpu.SemaphoreType.DMA((2, ring)),
            pltpu.SemaphoreType.DMA((2, ring, across)),
            pltpu.SemaphoreType.DMA((2, 2, half_ring - 1, PARTS)),
            pltpu.SemaphoreType.DMA((2, 2, half_ring - 1, PARTS)),
            pltpu.SemaphoreType.DMA((2, ring, across)),
            pltpu.SemaphoreType.DMA((2, 2)),
            pltpu.SemaphoreType.DMA((2, levels)),
            pltpu.SemaphoreType.DMA((2, across)),
            pltpu.SemaphoreType.DMA((2, ring)),
            pltpu.SemaphoreType.DMA((2, across)),
            pltpu.SemaphoreType.DMA((2, levels)),
            pltpu.SemaphoreType.DMA((2, levels)),
            pltpu.SemaphoreType.DMA((2, ring)),
            pltpu.SemaphoreType.DMA((2, across)),
            pltpu.SemaphoreType.DMA((2, n_gy)),
            pltpu.SemaphoreType.DMA,
            pltpu.VMEM((2, across * CHUNK // 2, channels), BF16),
            pltpu.VMEM((2, across * CHUNK // 2, channels), BF16),
            pltpu.VMEM((2, count, across * CHUNK // 2), BF16),
            pltpu.VMEM((2, across * CHUNK // 2, count), BF16),
            pltpu.SemaphoreType.DMA((2, 2, across)),
            pltpu.SemaphoreType.DMA((2, 2, across)),
        ],
        compiler_params=pltpu.CompilerParams(
            vmem_limit_bytes=VMEM_LIMIT, collective_id=1, has_side_effects=True
        ),
        name="map_step",
    )(
        pillars,
        recv_cell.reshape(blocks, CHUNK),
        cell_mask.T,
        occupancy.T,
        weights.reshape(2, taps * channels, channels),
        head_weight.reshape(1, channels),
        points,
        local,
        point_weight,
        table,
        counts,
        conv_second.reshape(n_gy * share, channels),
        point_second,
        head_second.reshape(1, channels),
    )


def on_device(
    points,
    point_pillar,
    point_weight,
    recv_cell,
    cell_mask,
    occupancy,
    conv_weight,
    head_weight,
    conv_second,
    point_second,
    head_second,
):
    rows, columns = lax.axis_size("gy"), lax.axis_size("gx")
    tile_rows, tile_cols = cell_mask.shape
    channels = point_weight.shape[1]
    slots = recv_cell.shape[0]
    grid = (rows, columns, tile_rows, tile_cols)

    pillars, table, local, counts = pool(points, point_pillar, point_weight, slots)
    conv_step, point_step, head_step = map_step(
        grid,
        pillars,
        recv_cell,
        cell_mask,
        occupancy,
        conv_weight,
        head_weight,
        points,
        local,
        point_weight,
        table,
        counts,
        conv_second,
        point_second,
        head_second,
    )
    return conv_step.astype(F32).reshape(conv_second.shape), point_step, head_step[0]


def solution(mesh):
    return jax.shard_map(
        on_device,
        mesh=mesh,
        in_specs=(
            P(None, ("gy", "gx")),
            P(("gy", "gx")),
            P(),
            P(("gy", "gx")),
            P("gy", "gx"),
            P("gy", "gx"),
            P(),
            P(),
            P(),
            P(),
            P(),
        ),
        out_specs=(P(), P(), P()),
        check_vma=False,
    )
```

```python
import functools

import jax
import jax.numpy as jnp
from jax import lax
from jax.experimental import pallas as pl
from jax.experimental.pallas import tpu as pltpu
from jax.sharding import PartitionSpec as P

MESH = pl.DeviceIdType.MESH
F32 = jnp.float32
BF16 = jnp.bfloat16
VMEM_LIMIT = 56 * 1024 * 1024
CHUNK = 128
SIDE = 8
HALO = 4
STEPS = ((0, -1), (0, 1), (-1, 0), (1, 0), (-1, -1), (1, 1), (-1, 1), (1, -1))


def iota(shape, dim):
    return lax.broadcasted_iota(jnp.int32, shape, dim)


def dot(a, b):
    return jnp.dot(a, b, preferred_element_type=F32)


def dot_nt(a, b):
    return lax.dot_general(a, b, (((1,), (1,)), ((), ())), preferred_element_type=F32)


def dot_tn(a, b):
    return lax.dot_general(a, b, (((0,), (0,)), ((), ())), preferred_element_type=F32)


def slope(value):
    sig = jax.nn.sigmoid(value)
    return sig * (1.0 + value * (1.0 - sig))


def rms_step(gradient, second):
    moment = 0.95 * second + 0.05 * gradient * gradient
    return gradient / (jnp.sqrt(moment) + 1e-08)


def ring_size(columns):
    return {32: 8, 8: 4, 4: 2}[columns]


def tile_places(columns):
    ring = ring_size(columns)
    across = columns // ring
    gx = lax.axis_index("gx")
    x, y = gx // ring, lax.rem(gx, ring)

    def rows(d):
        away = lax.rem(d // ring - x + across, across)
        place = lax.rem(d % ring - y + ring + ring // 2 - 1, ring)
        return pl.ds(pl.multiple_of((away * ring + place) * CHUNK, CHUNK), CHUNK)

    return rows


def pool_kernel(
    columns,
    points, ids, ids_row, weight, pillars, table, local, counts, table_s, partial, sums, numbers, sem
):
    chunks = ids.shape[0]
    blocks = pillars.shape[0] // CHUNK
    total = chunks * CHUNK
    here = ids[...]
    back = pltpu.roll(here, 1, axis=1)
    lane = iota(here.shape, 1)
    before = jnp.where(lane == 0, pltpu.roll(back, 1, axis=0), back)
    first = (lane == 0) & (iota(here.shape, 0) == 0)
    flags = jnp.where((here != before) | first, 1.0, 0.0).astype(BF16)
    upto = jnp.where(iota((CHUNK, CHUNK), 0) <= iota((CHUNK, CHUNK), 1), 1.0, 0.0).astype(BF16)
    inside = dot(flags, upto)
    whole = dot(flags, jnp.ones((CHUNK, CHUNK), BF16))
    lower = jnp.where(iota((chunks, chunks), 0) > iota((chunks, chunks), 1), 1.0, 0.0)
    ahead = dot(lower.astype(BF16), whole.astype(BF16))
    head = jnp.broadcast_to(inside[:, 0:1], inside.shape)
    local[...] = (inside - head).astype(jnp.int32)
    row = ids_row[...]
    row_before = pltpu.roll(row, 1, axis=1)
    row_first = (row != row_before) | (iota(row.shape, 1) == 0)
    row_block = jnp.where(row_first, row // CHUNK, blocks + 8)
    below = jnp.where(row_block < iota((blocks + 8, total), 0), 1.0, 0.0).astype(BF16)
    table[0:chunks, :] = (ahead + head - 1.0).astype(jnp.int32)
    table[chunks : chunks + blocks + 8, :] = dot(below, jnp.ones((total, CHUNK), BF16)).astype(
        jnp.int32
    )
    copy = pltpu.make_async_copy(table, table_s, sem)
    copy.start()
    ranks = local[...]
    for k in range(chunks):
        part = pl.ds(k * CHUNK, CHUNK)
        pre = dot_tn(points[:, part], weight[...])
        act = (pre * jax.nn.sigmoid(pre)).astype(BF16)
        pick = jnp.where(iota((CHUNK, CHUNK), 0) == ranks[k : k + 1, :], 1.0, 0.0).astype(BF16)
        partial[part, :] = dot(pick, jnp.concatenate([act, jnp.ones_like(act)], axis=1))
    copy.wait()
    edge = jnp.zeros((8, CHUNK), F32)
    for k in range(chunks):
        at = table_s[k, 0]
        for side, compact in enumerate((sums, numbers)):
            got = partial[pl.ds(k * CHUNK, CHUNK), pl.ds(side * CHUNK, CHUNK)]
            first_rows = got[0:8] if k == 0 else compact[pl.ds(at, 8), :] + got[0:8]
            compact[pl.ds(at, CHUNK + 8), :] = jnp.concatenate([first_rows, got[8:], edge], axis=0)
    diagonal = iota((CHUNK, CHUNK), 0) == iota((CHUNK, CHUNK), 1)
    places = tile_places(columns)
    for d in range(blocks):
        at = table_s[chunks + d, 0]
        held = table_s[chunks + d + 1, 0] - at
        named = iota((CHUNK, CHUNK), 0) < held
        count = jnp.where(named, numbers[pl.ds(at, CHUNK), :], 1.0)
        mean = jnp.where(named, sums[pl.ds(at, CHUNK), :] / count, 0.0)
        pillars[places(d), :] = mean.astype(BF16)
        counts[d : d + 1, :] = jnp.sum(jnp.where(diagonal, count, 0.0), axis=0, keepdims=True)


def pool(columns, points, point_pillar, weight, slots):
    total = point_pillar.shape[0]
    chunks, blocks = total // CHUNK, slots // CHUNK
    channels = weight.shape[1]
    rows = chunks + blocks + 8
    vmem = pl.BlockSpec(memory_space=pltpu.VMEM)
    return pl.pallas_call(
        functools.partial(pool_kernel, columns),
        out_shape=(
            jax.ShapeDtypeStruct((slots, channels), BF16),
            jax.ShapeDtypeStruct((rows, CHUNK), jnp.int32),
            jax.ShapeDtypeStruct((chunks, CHUNK), jnp.int32),
            jax.ShapeDtypeStruct((blocks, CHUNK), F32),
        ),
        in_specs=[vmem] * 4,
        out_specs=(vmem,) * 4,
        scratch_shapes=[
            pltpu.SMEM((rows, CHUNK), jnp.int32),
            pltpu.VMEM((total, 2 * CHUNK), F32),
            pltpu.VMEM((total + 2 * CHUNK, CHUNK), F32),
            pltpu.VMEM((total + 2 * CHUNK, CHUNK), F32),
            pltpu.SemaphoreType.DMA,
        ],
        compiler_params=pltpu.CompilerParams(vmem_limit_bytes=VMEM_LIMIT),
        name="pool",
    )(points, point_pillar.reshape(chunks, CHUNK), point_pillar.reshape(1, total), weight)


def message_rows(tile_rows, tile_cols):
    spans, at = [], 0
    for down, right in STEPS:
        size = (HALO if down else tile_rows) * (SIDE if right else tile_cols)
        spans.append((at, size))
        at += size
    return spans, at


def ring_order(ring):
    order = [ring // 2]
    for far in range(ring // 2 - 1, 0, -1):
        order += [far, -far]
    return order + [0]


def map_kernel(
    grid,
    pillars,
    cells,
    mask_t,
    occupied_t,
    weights,
    head_row,
    points,
    local,
    point_weight,
    table,
    counts,
    conv_second,
    point_second,
    head_second,
    conv_out,
    point_out,
    head_out,
    place,
    pick,
    send_f,
    got_f,
    send_m,
    got_m,
    v0,
    v1,
    v2,
    v3,
    send_i,
    got_i,
    got_x,
    send_y,
    got_y,
    own_g,
    got_g,
    send_r,
    returned,
    own_k,
    core_k,
    send_k,
    got_kz,
    send_kx,
    got_kx,
    got_ky,
    got_ax,
    second,
    merge_a,
    merge_b,
    slopes,
    picks,
    rows_b,
    own_s,
    got_sy,
    got_sx,
    got_sz,
    sem_f,
    sem_m,
    sem_i,
    sem_x,
    sem_y,
    sem_g,
    sem_r,
    sem_c,
    sem_kz,
    sem_kx,
    sem_ky,
    sem_ax,
    sem_az,
    sem_ac,
    sem_sy,
    sem_sx,
    sem_sz,
    sem_l,
):
    n_gy, n_gx, tile_rows, tile_cols = grid
    gy, gx = lax.axis_index("gy"), lax.axis_index("gx")
    ring = ring_size(n_gx)
    across = n_gx // ring
    half_ring = ring // 2
    order = ring_order(ring)
    slot_of = {rel: r for r, rel in enumerate(order)}
    slot_of[-half_ring] = slot_of[half_ring]
    x, y = gx // ring, lax.rem(gx, ring)
    channels = pillars.shape[1]
    spans, _ = message_rows(tile_rows, tile_cols)
    width = tile_cols + 2 * SIDE
    height = tile_rows + 2 * HALO
    count = tile_rows * tile_cols
    part_rows = count // 2
    fan = across * CHUNK

    def neighbour(k):
        down, right = STEPS[k]
        return lax.rem(gy + down + n_gy, n_gy), lax.rem(gx + right + n_gx, n_gx)

    def along(step):
        return lax.rem(y + step + ring, ring)

    def over(step):
        return lax.rem(x + step + across, across)

    def ring_device(step):
        return gy, x * ring + along(step)

    def across_device(step):
        return gy, over(step) * ring + y

    levels = n_gy // 2
    z, core = gy // 2, lax.rem(gy, 2)

    def level_device(step):
        return lax.rem(z + step, levels) * 2 + core, gx

    other_core = (z * 2 + 1 - core, gx)

    def stack_device(step):
        return lax.rem(gy + step, n_gy), gx

    def slot_block(column, place_on_ring):
        return pl.ds(pl.multiple_of((column * ring + place_on_ring) * CHUNK, CHUNK), CHUNK)

    def remote(src, dst, send, recv, device):
        return pltpu.make_async_remote_copy(
            src_ref=src,
            dst_ref=dst,
            send_sem=send,
            recv_sem=recv,
            device_id=device,
            device_id_type=MESH,
        )

    def arrival(ref, sem):
        remote(ref, ref, sem, sem, ring_device(1)).wait_recv()

    share = own_k.shape[2]
    piece = got_ky.shape[1]
    load = pltpu.make_async_copy(
        conv_second.at[pl.ds(pl.multiple_of(gy * share, 8), share)],
        second.at[pl.ds(0, share)],
        sem_l,
    )
    load.start()
    barrier = pltpu.get_barrier_semaphore()
    partners = [neighbour(k) for k in range(len(STEPS))]
    partners += [ring_device(step) for step in range(1, ring)]
    partners += [across_device(step) for step in range(1, across)]
    partners += [stack_device(step) for step in range(1, n_gy)]
    for device in partners:
        pl.semaphore_signal(barrier, inc=1, device_id=device, device_id_type=MESH)
    pl.semaphore_wait(barrier, len(partners))

    started = []

    def go(copy):
        copy.start()
        started.append(copy)

    groups = {8: [(6, 8), (0, 2), (4, 6), (2, 4)], 4: [(2, 4), (0, 2)], 2: [(0, 2)]}[ring]
    waited = set()

    def block(o, rel):
        return pl.ds((o * ring + rel + half_ring - 1) * CHUNK, CHUNK)

    def span(o, group):
        return pl.ds((o * ring + group[0]) * CHUNK, (group[1] - group[0]) * CHUNK)

    def send_pillars(g):
        for o in range(1, across):
            rows = span(o, groups[g])
            go(
                remote(
                    pillars.at[rows],
                    got_x.at[rows],
                    sem_x.at[0, g, o],
                    sem_x.at[1, g, o],
                    across_device(o),
                )
            )

    send_pillars(0)

    send_i[...] = jnp.zeros_like(send_i)
    for step in range(ring):
        lead = step * 8
        for o in range(across):
            row = over(-o) * ring + along(step)
            send_i[lead + o : lead + o + 1, :] = cells[pl.ds(row, 1), :]
        if step == 0:
            got_i[pl.ds(slot_of[0] * 8, 8), :] = send_i[pl.ds(0, 8), :]
        else:
            rel = -step if step <= half_ring else ring - step
            slot = slot_of[rel]
            go(
                remote(
                    send_i.at[pl.ds(lead, 8)],
                    got_i.at[pl.ds(slot * 8, 8)],
                    sem_i.at[0, step],
                    sem_i.at[1, slot],
                    ring_device(step),
                )
            )

    def post(own, send, got, sem):
        grid3 = own.reshape(tile_rows, tile_cols, channels)
        for k, (down, right) in enumerate(STEPS):
            part = grid3
            if down:
                part = part[:HALO] if down < 0 else part[tile_rows - HALO :]
            if right:
                part = part[:, :SIDE] if right < 0 else part[:, tile_cols - SIDE :]
            at, size = spans[k]
            send[pl.ds(at, size), :] = part.reshape(size, channels).astype(BF16)
            there, _ = spans[k ^ 1]
            go(
                remote(
                    send.at[pl.ds(at, size)],
                    got.at[pl.ds(there, size)],
                    sem.at[0, k],
                    sem.at[1, k ^ 1],
                    neighbour(k),
                )
            )

    def collect(own, got, sem):
        parts = {}
        for k, (down, right) in enumerate(STEPS):
            at, size = spans[k]
            arrival(got.at[pl.ds(at, size)], sem.at[1, k])
            rows = HALO if down else tile_rows
            parts[down, right] = (
                got[pl.ds(at, size), :].astype(F32).reshape(rows, size // rows, channels)
            )
        parts[0, 0] = own.reshape(tile_rows, tile_cols, channels)
        return jnp.concatenate(
            [
                jnp.concatenate([parts[down, right] for right in (-1, 0, 1)], axis=1).reshape(
                    -1, channels
                )
                for down in (-1, 0, 1)
            ],
            axis=0,
        )

    if len(groups) > 1:
        send_pillars(1)

    flat = iota((height * width, channels), 0)
    row = flat // width + gy * tile_rows - HALO
    col = flat % width + gx * tile_cols - SIDE
    in_slab = jnp.where(
        (row >= 0) & (row < n_gy * tile_rows) & (col >= 0) & (col < n_gx * tile_cols), 1.0, 0.0
    )
    column = iota((tile_rows * width, channels), 0) % width
    own_column = jnp.where((column >= SIDE) & (column < SIDE + tile_cols), 1.0, 0.0)

    for r in range(ring - 1):
        arrival(got_i.at[pl.ds(r * 8, 8)], sem_i.at[1, r])
    rows_i = ring * 8
    cells_i = got_i[...]
    cells_t = jnp.concatenate(
        [cells_i.astype(F32), jnp.zeros(((-rows_i) % CHUNK, CHUNK), F32)], axis=0
    ).T.astype(jnp.int32)
    def build_place(r):
        for o in range(across):
            at = r * 8 + o
            place[r, :, pl.ds(o * CHUNK, CHUNK)] = jnp.where(
                iota((count, CHUNK), 0) == cells_i[at : at + 1, :], 1.0, 0.0
            ).astype(BF16)

    def build_pick(r):
        for o in range(across):
            at = r * 8 + o
            pick[r, pl.ds(o * CHUNK, CHUNK), :] = jnp.where(
                cells_t[:, at : at + 1] == iota((CHUNK, count), 1), 1.0, 0.0
            ).astype(BF16)

    def cut(value, lead, rows):
        return value[lead * width : (lead + rows) * width]

    def side_by_side(value, ref):
        size = value.shape[0]
        left = pltpu.roll(value, 1, axis=0)
        right = pltpu.roll(value, size - 1, axis=0)
        ref[...] = jnp.concatenate([left.astype(BF16), value.astype(BF16), right.astype(BF16)], 1)

    def windows(ref, lead, rows):
        return jnp.concatenate(
            [ref[pl.ds((lead + a) * width, rows * width), :] for a in (0, 1, 2)], axis=1
        )

    def flipped(layer):
        return jnp.concatenate(
            [weights[layer, pl.ds((8 - k) * channels, channels), :] for k in range(9)], axis=1
        )

    def placed_for(r):
        place_at = order[r] + half_ring - 1
        for g, group in enumerate(groups):
            if group[0] <= place_at < group[1] and g not in waited:
                waited.add(g)
                for o in range(1, across):
                    arrival(got_x.at[span(o, group)], sem_x.at[1, g, o])
        rows = [pillars[block(0, order[r]), :]]
        rows += [got_x[block(o, order[r]), :] for o in range(1, across)]
        return dot(place[r], jnp.concatenate(rows, axis=0))

    halves = (pl.ds(0, part_rows), pl.ds(part_rows, part_rows))

    def half_of(value, half):
        return value[half * part_rows : (half + 1) * part_rows]

    def grow(t, side, half, value):
        if t > 1 or (t == 1 and half == side):
            arrival(got_y.at[side, t - 1, halves[half]], sem_y.at[1, side, t - 1, half])
            value = value + got_y[side, t - 1, halves[half], :].astype(F32)
        send_y[side, t, halves[half], :] = value.astype(BF16)
        go(
            remote(
                send_y.at[side, t, halves[half]],
                got_y.at[side, t, halves[half]],
                sem_y.at[0, side, t, half],
                sem_y.at[1, side, t, half],
                ring_device(1 - 2 * side),
            )
        )

    left = list(range(ring))
    for t in range(half_ring):
        if t == 0:
            build_place(0)
            summed = placed_for(0)
            for side in (0, 1):
                grow(0, side, side, half_of(summed, side))
        else:
            summed = {}
            for side in (0, 1):
                r = slot_of[(1 - 2 * side) * (half_ring - t)]
                build_place(r)
                summed[side] = placed_for(r)
                if t == 1:
                    grow(t, side, 1 - side, half_of(summed[side], 1 - side))
            for order_half in (0, 1):
                for side in (0, 1):
                    half = 1 - side if order_half == 0 else side
                    if t > 1 or half == side:
                        grow(t, side, half, half_of(summed[side], half))
        if t + 2 < len(groups):
            send_pillars(t + 2)
        if t == 0:
            masks = jnp.concatenate([mask_t[...], mask_t[...] * occupied_t[...]], axis=0)
            masks = masks.astype(F32).astype(BF16)
            of_row = iota((count, tile_rows), 0) // tile_cols == iota((count, tile_rows), 1)
            by_column = dot_nt(jnp.where(of_row, 1.0, 0.0).astype(BF16), masks)
            pairs = (count, 2 * tile_cols)
            of_column = iota(pairs, 0) % tile_cols == iota(pairs, 1) % tile_cols
            both = (2 * tile_cols, channels)
            same_half = (iota(both, 0) < tile_cols) == (iota(both, 1) < channels // 2)
            mask_own = dot(
                jnp.where(of_column, by_column, 0.0).astype(BF16),
                jnp.where(same_half, 1.0, 0.0).astype(BF16),
            )
            post(mask_own, send_m, got_m, sem_m)
        for r in left[:2]:
            build_pick(r)
        left = left[2:]
    build_place(slot_of[0])
    placed = placed_for(slot_of[0])
    for r in left:
        build_pick(r)
    mask_all = (collect(mask_own, got_m, sem_m) * in_slab).astype(BF16)
    half = channels // 2
    spread = jnp.where(
        iota((channels, 2 * channels), 0)
        == jnp.where(iota((channels, 2 * channels), 1) < channels, 0, half),
        1.0,
        0.0,
    ).astype(BF16)
    mask_all = dot(mask_all, spread)
    hidden_cell = mask_all[:, :channels]
    target = mask_all[:, channels:]

    visible = 1.0 - cut(hidden_cell, HALO, tile_rows).reshape(tile_rows, width, channels)[
        :, SIDE : SIDE + tile_cols
    ].reshape(count, channels)

    last = half_ring - 1
    ends = []
    for half in (0, 1):
        value = half_of(placed, half)
        for side in (0, 1):
            if last or half == side:
                arrival(got_y.at[side, last, halves[half]], sem_y.at[1, side, last, half])
                value = value + got_y[side, last, halves[half], :].astype(F32)
        ends.append(value)
    placed = jnp.concatenate(ends, axis=0)
    features = (placed * visible).astype(BF16).astype(F32)
    post(features, send_f, got_f, sem_f)
    side_by_side(collect(features, got_f, sem_f) * in_slab, v0)

    pre1 = dot(windows(v0, 0, height - 2), weights[0])
    side_by_side(pre1 * jax.nn.sigmoid(pre1) * cut(in_slab, 1, height - 2), v1)
    pre2 = dot(windows(v1, 0, height - 4), weights[1])
    sig2 = jax.nn.sigmoid(pre2)
    hidden2 = (pre2 * sig2).astype(BF16)
    head = jnp.broadcast_to(head_row[...], (channels, channels))
    logits = dot_nt(hidden2, head)
    cells_all = n_gy * tile_rows * n_gx * tile_cols
    logit_grad = (
        cut(hidden_cell, 2, height - 4) * jax.nn.sigmoid(logits) - cut(target, 2, height - 4)
    ) / cells_all
    grad2 = logit_grad * head_row[...].astype(F32) * (sig2 * (1.0 + pre2 * (1.0 - sig2)))
    side_by_side(grad2, v2)
    back2 = dot_nt(windows(v2, 0, height - 6), flipped(1))
    grad1 = back2 * slope(cut(pre1, 2, height - 6)) * cut(in_slab, 3, height - 6)
    side_by_side(grad1, v3)
    back1 = dot_nt(windows(v3, 0, tile_rows), flipped(0))
    back1 = back1.reshape(tile_rows, width, channels)[:, SIDE : SIDE + tile_cols].reshape(
        count, channels
    )
    own_g[...] = (back1 * visible).astype(BF16)

    def pass_on(t, side, half):
        src = own_g if t == 1 else got_g.at[side, t - 2]
        go(
            remote(
                src.at[halves[half]],
                got_g.at[side, t - 1, halves[half]],
                sem_g.at[0, side, t - 1, half],
                sem_g.at[1, side, t - 1, half],
                ring_device(1 - 2 * side),
            )
        )

    def hand_out(rel, gradient):
        rows = dot(pick[slot_of[rel]], gradient).astype(BF16)
        returned[block(0, rel), :] = rows[:CHUNK]
        for o in range(1, across):
            send_r[block(o, rel), :] = rows[o * CHUNK : (o + 1) * CHUNK]

    back_groups = {8: [(2, 5), (5, 6), (0, 2), (6, 8)], 4: [(0, 3), (3, 4)], 2: [(0, 2)]}[ring]

    def send_back(g):
        for o in range(1, across):
            rows = span(o, back_groups[g])
            go(
                remote(
                    send_r.at[rows],
                    returned.at[rows],
                    sem_r.at[0, g, o],
                    sem_r.at[1, g, o],
                    across_device(-o),
                )
            )

    parts = levels // 2

    def halve(layer, gradient):
        own_k[pl.ds(layer * parts, parts)] = gradient.reshape(
            parts, 2, share, channels
        ).astype(BF16)
        go(
            remote(
                own_k.at[pl.ds(layer * parts, parts), 1 - core],
                core_k.at[pl.ds(layer * parts, parts)],
                sem_c.at[0, layer],
                sem_c.at[1, layer],
                other_core,
            )
        )

    def to_levels():
        for layer in (0, 1):
            arrival(core_k.at[pl.ds(layer * parts, parts)], sem_c.at[1, layer])
        for k in range(levels):
            send_k[k] = (own_k[k, core].astype(F32) + core_k[k].astype(F32)).astype(BF16)
        got_kz[z] = send_k[z]
        for step in range(1, levels):
            go(
                remote(
                    send_k.at[lax.rem(z + step, levels)],
                    got_kz.at[z],
                    sem_kz.at[0, step],
                    sem_kz.at[1, step],
                    level_device(step),
                )
            )

    def gathered(got, sem):
        summed = None
        for step in range(1, got.shape[0]):
            arrival(got.at[0], sem.at[1, step])
        for k in range(got.shape[0]):
            term = got[k].astype(F32)
            summed = term if summed is None else summed + term
        return summed

    def to_all(value, got, sem, me, device):
        got[me] = value.astype(got.dtype)
        for step in range(1, got.shape[0]):
            go(remote(got.at[me], got.at[me], sem.at[0, step], sem.at[1, step], device(step)))

    def to_pieces(summed):
        spare = across * piece - share
        if spare:
            summed = jnp.concatenate([summed, jnp.zeros((spare, channels), F32)], axis=0)
        send_kx[...] = summed.reshape(across, piece, channels).astype(BF16)
        got_kx[x] = send_kx[x]
        for step in range(1, across):
            go(
                remote(
                    send_kx.at[over(step)],
                    got_kx.at[x],
                    sem_kx.at[0, step],
                    sem_kx.at[1, step],
                    across_device(step),
                )
            )

    def take_step(summed):
        load.wait()
        if across * piece > share:
            second[pl.ds(share, across * piece - share), :] = jnp.ones(
                (across * piece - share, channels), F32
            )
        rows = pl.ds(pl.multiple_of(x * piece, 8), piece)
        return rms_step(summed, second[rows, :])

    chunks = local.shape[0]
    blocks = counts.shape[0]

    def turned(value):
        spare = (-value.shape[0]) % CHUNK
        return jnp.concatenate([value, jnp.zeros((spare, CHUNK), F32)], axis=0).T

    ranks_t = turned(local[...].astype(F32)).astype(jnp.int32)

    def prepare(begin, end):
        for k in range(begin, end):
            part = pl.ds(k * CHUNK, CHUNK)
            slopes[part, :] = slope(dot_tn(points[:, part], point_weight[...]))
            picks[part, :] = jnp.where(
                ranks_t[:, k : k + 1] == iota((CHUNK, CHUNK), 1), 1.0, 0.0
            ).astype(BF16)

    scale = turned(1.0 / counts[...])

    places = tile_places(n_gx)

    def start_merge():
        for d in range(blocks):
            block_d = returned[places(d), :].astype(F32)
            merge_a[pl.ds(d * CHUNK, CHUNK), :] = block_d * scale[:, d : d + 1]
        spare = merge_a.shape[0] - blocks * CHUNK
        for ref in (merge_a, merge_b):
            ref[pl.ds(blocks * CHUNK, spare), :] = jnp.zeros((spare, CHUNK), F32)

    def merge_level(level, src, dst):
        size = CHUNK << level
        for pair in range(blocks >> (level + 1)):
            lead = pair * 2 * size
            first = chunks + pair * (2 << level)
            held = table[first + (1 << level), 0] - table[first, 0]
            for at in range(0, 2 * size, 2 * CHUNK):
                rows = iota((2 * CHUNK, CHUNK), 0) + at
                dst[pl.ds(lead + at, 2 * CHUNK), :] = jnp.where(
                    rows < held,
                    src[pl.ds(lead + at, 2 * CHUNK), :],
                    src[pl.ds(lead + at + size - held, 2 * CHUNK), :],
                )

    levels_m = blocks.bit_length() - 1
    refs = (merge_a, merge_b)

    def merge(begin, end):
        for level in range(begin, end):
            merge_level(level, refs[level % 2], refs[1 - level % 2])

    def point_terms():
        joined = refs[levels_m % 2]
        for k in range(chunks):
            part = pl.ds(k * CHUNK, CHUNK)
            window = joined[pl.ds(table[k, 0], CHUNK), :].astype(BF16)
            rows_b[part, :] = (dot(picks[part, :], window) * slopes[part, :]).astype(BF16)
        return dot(points[...], rows_b[...])

    for order_half in (0, 1):
        for side in (0, 1):
            pass_on(1, side, side if order_half == 0 else 1 - side)
    own1 = (cut(grad1, 1, tile_rows) * own_column).astype(BF16)
    halve(0, dot_tn(windows(v0, 3, tile_rows), own1))
    own2 = (cut(grad2, 2, tile_rows) * own_column).astype(BF16)
    halve(1, dot_tn(windows(v1, 2, tile_rows), own2))
    hand_out(0, own_g[...])
    head_terms = cut(logit_grad * hidden2.astype(F32), 2, tile_rows) * own_column
    head_local = jnp.sum(head_terms, axis=0, keepdims=True)
    prepared = 0
    for t in range(1, half_ring + 1):
        if t < half_ring:
            for order_half in (0, 1):
                for side in (0, 1):
                    half = side if order_half == 0 else 1 - side
                    arrival(got_g.at[side, t - 1, halves[half]], sem_g.at[1, side, t - 1, half])
                    if t + 1 < half_ring or order_half == 0:
                        pass_on(t + 1, side, half)
        else:
            for side in (0, 1):
                arrival(got_g.at[side, t - 1, halves[side]], sem_g.at[1, side, t - 1, side])
        if t == 1:
            to_levels()
        if t == half_ring:
            hand_out(
                t,
                jnp.concatenate(
                    [got_g[side, t - 1, halves[side], :] for side in (0, 1)], axis=0
                ),
            )
        else:
            hand_out(-t, got_g[0, t - 1])
            hand_out(t, got_g[1, t - 1])
        send_back(t - 1)
        if t == half_ring:
            to_pieces(gathered(got_kz, sem_kz))
        share_to = chunks * t // half_ring
        prepare(prepared, share_to)
        prepared = share_to
    to_all(gathered(got_kx, sem_kx), got_ky, sem_ky, y, ring_device)
    for g, group in enumerate(back_groups):
        for o in range(1, across):
            arrival(returned.at[span(o, group)], sem_r.at[1, g, o])
    start_merge()
    merge(0, min(2, levels_m))
    to_all(take_step(gathered(got_ky, sem_ky)), got_ax, sem_ax, x, across_device)
    merge(min(2, levels_m), levels_m)
    for step in range(1, across):
        arrival(got_ax.at[0], sem_ax.at[1, step])
    conv_out[z, core] = got_ax[...].reshape(across * piece, channels)[:share]
    mine = conv_out.at[z, core]
    for step in range(1, levels):
        go(remote(mine, mine, sem_az.at[0, step], sem_az.at[1, step], level_device(step)))
    features_in = points.shape[0]
    own_s[...] = jnp.zeros_like(own_s)
    own_s[0:features_in, :] = point_terms()
    own_s[features_in : features_in + 1, :] = head_local
    to_all(own_s[...], got_sy, sem_sy, y, ring_device)

    to_all(gathered(got_sy, sem_sy), got_sx, sem_sx, x, across_device)
    for step in range(1, levels):
        arrival(conv_out.at[lax.rem(z - step + levels, levels), core], sem_az.at[1, step])
    chip = conv_out.at[:, core]
    go(remote(chip, chip, sem_ac.at[0], sem_ac.at[1], other_core))
    to_all(gathered(got_sx, sem_sx), got_sz, sem_sz, gy, stack_device)
    small = gathered(got_sz, sem_sz)
    point_out[...] = rms_step(small[:features_in], point_second[...])
    head_out[...] = rms_step(small[features_in : features_in + 1], head_second[...])
    arrival(conv_out.at[:, 1 - core], sem_ac.at[1])
    for copy in started:
        copy.wait_send()


def map_step(grid, pillars, recv_cell, cell_mask, occupancy, weights, head_weight, points, local,
             point_weight, table, counts, conv_second, point_second, head_second):
    n_gy, n_gx, tile_rows, tile_cols = grid
    slots, channels = pillars.shape
    total = points.shape[1]
    blocks = slots // CHUNK
    count = tile_rows * tile_cols
    width = tile_cols + 2 * SIDE
    height = tile_rows + 2 * HALO
    ring = ring_size(n_gx)
    across, half_ring = n_gx // ring, ring // 2
    _, rows = message_rows(tile_rows, tile_cols)
    vmem = pl.BlockSpec(memory_space=pltpu.VMEM)
    smem = pl.BlockSpec(memory_space=pltpu.SMEM)
    taps = weights.shape[1]
    levels = n_gy // 2
    share = 2 * taps * channels // n_gy
    piece = -(-share // (across * 16)) * 16
    few = -(-(points.shape[0] + 1) // 8) * 8
    return pl.pallas_call(
        functools.partial(map_kernel, grid),
        out_shape=(
            jax.ShapeDtypeStruct((levels, 2, share, channels), BF16),
            jax.ShapeDtypeStruct(point_weight.shape, F32),
            jax.ShapeDtypeStruct((1, channels), F32),
        ),
        in_specs=[vmem] * 9 + [smem, vmem, pl.BlockSpec(memory_space=pl.ANY), vmem, vmem],
        out_specs=(vmem,) * 3,
        scratch_shapes=[
            pltpu.VMEM((ring, count, across * CHUNK), BF16),
            pltpu.VMEM((ring, across * CHUNK, count), BF16),
            pltpu.VMEM((rows, channels), BF16),
            pltpu.VMEM((rows, channels), BF16),
            pltpu.VMEM((rows, channels), BF16),
            pltpu.VMEM((rows, channels), BF16),
            pltpu.VMEM((height * width, 3 * channels), BF16),
            pltpu.VMEM(((height - 2) * width, 3 * channels), BF16),
            pltpu.VMEM(((height - 4) * width, 3 * channels), BF16),
            pltpu.VMEM(((height - 6) * width, 3 * channels), BF16),
            pltpu.VMEM((ring * 8, CHUNK), jnp.int32),
            pltpu.VMEM((ring * 8, CHUNK), jnp.int32),
            pltpu.VMEM((slots, channels), BF16),
            pltpu.VMEM((2, half_ring, count, channels), BF16),
            pltpu.VMEM((2, half_ring, count, channels), BF16),
            pltpu.VMEM((count, channels), BF16),
            pltpu.VMEM((2, half_ring, count, channels), BF16),
            pltpu.VMEM((slots, channels), BF16),
            pltpu.VMEM((slots, channels), BF16),
            pltpu.VMEM((levels, 2, share, channels), BF16),
            pltpu.VMEM((levels, share, channels), BF16),
            pltpu.VMEM((levels, share, channels), BF16),
            pltpu.VMEM((levels, share, channels), BF16),
            pltpu.VMEM((across, piece, channels), BF16),
            pltpu.VMEM((across, piece, channels), BF16),
            pltpu.VMEM((ring, piece, channels), BF16),
            pltpu.VMEM((across, piece, channels), BF16),
            pltpu.VMEM((across * piece, channels), F32),
            pltpu.VMEM((slots + slots // 2, channels), F32),
            pltpu.VMEM((slots + slots // 2, channels), F32),
            pltpu.VMEM((total, channels), F32),
            pltpu.VMEM((total, CHUNK), BF16),
            pltpu.VMEM((total, channels), BF16),
            pltpu.VMEM((few, channels), F32),
            pltpu.VMEM((ring, few, channels), F32),
            pltpu.VMEM((across, few, channels), F32),
            pltpu.VMEM((n_gy, few, channels), F32),
            pltpu.SemaphoreType.DMA((2, len(STEPS))),
            pltpu.SemaphoreType.DMA((2, len(STEPS))),
            pltpu.SemaphoreType.DMA((2, ring)),
            pltpu.SemaphoreType.DMA((2, ring, across)),
            pltpu.SemaphoreType.DMA((2, 2, half_ring, 2)),
            pltpu.SemaphoreType.DMA((2, 2, half_ring, 2)),
            pltpu.SemaphoreType.DMA((2, ring, across)),
            pltpu.SemaphoreType.DMA((2, 2)),
            pltpu.SemaphoreType.DMA((2, levels)),
            pltpu.SemaphoreType.DMA((2, across)),
            pltpu.SemaphoreType.DMA((2, ring)),
            pltpu.SemaphoreType.DMA((2, across)),
            pltpu.SemaphoreType.DMA((2, levels)),
            pltpu.SemaphoreType.DMA((2,)),
            pltpu.SemaphoreType.DMA((2, ring)),
            pltpu.SemaphoreType.DMA((2, across)),
            pltpu.SemaphoreType.DMA((2, n_gy)),
            pltpu.SemaphoreType.DMA,
        ],
        compiler_params=pltpu.CompilerParams(
            vmem_limit_bytes=VMEM_LIMIT, collective_id=1, has_side_effects=True
        ),
        name="map_step",
    )(
        pillars,
        recv_cell.reshape(blocks, CHUNK),
        cell_mask.T,
        occupancy.T,
        weights.reshape(2, taps * channels, channels),
        head_weight.reshape(1, channels),
        points,
        local,
        point_weight,
        table,
        counts,
        conv_second.reshape(n_gy * share, channels),
        point_second,
        head_second.reshape(1, channels),
    )


def on_device(
    points,
    point_pillar,
    point_weight,
    recv_cell,
    cell_mask,
    occupancy,
    conv_weight,
    head_weight,
    conv_second,
    point_second,
    head_second,
):
    rows, columns = lax.axis_size("gy"), lax.axis_size("gx")
    tile_rows, tile_cols = cell_mask.shape
    channels = point_weight.shape[1]
    slots = recv_cell.shape[0]
    grid = (rows, columns, tile_rows, tile_cols)

    pillars, table, local, counts = pool(columns, points, point_pillar, point_weight, slots)
    conv_step, point_step, head_step = map_step(
        grid,
        pillars,
        recv_cell,
        cell_mask,
        occupancy,
        conv_weight,
        head_weight,
        points,
        local,
        point_weight,
        table,
        counts,
        conv_second,
        point_second,
        head_second,
    )
    return conv_step.astype(F32).reshape(conv_second.shape), point_step, head_step[0]


def solution(mesh):
    return jax.shard_map(
        on_device,
        mesh=mesh,
        in_specs=(
            P(None, ("gy", "gx")),
            P(("gy", "gx")),
            P(),
            P(("gy", "gx")),
            P("gy", "gx"),
            P("gy", "gx"),
            P(),
            P(),
            P(),
            P(),
            P(),
        ),
        out_specs=(P(), P(), P()),
        check_vma=False,
    )
```

```python
import functools

import jax
import jax.numpy as jnp
from jax import lax
from jax.experimental import pallas as pl
from jax.experimental.pallas import tpu as pltpu
from jax.sharding import PartitionSpec as P

MESH = pl.DeviceIdType.MESH
F32 = jnp.float32
BF16 = jnp.bfloat16
VMEM_LIMIT = 56 * 1024 * 1024
CHUNK = 128
SIDE = 8
HALO = 4
STEPS = ((0, -1), (0, 1), (-1, 0), (1, 0), (-1, -1), (1, 1), (-1, 1), (1, -1))


def iota(shape, dim):
    return lax.broadcasted_iota(jnp.int32, shape, dim)


def dot(a, b):
    return jnp.dot(a, b, preferred_element_type=F32)


def dot_nt(a, b):
    return lax.dot_general(a, b, (((1,), (1,)), ((), ())), preferred_element_type=F32)


def dot_tn(a, b):
    return lax.dot_general(a, b, (((0,), (0,)), ((), ())), preferred_element_type=F32)


def slope(value):
    sig = jax.nn.sigmoid(value)
    return sig * (1.0 + value * (1.0 - sig))


def rms_step(gradient, second):
    moment = 0.95 * second + 0.05 * gradient * gradient
    return gradient / (jnp.sqrt(moment) + 1e-08)


def pool_kernel(
    points, ids, ids_row, weight, pillars, table, local, counts, table_s, partial, sums, numbers, sem
):
    chunks = ids.shape[0]
    blocks = pillars.shape[0] // CHUNK
    total = chunks * CHUNK
    here = ids[...]
    back = pltpu.roll(here, 1, axis=1)
    lane = iota(here.shape, 1)
    before = jnp.where(lane == 0, pltpu.roll(back, 1, axis=0), back)
    first = (lane == 0) & (iota(here.shape, 0) == 0)
    flags = jnp.where((here != before) | first, 1.0, 0.0).astype(BF16)
    upto = jnp.where(iota((CHUNK, CHUNK), 0) <= iota((CHUNK, CHUNK), 1), 1.0, 0.0).astype(BF16)
    inside = dot(flags, upto)
    whole = dot(flags, jnp.ones((CHUNK, CHUNK), BF16))
    lower = jnp.where(iota((chunks, chunks), 0) > iota((chunks, chunks), 1), 1.0, 0.0)
    ahead = dot(lower.astype(BF16), whole.astype(BF16))
    head = jnp.broadcast_to(inside[:, 0:1], inside.shape)
    local[...] = (inside - head).astype(jnp.int32)
    row = ids_row[...]
    row_before = pltpu.roll(row, 1, axis=1)
    row_first = (row != row_before) | (iota(row.shape, 1) == 0)
    row_block = jnp.where(row_first, row // CHUNK, blocks + 8)
    below = jnp.where(row_block < iota((blocks + 8, total), 0), 1.0, 0.0).astype(BF16)
    table[0:chunks, :] = (ahead + head - 1.0).astype(jnp.int32)
    table[chunks : chunks + blocks + 8, :] = dot(below, jnp.ones((total, CHUNK), BF16)).astype(
        jnp.int32
    )
    copy = pltpu.make_async_copy(table, table_s, sem)
    copy.start()
    ranks = local[...]
    for k in range(chunks):
        part = pl.ds(k * CHUNK, CHUNK)
        pre = dot_tn(points[:, part], weight[...])
        act = (pre * jax.nn.sigmoid(pre)).astype(BF16)
        pick = jnp.where(iota((CHUNK, CHUNK), 0) == ranks[k : k + 1, :], 1.0, 0.0).astype(BF16)
        partial[part, :] = dot(pick, jnp.concatenate([act, jnp.ones_like(act)], axis=1))
    copy.wait()
    edge = jnp.zeros((8, CHUNK), F32)
    for k in range(chunks):
        at = table_s[k, 0]
        for side, compact in enumerate((sums, numbers)):
            got = partial[pl.ds(k * CHUNK, CHUNK), pl.ds(side * CHUNK, CHUNK)]
            first_rows = got[0:8] if k == 0 else compact[pl.ds(at, 8), :] + got[0:8]
            compact[pl.ds(at, CHUNK + 8), :] = jnp.concatenate([first_rows, got[8:], edge], axis=0)
    diagonal = iota((CHUNK, CHUNK), 0) == iota((CHUNK, CHUNK), 1)
    for d in range(blocks):
        at = table_s[chunks + d, 0]
        held = table_s[chunks + d + 1, 0] - at
        named = iota((CHUNK, CHUNK), 0) < held
        count = jnp.where(named, numbers[pl.ds(at, CHUNK), :], 1.0)
        mean = jnp.where(named, sums[pl.ds(at, CHUNK), :] / count, 0.0)
        pillars[pl.ds(d * CHUNK, CHUNK), :] = mean.astype(BF16)
        counts[d : d + 1, :] = jnp.sum(jnp.where(diagonal, count, 0.0), axis=0, keepdims=True)


def pool(points, point_pillar, weight, slots):
    total = point_pillar.shape[0]
    chunks, blocks = total // CHUNK, slots // CHUNK
    channels = weight.shape[1]
    rows = chunks + blocks + 8
    vmem = pl.BlockSpec(memory_space=pltpu.VMEM)
    return pl.pallas_call(
        pool_kernel,
        out_shape=(
            jax.ShapeDtypeStruct((slots, channels), BF16),
            jax.ShapeDtypeStruct((rows, CHUNK), jnp.int32),
            jax.ShapeDtypeStruct((chunks, CHUNK), jnp.int32),
            jax.ShapeDtypeStruct((blocks, CHUNK), F32),
        ),
        in_specs=[vmem] * 4,
        out_specs=(vmem,) * 4,
        scratch_shapes=[
            pltpu.SMEM((rows, CHUNK), jnp.int32),
            pltpu.VMEM((total, 2 * CHUNK), F32),
            pltpu.VMEM((total + 2 * CHUNK, CHUNK), F32),
            pltpu.VMEM((total + 2 * CHUNK, CHUNK), F32),
            pltpu.SemaphoreType.DMA,
        ],
        compiler_params=pltpu.CompilerParams(vmem_limit_bytes=VMEM_LIMIT),
        name="pool",
    )(points, point_pillar.reshape(chunks, CHUNK), point_pillar.reshape(1, total), weight)


def message_rows(tile_rows, tile_cols):
    spans, at = [], 0
    for down, right in STEPS:
        size = (HALO if down else tile_rows) * (SIDE if right else tile_cols)
        spans.append((at, size))
        at += size
    return spans, at


def ring_size(columns):
    return {32: 8, 8: 4, 4: 2}[columns]


def ring_order(ring):
    order = [ring // 2]
    for far in range(ring // 2 - 1, 0, -1):
        order += [far, -far]
    return order + [0]


def map_kernel(
    grid,
    pillars,
    cells,
    mask_t,
    occupied_t,
    weights,
    head_row,
    points,
    local,
    point_weight,
    table,
    counts,
    conv_second,
    point_second,
    head_second,
    conv_out,
    point_out,
    head_out,
    place,
    pick,
    send_f,
    got_f,
    send_m,
    got_m,
    v0,
    v1,
    v2,
    v3,
    send_i,
    got_i,
    got_x,
    send_y,
    got_y,
    own_g,
    got_g,
    send_r,
    returned,
    own_k,
    core_k,
    send_k,
    got_kz,
    send_kx,
    got_kx,
    got_ky,
    got_ax,
    second,
    merge_a,
    merge_b,
    slopes,
    picks,
    rows_b,
    own_s,
    got_sy,
    got_sx,
    got_sz,
    sem_f,
    sem_m,
    sem_i,
    sem_x,
    sem_y,
    sem_g,
    sem_r,
    sem_c,
    sem_kz,
    sem_kx,
    sem_ky,
    sem_ax,
    sem_az,
    sem_ac,
    sem_sy,
    sem_sx,
    sem_sz,
    sem_l,
):
    n_gy, n_gx, tile_rows, tile_cols = grid
    gy, gx = lax.axis_index("gy"), lax.axis_index("gx")
    ring = ring_size(n_gx)
    across = n_gx // ring
    half_ring = ring // 2
    order = ring_order(ring)
    slot_of = {rel: r for r, rel in enumerate(order)}
    slot_of[-half_ring] = slot_of[half_ring]
    x, y = gx // ring, lax.rem(gx, ring)
    channels = pillars.shape[1]
    spans, _ = message_rows(tile_rows, tile_cols)
    width = tile_cols + 2 * SIDE
    height = tile_rows + 2 * HALO
    count = tile_rows * tile_cols
    part_rows = count // 2
    fan = across * CHUNK

    def neighbour(k):
        down, right = STEPS[k]
        return lax.rem(gy + down + n_gy, n_gy), lax.rem(gx + right + n_gx, n_gx)

    def along(step):
        return lax.rem(y + step + ring, ring)

    def over(step):
        return lax.rem(x + step + across, across)

    def ring_device(step):
        return gy, x * ring + along(step)

    def across_device(step):
        return gy, over(step) * ring + y

    levels = n_gy // 2
    z, core = gy // 2, lax.rem(gy, 2)

    def level_device(step):
        return lax.rem(z + step, levels) * 2 + core, gx

    other_core = (z * 2 + 1 - core, gx)

    def stack_device(step):
        return lax.rem(gy + step, n_gy), gx

    def slot_block(column, place_on_ring):
        return pl.ds(pl.multiple_of((column * ring + place_on_ring) * CHUNK, CHUNK), CHUNK)

    def remote(src, dst, send, recv, device):
        return pltpu.make_async_remote_copy(
            src_ref=src,
            dst_ref=dst,
            send_sem=send,
            recv_sem=recv,
            device_id=device,
            device_id_type=MESH,
        )

    def arrival(ref, sem):
        remote(ref, ref, sem, sem, ring_device(1)).wait_recv()

    share = own_k.shape[2]
    piece = got_ky.shape[1]
    load = pltpu.make_async_copy(
        conv_second.at[pl.ds(pl.multiple_of(gy * share, 8), share)],
        second.at[pl.ds(0, share)],
        sem_l,
    )
    load.start()
    barrier = pltpu.get_barrier_semaphore()
    partners = [neighbour(k) for k in range(len(STEPS))]
    partners += [ring_device(step) for step in range(1, ring)]
    partners += [across_device(step) for step in range(1, across)]
    partners += [stack_device(step) for step in range(1, n_gy)]
    for device in partners:
        pl.semaphore_signal(barrier, inc=1, device_id=device, device_id_type=MESH)
    pl.semaphore_wait(barrier, len(partners))

    started = []

    def go(copy):
        copy.start()
        started.append(copy)

    def send_pillars(r):
        for o in range(1, across):
            go(
                remote(
                    pillars.at[slot_block(over(o), along(order[r]))],
                    got_x.at[pl.ds((r * across + o) * CHUNK, CHUNK)],
                    sem_x.at[0, r, o],
                    sem_x.at[1, r, o],
                    across_device(o),
                )
            )

    for r in range(min(3, ring)):
        send_pillars(r)

    send_i[...] = jnp.zeros_like(send_i)
    for step in range(ring):
        lead = step * 8
        for o in range(across):
            row = over(-o) * ring + along(step)
            send_i[lead + o : lead + o + 1, :] = cells[pl.ds(row, 1), :]
        if step == 0:
            got_i[pl.ds(slot_of[0] * 8, 8), :] = send_i[pl.ds(0, 8), :]
        else:
            rel = -step if step <= half_ring else ring - step
            slot = slot_of[rel]
            go(
                remote(
                    send_i.at[pl.ds(lead, 8)],
                    got_i.at[pl.ds(slot * 8, 8)],
                    sem_i.at[0, step],
                    sem_i.at[1, slot],
                    ring_device(step),
                )
            )

    def post(own, send, got, sem):
        grid3 = own.reshape(tile_rows, tile_cols, channels)
        for k, (down, right) in enumerate(STEPS):
            part = grid3
            if down:
                part = part[:HALO] if down < 0 else part[tile_rows - HALO :]
            if right:
                part = part[:, :SIDE] if right < 0 else part[:, tile_cols - SIDE :]
            at, size = spans[k]
            send[pl.ds(at, size), :] = part.reshape(size, channels).astype(BF16)
            there, _ = spans[k ^ 1]
            go(
                remote(
                    send.at[pl.ds(at, size)],
                    got.at[pl.ds(there, size)],
                    sem.at[0, k],
                    sem.at[1, k ^ 1],
                    neighbour(k),
                )
            )

    def collect(own, got, sem):
        parts = {}
        for k, (down, right) in enumerate(STEPS):
            at, size = spans[k]
            arrival(got.at[pl.ds(at, size)], sem.at[1, k])
            rows = HALO if down else tile_rows
            parts[down, right] = (
                got[pl.ds(at, size), :].astype(F32).reshape(rows, size // rows, channels)
            )
        parts[0, 0] = own.reshape(tile_rows, tile_cols, channels)
        return jnp.concatenate(
            [
                jnp.concatenate([parts[down, right] for right in (-1, 0, 1)], axis=1).reshape(
                    -1, channels
                )
                for down in (-1, 0, 1)
            ],
            axis=0,
        )

    masks = jnp.concatenate([mask_t[...], mask_t[...] * occupied_t[...]], axis=0)
    masks = masks.astype(F32).astype(BF16)
    of_row = iota((count, tile_rows), 0) // tile_cols == iota((count, tile_rows), 1)
    by_column = dot_nt(jnp.where(of_row, 1.0, 0.0).astype(BF16), masks)
    pairs = (count, 2 * tile_cols)
    of_column = iota(pairs, 0) % tile_cols == iota(pairs, 1) % tile_cols
    halves = (2 * tile_cols, channels)
    same_half = (iota(halves, 0) < tile_cols) == (iota(halves, 1) < channels // 2)
    mask_own = dot(
        jnp.where(of_column, by_column, 0.0).astype(BF16),
        jnp.where(same_half, 1.0, 0.0).astype(BF16),
    )
    post(mask_own, send_m, got_m, sem_m)

    flat = iota((height * width, channels), 0)
    row = flat // width + gy * tile_rows - HALO
    col = flat % width + gx * tile_cols - SIDE
    in_slab = jnp.where(
        (row >= 0) & (row < n_gy * tile_rows) & (col >= 0) & (col < n_gx * tile_cols), 1.0, 0.0
    )
    column = iota((tile_rows * width, channels), 0) % width
    own_column = jnp.where((column >= SIDE) & (column < SIDE + tile_cols), 1.0, 0.0)

    for r in range(ring - 1):
        arrival(got_i.at[pl.ds(r * 8, 8)], sem_i.at[1, r])
    rows_i = ring * 8
    cells_i = got_i[...]
    cells_t = jnp.concatenate(
        [cells_i.astype(F32), jnp.zeros(((-rows_i) % CHUNK, CHUNK), F32)], axis=0
    ).T.astype(jnp.int32)
    def build_place(r):
        for o in range(across):
            at = r * 8 + o
            place[r, :, pl.ds(o * CHUNK, CHUNK)] = jnp.where(
                iota((count, CHUNK), 0) == cells_i[at : at + 1, :], 1.0, 0.0
            ).astype(BF16)

    def build_pick(r):
        for o in range(across):
            at = r * 8 + o
            pick[r, pl.ds(o * CHUNK, CHUNK), :] = jnp.where(
                cells_t[:, at : at + 1] == iota((CHUNK, count), 1), 1.0, 0.0
            ).astype(BF16)

    def cut(value, lead, rows):
        return value[lead * width : (lead + rows) * width]

    def side_by_side(value, ref):
        size = value.shape[0]
        left = pltpu.roll(value, 1, axis=0)
        right = pltpu.roll(value, size - 1, axis=0)
        ref[...] = jnp.concatenate([left.astype(BF16), value.astype(BF16), right.astype(BF16)], 1)

    def windows(ref, lead, rows):
        return jnp.concatenate(
            [ref[pl.ds((lead + a) * width, rows * width), :] for a in (0, 1, 2)], axis=1
        )

    def flipped(layer):
        return jnp.concatenate(
            [weights[layer, pl.ds((8 - k) * channels, channels), :] for k in range(9)], axis=1
        )

    def placed_for(r):
        for o in range(1, across):
            arrival(got_x.at[pl.ds((r * across + o) * CHUNK, CHUNK)], sem_x.at[1, r, o])
        own = pillars[slot_block(x, along(order[r])), :]
        rest = got_x[pl.ds((r * across + 1) * CHUNK, fan - CHUNK), :]
        return dot(place[r], jnp.concatenate([own, rest], axis=0))

    halves = (pl.ds(0, part_rows), pl.ds(part_rows, part_rows))

    def half_of(value, half):
        return value[half * part_rows : (half + 1) * part_rows]

    def grow(t, side, half, value):
        if t > 1 or (t == 1 and half == side):
            arrival(got_y.at[side, t - 1, halves[half]], sem_y.at[1, side, t - 1, half])
            value = value + got_y[side, t - 1, halves[half], :].astype(F32)
        send_y[side, t, halves[half], :] = value.astype(BF16)
        go(
            remote(
                send_y.at[side, t, halves[half]],
                got_y.at[side, t, halves[half]],
                sem_y.at[0, side, t, half],
                sem_y.at[1, side, t, half],
                ring_device(1 - 2 * side),
            )
        )

    left = list(range(ring))
    for t in range(half_ring):
        for r in range(2 * t + 1, min(2 * t + 3, ring)) if t else ():
            send_pillars(r)
        if t == 0:
            build_place(0)
            summed = placed_for(0)
            for side in (0, 1):
                grow(0, side, side, half_of(summed, side))
        else:
            summed = {}
            for side in (0, 1):
                r = slot_of[(1 - 2 * side) * (half_ring - t)]
                build_place(r)
                summed[side] = placed_for(r)
                if t == 1:
                    grow(t, side, 1 - side, half_of(summed[side], 1 - side))
            for order_half in (0, 1):
                for side in (0, 1):
                    half = 1 - side if order_half == 0 else side
                    if t > 1 or half == side:
                        grow(t, side, half, half_of(summed[side], half))
        for r in left[:2]:
            build_pick(r)
        left = left[2:]
    build_place(slot_of[0])
    placed = placed_for(slot_of[0])
    for r in left:
        build_pick(r)
    mask_all = (collect(mask_own, got_m, sem_m) * in_slab).astype(BF16)
    half = channels // 2
    spread = jnp.where(
        iota((channels, 2 * channels), 0)
        == jnp.where(iota((channels, 2 * channels), 1) < channels, 0, half),
        1.0,
        0.0,
    ).astype(BF16)
    mask_all = dot(mask_all, spread)
    hidden_cell = mask_all[:, :channels]
    target = mask_all[:, channels:]

    visible = 1.0 - cut(hidden_cell, HALO, tile_rows).reshape(tile_rows, width, channels)[
        :, SIDE : SIDE + tile_cols
    ].reshape(count, channels)

    last = half_ring - 1
    ends = []
    for half in (0, 1):
        value = half_of(placed, half)
        for side in (0, 1):
            if last or half == side:
                arrival(got_y.at[side, last, halves[half]], sem_y.at[1, side, last, half])
                value = value + got_y[side, last, halves[half], :].astype(F32)
        ends.append(value)
    placed = jnp.concatenate(ends, axis=0)
    features = (placed * visible).astype(BF16).astype(F32)
    post(features, send_f, got_f, sem_f)
    side_by_side(collect(features, got_f, sem_f) * in_slab, v0)

    pre1 = dot(windows(v0, 0, height - 2), weights[0])
    side_by_side(pre1 * jax.nn.sigmoid(pre1) * cut(in_slab, 1, height - 2), v1)
    pre2 = dot(windows(v1, 0, height - 4), weights[1])
    sig2 = jax.nn.sigmoid(pre2)
    hidden2 = (pre2 * sig2).astype(BF16)
    head = jnp.broadcast_to(head_row[...], (channels, channels))
    logits = dot_nt(hidden2, head)
    cells_all = n_gy * tile_rows * n_gx * tile_cols
    logit_grad = (
        cut(hidden_cell, 2, height - 4) * jax.nn.sigmoid(logits) - cut(target, 2, height - 4)
    ) / cells_all
    grad2 = logit_grad * head_row[...].astype(F32) * (sig2 * (1.0 + pre2 * (1.0 - sig2)))
    side_by_side(grad2, v2)
    back2 = dot_nt(windows(v2, 0, height - 6), flipped(1))
    grad1 = back2 * slope(cut(pre1, 2, height - 6)) * cut(in_slab, 3, height - 6)
    side_by_side(grad1, v3)
    back1 = dot_nt(windows(v3, 0, tile_rows), flipped(0))
    back1 = back1.reshape(tile_rows, width, channels)[:, SIDE : SIDE + tile_cols].reshape(
        count, channels
    )
    own_g[...] = (back1 * visible).astype(BF16)

    def pass_on(t, side, half):
        src = own_g if t == 1 else got_g.at[side, t - 2]
        go(
            remote(
                src.at[halves[half]],
                got_g.at[side, t - 1, halves[half]],
                sem_g.at[0, side, t - 1, half],
                sem_g.at[1, side, t - 1, half],
                ring_device(1 - 2 * side),
            )
        )

    def hand_out(rel, gradient):
        r = slot_of[rel]
        rows = dot(pick[r], gradient).astype(BF16)
        returned[slot_block(x, along(rel)), :] = rows[:CHUNK]
        send_r[r] = rows
        for o in range(1, across):
            go(
                remote(
                    send_r.at[r, pl.ds(o * CHUNK, CHUNK)],
                    returned.at[slot_block(x, along(rel))],
                    sem_r.at[0, r, o],
                    sem_r.at[1, r, o],
                    across_device(-o),
                )
            )

    parts = levels // 2

    def halve(layer, gradient):
        own_k[pl.ds(layer * parts, parts)] = gradient.reshape(
            parts, 2, share, channels
        ).astype(BF16)
        go(
            remote(
                own_k.at[pl.ds(layer * parts, parts), 1 - core],
                core_k.at[pl.ds(layer * parts, parts)],
                sem_c.at[0, layer],
                sem_c.at[1, layer],
                other_core,
            )
        )

    def kernel_gradient(ref, lead, gradient):
        by_output = dot_tn(gradient, windows(ref, lead, tile_rows))
        taps = [by_output[:, k * channels : (k + 1) * channels].T for k in range(9)]
        return jnp.concatenate(taps, axis=0)

    def to_levels():
        for layer in (0, 1):
            arrival(core_k.at[pl.ds(layer * parts, parts)], sem_c.at[1, layer])
        for k in range(levels):
            send_k[k] = (own_k[k, core].astype(F32) + core_k[k].astype(F32)).astype(BF16)
        got_kz[z] = send_k[z]
        for step in range(1, levels):
            go(
                remote(
                    send_k.at[lax.rem(z + step, levels)],
                    got_kz.at[z],
                    sem_kz.at[0, step],
                    sem_kz.at[1, step],
                    level_device(step),
                )
            )

    def gathered(got, sem):
        summed = None
        for step in range(1, got.shape[0]):
            arrival(got.at[0], sem.at[1, step])
        for k in range(got.shape[0]):
            term = got[k].astype(F32)
            summed = term if summed is None else summed + term
        return summed

    def to_all(value, got, sem, me, device):
        got[me] = value.astype(got.dtype)
        for step in range(1, got.shape[0]):
            go(remote(got.at[me], got.at[me], sem.at[0, step], sem.at[1, step], device(step)))

    def to_pieces(summed):
        spare = across * piece - share
        if spare:
            summed = jnp.concatenate([summed, jnp.zeros((spare, channels), F32)], axis=0)
        send_kx[...] = summed.reshape(across, piece, channels).astype(BF16)
        got_kx[x] = send_kx[x]
        for step in range(1, across):
            go(
                remote(
                    send_kx.at[over(step)],
                    got_kx.at[x],
                    sem_kx.at[0, step],
                    sem_kx.at[1, step],
                    across_device(step),
                )
            )

    def take_step(summed):
        load.wait()
        if across * piece > share:
            second[pl.ds(share, across * piece - share), :] = jnp.ones(
                (across * piece - share, channels), F32
            )
        rows = pl.ds(pl.multiple_of(x * piece, 8), piece)
        return rms_step(summed, second[rows, :])

    chunks = local.shape[0]
    blocks = counts.shape[0]

    def turned(value):
        spare = (-value.shape[0]) % CHUNK
        return jnp.concatenate([value, jnp.zeros((spare, CHUNK), F32)], axis=0).T

    ranks_t = turned(local[...].astype(F32)).astype(jnp.int32)

    def prepare(begin, end):
        for k in range(begin, end):
            part = pl.ds(k * CHUNK, CHUNK)
            slopes[part, :] = slope(dot_tn(points[:, part], point_weight[...]))
            picks[part, :] = jnp.where(
                ranks_t[:, k : k + 1] == iota((CHUNK, CHUNK), 1), 1.0, 0.0
            ).astype(BF16)

    scale = turned(1.0 / counts[...])

    def start_merge():
        for d in range(blocks):
            part = pl.ds(d * CHUNK, CHUNK)
            merge_a[part, :] = returned[part, :].astype(F32) * scale[:, d : d + 1]
        spare = merge_a.shape[0] - blocks * CHUNK
        for ref in (merge_a, merge_b):
            ref[pl.ds(blocks * CHUNK, spare), :] = jnp.zeros((spare, CHUNK), F32)

    def merge_level(level, src, dst):
        size = CHUNK << level
        for pair in range(blocks >> (level + 1)):
            lead = pair * 2 * size
            first = chunks + pair * (2 << level)
            held = table[first + (1 << level), 0] - table[first, 0]
            for at in range(0, 2 * size, 2 * CHUNK):
                rows = iota((2 * CHUNK, CHUNK), 0) + at
                dst[pl.ds(lead + at, 2 * CHUNK), :] = jnp.where(
                    rows < held,
                    src[pl.ds(lead + at, 2 * CHUNK), :],
                    src[pl.ds(lead + at + size - held, 2 * CHUNK), :],
                )

    levels_m = blocks.bit_length() - 1
    refs = (merge_a, merge_b)

    def merge(begin, end):
        for level in range(begin, end):
            merge_level(level, refs[level % 2], refs[1 - level % 2])

    def point_terms():
        joined = refs[levels_m % 2]
        for k in range(chunks):
            part = pl.ds(k * CHUNK, CHUNK)
            window = joined[pl.ds(table[k, 0], CHUNK), :].astype(BF16)
            rows_b[part, :] = (dot(picks[part, :], window) * slopes[part, :]).astype(BF16)
        return dot(points[...], rows_b[...])

    for order_half in (0, 1):
        for side in (0, 1):
            pass_on(1, side, side if order_half == 0 else 1 - side)
    own1 = (cut(grad1, 1, tile_rows) * own_column).astype(BF16)
    halve(0, kernel_gradient(v0, 3, own1))
    own2 = (cut(grad2, 2, tile_rows) * own_column).astype(BF16)
    halve(1, kernel_gradient(v1, 2, own2))
    hand_out(0, own_g[...])
    head_terms = cut(logit_grad * hidden2.astype(F32), 2, tile_rows) * own_column
    head_local = jnp.sum(head_terms, axis=0, keepdims=True)
    prepared = 0
    for t in range(1, half_ring + 1):
        if t < half_ring:
            for order_half in (0, 1):
                for side in (0, 1):
                    half = side if order_half == 0 else 1 - side
                    arrival(got_g.at[side, t - 1, halves[half]], sem_g.at[1, side, t - 1, half])
                    if t + 1 < half_ring or order_half == 0:
                        pass_on(t + 1, side, half)
        else:
            for side in (0, 1):
                arrival(got_g.at[side, t - 1, halves[side]], sem_g.at[1, side, t - 1, side])
        if t == 1:
            to_levels()
        if t == half_ring:
            to_pieces(gathered(got_kz, sem_kz))
            hand_out(
                t,
                jnp.concatenate(
                    [got_g[side, t - 1, halves[side], :] for side in (0, 1)], axis=0
                ),
            )
        else:
            hand_out(-t, got_g[0, t - 1])
            hand_out(t, got_g[1, t - 1])
        share_to = chunks * t // half_ring
        prepare(prepared, share_to)
        prepared = share_to
    to_all(gathered(got_kx, sem_kx), got_ky, sem_ky, y, ring_device)
    for r, rel in enumerate(order):
        for o in range(1, across):
            arrival(returned.at[slot_block(over(o), along(rel))], sem_r.at[1, r, o])
    start_merge()
    merge(0, min(2, levels_m))
    to_all(take_step(gathered(got_ky, sem_ky)), got_ax, sem_ax, x, across_device)
    merge(min(2, levels_m), levels_m)
    for step in range(1, across):
        arrival(got_ax.at[0], sem_ax.at[1, step])
    conv_out[gy] = got_ax[...].reshape(across * piece, channels)[:share]
    mine = conv_out.at[gy]
    for step in range(1, levels):
        go(remote(mine, mine, sem_az.at[0, step], sem_az.at[1, step], level_device(step)))
    go(remote(mine, mine, sem_ac.at[0, 0], sem_ac.at[1, 0], other_core))
    features_in = points.shape[0]
    own_s[...] = jnp.zeros_like(own_s)
    own_s[0:features_in, :] = point_terms()
    own_s[features_in : features_in + 1, :] = head_local
    to_all(own_s[...], got_sy, sem_sy, y, ring_device)

    def relay(begin, end):
        for step in range(begin, end):
            held = conv_out.at[lax.rem(z - step + levels, levels) * 2 + core]
            arrival(held, sem_az.at[1, step])
            go(remote(held, held, sem_ac.at[0, step], sem_ac.at[1, step], other_core))

    relay(1, min(3, levels))
    to_all(gathered(got_sy, sem_sy), got_sx, sem_sx, x, across_device)
    relay(min(3, levels), min(6, levels))
    to_all(gathered(got_sx, sem_sx), got_sz, sem_sz, gy, stack_device)
    relay(min(6, levels), levels)
    small = gathered(got_sz, sem_sz)
    point_out[...] = rms_step(small[:features_in], point_second[...])
    head_out[...] = rms_step(small[features_in : features_in + 1], head_second[...])
    for step in range(levels):
        level = lax.rem(z - step + levels, levels)
        arrival(conv_out.at[level * 2 + 1 - core], sem_ac.at[1, step])
    for copy in started:
        copy.wait_send()


def map_step(grid, pillars, recv_cell, cell_mask, occupancy, weights, head_weight, points, local,
             point_weight, table, counts, conv_second, point_second, head_second):
    n_gy, n_gx, tile_rows, tile_cols = grid
    slots, channels = pillars.shape
    total = points.shape[1]
    blocks = slots // CHUNK
    count = tile_rows * tile_cols
    width = tile_cols + 2 * SIDE
    height = tile_rows + 2 * HALO
    ring = ring_size(n_gx)
    across, half_ring = n_gx // ring, ring // 2
    _, rows = message_rows(tile_rows, tile_cols)
    vmem = pl.BlockSpec(memory_space=pltpu.VMEM)
    smem = pl.BlockSpec(memory_space=pltpu.SMEM)
    taps = weights.shape[1]
    levels = n_gy // 2
    share = 2 * taps * channels // n_gy
    piece = -(-share // (across * 16)) * 16
    few = -(-(points.shape[0] + 1) // 8) * 8
    return pl.pallas_call(
        functools.partial(map_kernel, grid),
        out_shape=(
            jax.ShapeDtypeStruct((n_gy, share, channels), BF16),
            jax.ShapeDtypeStruct(point_weight.shape, F32),
            jax.ShapeDtypeStruct((1, channels), F32),
        ),
        in_specs=[vmem] * 9 + [smem, vmem, pl.BlockSpec(memory_space=pl.ANY), vmem, vmem],
        out_specs=(vmem,) * 3,
        scratch_shapes=[
            pltpu.VMEM((ring, count, across * CHUNK), BF16),
            pltpu.VMEM((ring, across * CHUNK, count), BF16),
            pltpu.VMEM((rows, channels), BF16),
            pltpu.VMEM((rows, channels), BF16),
            pltpu.VMEM((rows, channels), BF16),
            pltpu.VMEM((rows, channels), BF16),
            pltpu.VMEM((height * width, 3 * channels), BF16),
            pltpu.VMEM(((height - 2) * width, 3 * channels), BF16),
            pltpu.VMEM(((height - 4) * width, 3 * channels), BF16),
            pltpu.VMEM(((height - 6) * width, 3 * channels), BF16),
            pltpu.VMEM((ring * 8, CHUNK), jnp.int32),
            pltpu.VMEM((ring * 8, CHUNK), jnp.int32),
            pltpu.VMEM((slots, channels), BF16),
            pltpu.VMEM((2, half_ring, count, channels), BF16),
            pltpu.VMEM((2, half_ring, count, channels), BF16),
            pltpu.VMEM((count, channels), BF16),
            pltpu.VMEM((2, half_ring, count, channels), BF16),
            pltpu.VMEM((ring, across * CHUNK, channels), BF16),
            pltpu.VMEM((slots, channels), BF16),
            pltpu.VMEM((levels, 2, share, channels), BF16),
            pltpu.VMEM((levels, share, channels), BF16),
            pltpu.VMEM((levels, share, channels), BF16),
            pltpu.VMEM((levels, share, channels), BF16),
            pltpu.VMEM((across, piece, channels), BF16),
            pltpu.VMEM((across, piece, channels), BF16),
            pltpu.VMEM((ring, piece, channels), BF16),
            pltpu.VMEM((across, piece, channels), BF16),
            pltpu.VMEM((across * piece, channels), F32),
            pltpu.VMEM((slots + slots // 2, channels), F32),
            pltpu.VMEM((slots + slots // 2, channels), F32),
            pltpu.VMEM((total, channels), F32),
            pltpu.VMEM((total, CHUNK), BF16),
            pltpu.VMEM((total, channels), BF16),
            pltpu.VMEM((few, channels), F32),
            pltpu.VMEM((ring, few, channels), F32),
            pltpu.VMEM((across, few, channels), F32),
            pltpu.VMEM((n_gy, few, channels), F32),
            pltpu.SemaphoreType.DMA((2, len(STEPS))),
            pltpu.SemaphoreType.DMA((2, len(STEPS))),
            pltpu.SemaphoreType.DMA((2, ring)),
            pltpu.SemaphoreType.DMA((2, ring, across)),
            pltpu.SemaphoreType.DMA((2, 2, half_ring, 2)),
            pltpu.SemaphoreType.DMA((2, 2, half_ring, 2)),
            pltpu.SemaphoreType.DMA((2, ring, across)),
            pltpu.SemaphoreType.DMA((2, 2)),
            pltpu.SemaphoreType.DMA((2, levels)),
            pltpu.SemaphoreType.DMA((2, across)),
            pltpu.SemaphoreType.DMA((2, ring)),
            pltpu.SemaphoreType.DMA((2, across)),
            pltpu.SemaphoreType.DMA((2, levels)),
            pltpu.SemaphoreType.DMA((2, levels)),
            pltpu.SemaphoreType.DMA((2, ring)),
            pltpu.SemaphoreType.DMA((2, across)),
            pltpu.SemaphoreType.DMA((2, n_gy)),
            pltpu.SemaphoreType.DMA,
        ],
        compiler_params=pltpu.CompilerParams(
            vmem_limit_bytes=VMEM_LIMIT, collective_id=1, has_side_effects=True
        ),
        name="map_step",
    )(
        pillars,
        recv_cell.reshape(blocks, CHUNK),
        cell_mask.T,
        occupancy.T,
        weights.reshape(2, taps * channels, channels),
        head_weight.reshape(1, channels),
        points,
        local,
        point_weight,
        table,
        counts,
        conv_second.reshape(n_gy * share, channels),
        point_second,
        head_second.reshape(1, channels),
    )


def on_device(
    points,
    point_pillar,
    point_weight,
    recv_cell,
    cell_mask,
    occupancy,
    conv_weight,
    head_weight,
    conv_second,
    point_second,
    head_second,
):
    rows, columns = lax.axis_size("gy"), lax.axis_size("gx")
    tile_rows, tile_cols = cell_mask.shape
    channels = point_weight.shape[1]
    slots = recv_cell.shape[0]
    grid = (rows, columns, tile_rows, tile_cols)

    pillars, table, local, counts = pool(points, point_pillar, point_weight, slots)
    conv_step, point_step, head_step = map_step(
        grid,
        pillars,
        recv_cell,
        cell_mask,
        occupancy,
        conv_weight,
        head_weight,
        points,
        local,
        point_weight,
        table,
        counts,
        conv_second,
        point_second,
        head_second,
    )
    return conv_step.astype(F32).reshape(conv_second.shape), point_step, head_step[0]


def solution(mesh):
    return jax.shard_map(
        on_device,
        mesh=mesh,
        in_specs=(
            P(None, ("gy", "gx")),
            P(("gy", "gx")),
            P(),
            P(("gy", "gx")),
            P("gy", "gx"),
            P("gy", "gx"),
            P(),
            P(),
            P(),
            P(),
            P(),
        ),
        out_specs=(P(), P(), P()),
        check_vma=False,
    )
```
